128 devices in a mesh: dp: 4 (over x), ctx: 16 (over z, y_hi, core), tp: 2 (over y_lo).
Axes of the slice: x: 4, y: 4 (y_hi: 2, y_lo: 2; y = y_hi * 2 + y_lo), z: 4, core: 2. Of those that a mesh axis runs over, the one named last changes fastest.
Arguments:
- tokens: bfloat16 [4, 4096, 2048], P('dp', 'ctx'), may hold values from -6 to 6
- w_query: bfloat16 [2048, 2048], P(('dp', 'ctx'), 'tp'), may hold values from -0.125 to 0.125
- w_key: bfloat16 [2048, 256], P(('dp', 'ctx'), 'tp'), may hold values from -0.125 to 0.125
- w_value: bfloat16 [2048, 256], P(('dp', 'ctx'), 'tp'), may hold values from -0.125 to 0.125
- w_output: bfloat16 [2048, 2048], P('tp', ('dp', 'ctx')), may hold values from -0.375 to 0.375
- w_gate: bfloat16 [2048, 5632], P(('dp', 'ctx'), 'tp'), may hold values from -0.125 to 0.125
- w_up: bfloat16 [2048, 5632], P(('dp', 'ctx'), 'tp'), may hold values from -0.125 to 0.125
- w_down: bfloat16 [5632, 2048], P('tp', ('dp', 'ctx')), may hold values from -0.078125 to 0.078125
- norm_attn: bfloat16 [2048], P(('dp', 'ctx')), may hold values from 0.5 to 1.5
- norm_ffn: bfloat16 [2048], P(('dp', 'ctx')), may hold values from 0.5 to 1.5
- cotangent: bfloat16 [4, 4096, 2048], P('dp', 'ctx'), may hold values from -6 to 6
Outputs:
- block_out: bfloat16 [4, 4096, 2048], P('dp', 'ctx')
- input_grad: float32 [4, 4096, 2048], P('dp', 'ctx')
- grad_query: float32 [2048, 2048], P(('dp', 'ctx'), 'tp')
- grad_key: float32 [2048, 256], P(('dp', 'ctx'), 'tp')
- grad_value: float32 [2048, 256], P(('dp', 'ctx'), 'tp')
- grad_output: float32 [2048, 2048], P('tp', ('dp', 'ctx'))
- grad_gate: float32 [2048, 5632], P(('dp', 'ctx'), 'tp')
- grad_up: float32 [2048, 5632], P(('dp', 'ctx'), 'tp')
- grad_down: float32 [5632, 2048], P('tp', ('dp', 'ctx'))
- grad_norm_attn: float32 [2048], P(('dp', 'ctx'))
- grad_norm_ffn: float32 [2048], P(('dp', 'ctx'))
The draws below stay inside these ranges and needn't reach their ends.
All inputs are finite; a program needn't handle non-finite values.
Results may differ from the reference program's by a relative error of at most 0.025.
Values may be sent and summed in bfloat16 or wider, within the bound.
No kernel may reach another device: no remote copies, remote signals or barrier semaphores. Data moves between devices by JAX's collectives and lax.ppermute only.
A program may use at most 256 MiB of HBM per device.

```python
import jax
import jax.numpy as jnp
from jax import lax

D = 2048
HQ = 32
KV = 4
HD = 64
FF = 5632
BATCH = 4
LENGTH = 4096


def block_scale(key, extent, pieces, low, top_value):
    level, own = 1.0, jax.random.fold_in(key, 6)
    for position, shards_of in pieces:
        draws = jnp.exp(jax.random.uniform(jax.random.fold_in(own, position), (shards_of,), jnp.float32, low / len(pieces), top_value / len(pieces)))
        level = level * jnp.repeat(draws, extent[position] // shards_of).reshape([-1 if axis == position else 1 for axis in range(len(extent))])
    return level


def bell_draw(stream_key, shape, spread, bound, cuts=(), kind=jnp.bfloat16):
    drawn = jax.random.normal(stream_key, shape, jnp.float32) * spread
    if len(cuts) > 0:
        drawn = block_scale(stream_key, shape, cuts, -0.22, 0.18) * drawn
    return jnp.clip(drawn, min=-bound, max=bound).astype(kind)


def setup_inputs(seed: int = 0) -> dict:
    splits = jax.random.split(jax.random.key(seed), 12)
    return {
        "tokens": bell_draw(splits[0], (BATCH, LENGTH, D), 1.0, 6.0, ((0, 4), (1, 16))),
        "w_query": bell_draw(splits[1], (D, HQ * HD), D ** -0.5, 0.125, ((0, 64), (1, 2))),
        "w_key": bell_draw(splits[2], (D, KV * HD), D ** -0.5, 0.125, ((0, 64), (1, 2))),
        "w_value": bell_draw(splits[3], (D, KV * HD), D ** -0.5, 0.125, ((0, 64), (1, 2))),
        "w_output": bell_draw(splits[4], (HQ * HD, D), (HQ * HD // 8) ** -0.5, 0.375, ((0, 2), (1, 64))),
        "w_gate": bell_draw(splits[5], (D, FF), D ** -0.5, 0.125, ((0, 64), (1, 2))),
        "w_up": bell_draw(splits[6], (D, FF), D ** -0.5, 0.125, ((0, 64), (1, 2))),
        "w_down": bell_draw(splits[7], (FF, D), FF ** -0.5, 0.078125, ((0, 2), (1, 64))),
        "norm_attn": jnp.clip(1.0 + 0.1 * jax.random.normal(splits[8], (D,), jnp.float32), 0.5, 1.5).astype(jnp.bfloat16),
        "norm_ffn": jnp.clip(1.0 + 0.1 * jax.random.normal(splits[9], (D,), jnp.float32), 0.5, 1.5).astype(jnp.bfloat16),
        "cotangent": bell_draw(splits[10], (BATCH, LENGTH, D), 1.0, 6.0, ((0, 4), (1, 16))),
    }


epsilon = 1e-05
rope_base = 10000.0
masked_low = -1e+30
highest = lax.Precision.HIGHEST

@jax.custom_vjp
def low(v):
    return lax.optimization_barrier(v.astype(jnp.bfloat16)).astype(jnp.float32)

@jax.custom_vjp
def low_back(v):
    return v

def low_keep(v):
    return (low(v), None)

def low_pass(kept, grad):
    return (grad,)

def back_keep(v):
    return (v, None)

def back_low(kept, grad):
    return (low(grad),)
low.defvjp(low_keep, low_pass)
low_back.defvjp(back_keep, back_low)

def tables(positions, width):
    half_width = width // 2
    freqs = rope_base ** (-2.0 * jnp.arange(half_width, dtype=jnp.float32) / width)
    angles = positions[:, None] * freqs[None, :]
    cosine = jnp.cos(angles)
    sine = jnp.sin(angles)
    return (jnp.concatenate([cosine, cosine], -1), jnp.concatenate([sine, sine], -1))

def rotate(values, cosine, sine):
    half_width = values.shape[-1] // 2
    turned = jnp.concatenate([-values[..., half_width:], values[..., :half_width]], -1)
    return values * cosine[:, None, :] + turned * sine[:, None, :]

def matmul(left, right):
    return jnp.dot(left, right, precision=highest)

def sequence_layer(inputs, w_query, w_key, w_value, w_output, w_gate, w_up, w_down, gain_one, gain_two):
    length = inputs.shape[0]
    heads = w_query.shape[1] // HD
    kv_heads = w_key.shape[1] // HD
    group = heads // kv_heads
    scale = HD ** (-0.5)
    inverse_one = lax.rsqrt(lax.optimization_barrier(jnp.mean(inputs * inputs, axis=-1, keepdims=True)) + epsilon)
    normed_one = low(inputs * inverse_one * gain_one)
    cosine, sine = tables(jnp.arange(length).astype(jnp.float32), HD)
    query = low(rotate(low_back(matmul(normed_one, w_query)).reshape(length, heads, HD), cosine, sine))
    keys = low(rotate(low_back(matmul(normed_one, w_key)).reshape(length, kv_heads, HD), cosine, sine))
    values = low(low_back(matmul(normed_one, w_value))).reshape(length, kv_heads, HD)
    block = min(512, length)
    blocks = length // block
    grouped = query.reshape(blocks, block, kv_heads, group, HD)
    starts = jnp.arange(blocks, dtype=jnp.int32) * block
    key_pos = jnp.arange(length, dtype=jnp.int32)

    def attend(pair):
        query_block, start = pair
        scores = jnp.einsum('tgjd,sgd->gjts', query_block, keys, precision=highest)
        scores = low_back(scores) * scale
        query_pos = start + jnp.arange(block, dtype=jnp.int32)
        visible = key_pos[None, :] <= query_pos[:, None]
        scores = jnp.where(visible, scores, masked_low)
        top = lax.optimization_barrier(jnp.max(scores, axis=-1, keepdims=True))
        weights = jnp.exp(scores - top)
        probs = weights / lax.optimization_barrier(jnp.sum(weights, axis=-1, keepdims=True))
        mixed = jnp.einsum('gjts,sgd->tgjd', low(probs), values, precision=highest)
        return mixed.reshape(block, heads * HD)
    attn_raw = lax.map(jax.checkpoint(attend), (grouped, starts)).reshape(length, heads * HD)
    attn_low = low(low_back(attn_raw))
    branch_one = low_back(matmul(attn_low, w_output))
    middle = inputs + branch_one
    inverse_two = lax.rsqrt(lax.optimization_barrier(jnp.mean(middle * middle, axis=-1, keepdims=True)) + epsilon)
    normed_two = low(middle * inverse_two * gain_two)
    gate_lin = low_back(matmul(normed_two, w_gate))
    up_lin = low_back(matmul(normed_two, w_up))
    inner = low(gate_lin * jax.nn.sigmoid(gate_lin) * up_lin)
    return middle + matmul(inner, w_down)

def forward(tokens, w_query, w_key, w_value, w_output, w_gate, w_up, w_down, gain_one, gain_two):
    layer_fn = jax.checkpoint(sequence_layer)

    def per_sequence(sequence):
        return layer_fn(sequence, w_query, w_key, w_value, w_output, w_gate, w_up, w_down, gain_one, gain_two)
    return lax.map(per_sequence, tokens)

def reference(tokens, w_query, w_key, w_value, w_output, w_gate, w_up, w_down, norm_attn, norm_ffn, cotangent):
    prims = tuple((item.astype(jnp.float32) for item in (tokens, w_query, w_key, w_value, w_output, w_gate, w_up, w_down, norm_attn, norm_ffn)))
    result, pull = jax.vjp(forward, *prims)
    grads = pull(cotangent.astype(jnp.float32))
    return (result.astype(jnp.bfloat16), grads[0], grads[1], grads[2], grads[3], grads[4], grads[5], grads[6], grads[7], grads[8], grads[9])
```

```python
import functools

import jax
import jax.numpy as jnp
from jax import lax
from jax.experimental import pallas as pl
from jax.experimental.pallas import tpu as pltpu
from jax.sharding import Mesh, PartitionSpec as P

HD = 64
HEADS = 4
FF_BLOCK = 704
FF_PAD = 768
LOG2E = 1.4426950408889634
epsilon = 1e-05
rope_base = 10000.0
masked_low = -1e30
f32 = jnp.float32
bf16 = jnp.bfloat16

ALL = ("x", "z", "yh", "c")
MODEL = ("yh", "c")

NN = (((1,), (0,)), ((), ()))
NT = (((1,), (1,)), ((), ()))
TN = (((0,), (0,)), ((), ()))

VMEM = pl.BlockSpec(memory_space=pltpu.VMEM)
SMEM = pl.BlockSpec(memory_space=pltpu.SMEM)
BIG = pltpu.CompilerParams(vmem_limit_bytes=56 * 2**20)


def mm(a, b, dims):
    return lax.dot_general(a, b, dims, preferred_element_type=f32)


def turn(u, cosine, sine_signed):
    width = u.shape[-1]
    lane = lax.broadcasted_iota(jnp.int32, u.shape, 1)
    turned = jnp.where(
        lane % HD < HD // 2, pltpu.roll(u, width - HD // 2, 1), pltpu.roll(u, HD // 2, 1)
    )
    return u * cosine + turned * sine_signed


def qkv_kernel(x_ref, w_ref, cos_ref, sin_ref, q_ref, kv_ref):
    lin = mm(x_ref[...], w_ref[...], NN)
    cosine, sine = cos_ref[...], sin_ref[...]
    for part in range(2):
        cols = slice(part * 128, part * 128 + 128)
        q_ref[:, cols] = turn(lin[:, cols], cosine, sine).astype(bf16)
    kv = lin[:, 256:384]
    lane = lax.broadcasted_iota(jnp.int32, kv.shape, 1)
    kv_ref[...] = jnp.where(lane < HD, turn(kv, cosine, sine), kv).astype(bf16)


def qkv_project(x, w, cosine, sine):
    rows, depth = x.shape
    block = 256
    return pl.pallas_call(
        qkv_kernel,
        grid=(rows // block,),
        in_specs=[
            pl.BlockSpec((block, depth), lambda i: (i, 0)),
            pl.BlockSpec((depth, 384), lambda i: (0, 0)),
            pl.BlockSpec((block, 128), lambda i: (i, 0)),
            pl.BlockSpec((block, 128), lambda i: (i, 0)),
        ],
        out_specs=(
            pl.BlockSpec((block, 256), lambda i: (i, 0)),
            pl.BlockSpec((block, 128), lambda i: (i, 0)),
        ),
        out_shape=(
            jax.ShapeDtypeStruct((rows, 256), bf16),
            jax.ShapeDtypeStruct((rows, 128), bf16),
        ),
        cost_estimate=pl.CostEstimate(
            flops=2 * rows * depth * 384, bytes_accessed=6 * 2**20, transcendentals=0
        ),
        compiler_params=BIG,
        name="qkv_project",
    )(x, w, cosine, sine)


def attn_fwd_kernel(
    at_ref, q_ref, kv_ref, o_ref, ot_ref, lse_ref, q_pad, kvt, *, bq, bk
):
    rows = q_ref.shape[0]
    depth, flip = at_ref[0], at_ref[1]
    scale = HD**-0.5 * LOG2E
    for h in range(HEADS):
        q_pad[h, :, :HD] = q_ref[:, h * HD : (h + 1) * HD]
        q_pad[h, :, HD:] = jnp.zeros((rows, HD), bf16)

    def flip_over(b, _):
        kvt[b] = kv_ref[b].T
        return 0

    lax.fori_loop(0, depth + 1, flip_over, 0)
    pair = flip // bq

    def q_step(i, _):
        cols = pl.ds(pl.multiple_of(i * bq, bq), bq)
        queries = [q_pad[h, cols, :] for h in range(HEADS)]

        def block(b, offset, state, masked, count):
            keys = kv_ref[b, pl.ds(offset, count), :]
            values = kvt[b, HD:, pl.ds(offset, count)]
            scores = [mm(keys, queries[h], NT) * scale for h in range(HEADS)]
            if masked:
                k_pos = (lax.broadcasted_iota(jnp.int32, (count, bq), 0) + offset) ^ flip
                q_pos = (lax.broadcasted_iota(jnp.int32, (count, bq), 1) + i * bq) ^ flip
                visible = k_pos <= q_pos
                scores = [jnp.where(visible, s, masked_low) for s in scores]
            out = []
            for h in range(HEADS):
                top, total, acc = state[h]
                s = scores[h]
                new_top = jnp.maximum(top, jnp.max(s, axis=0, keepdims=True))
                p = jnp.exp2(s - new_top)
                fade = jnp.exp2(top - new_top)
                total = total * fade + jnp.sum(p, axis=0, keepdims=True)
                acc = acc * fade + mm(values, p.astype(bf16), NN)
                out.append((new_top, total, acc))
            return tuple(out)

        state = tuple(
            (
                jnp.full((1, bq), masked_low, f32),
                jnp.zeros((1, bq), f32),
                jnp.zeros((HD, bq), f32),
            )
            for _ in range(HEADS)
        )
        state = block(0, pl.multiple_of(i * bq, bq), state, True, bq)
        state = lax.fori_loop(
            0,
            i ^ pair,
            lambda j, st: block(0, pl.multiple_of((j ^ pair) * bq, bq), st, False, bq),
            state,
        )
        per = rows // bk
        state = lax.fori_loop(
            0,
            depth * per,
            lambda j, st: block(
                1 + j // per, pl.multiple_of((j % per) * bk, bk), st, False, bk
            ),
            state,
        )
        outs = []
        for h in range(HEADS):
            top, total, acc = state[h]
            lse_ref[pl.ds(h, 1), cols] = top + jnp.log2(total)
            outs.append(acc * (1.0 / total))
        o_t = jnp.concatenate(outs, 0)
        ot_ref[:, cols] = o_t
        o_ref[cols, :] = o_t.T.astype(bf16)
        return 0

    lax.fori_loop(0, rows // bq, q_step, 0)


def attn_fwd(at, q, kv):
    rows = q.shape[0]
    return pl.pallas_call(
        functools.partial(attn_fwd_kernel, bq=512, bk=512),
        out_shape=(
            jax.ShapeDtypeStruct((rows, HEADS * HD), bf16),
            jax.ShapeDtypeStruct((HEADS * HD, rows), f32),
            jax.ShapeDtypeStruct((HEADS, rows), f32),
        ),
        in_specs=[SMEM, VMEM, VMEM],
        out_specs=(VMEM, VMEM, VMEM),
        scratch_shapes=[
            pltpu.VMEM((HEADS, rows, 128), bf16),
            pltpu.VMEM((4, 128, rows), bf16),
        ],
        cost_estimate=pl.CostEstimate(
            flops=20 * 10**9, bytes_accessed=6 * 2**20, transcendentals=12 * 10**6
        ),
        compiler_params=BIG,
        name="attn_fwd",
    )(at, q, kv)


def attn_bwd_kernel(
    at_ref, q_ref, kv_ref, do_ref, ot_ref, lse_ref, dq_ref, dkv_ref,
    q_pad, do_pad, kt, dqt, delta, *, bq, bk,
):
    rows = q_ref.shape[0]
    depth, flip = at_ref[0], at_ref[1]
    scale = HD**-0.5 * LOG2E
    nothing = jnp.zeros((rows, HD), bf16)
    for h in range(HEADS):
        cols = slice(h * HD, (h + 1) * HD)
        q_pad[h, :, :HD] = q_ref[:, cols]
        q_pad[h, :, HD:] = nothing
        do_pad[h, :, :HD] = nothing
        do_pad[h, :, HD:] = do_ref[:, cols]
    do_t = do_ref[...].astype(f32).T
    for h in range(HEADS):
        cols = slice(h * HD, (h + 1) * HD)
        delta[pl.ds(h, 1), :] = jnp.sum(do_t[cols] * ot_ref[cols, :], axis=0, keepdims=True)

    def flip_over(b, _):
        kt[b] = kv_ref[b].T[:HD]
        return 0

    lax.fori_loop(0, depth + 1, flip_over, 0)
    dqt[...] = jnp.zeros_like(dqt)
    pair = flip // bq

    def tile(b, offset, i, masked, count, dkv):
        keys = kv_ref[b, pl.ds(offset, count), :]
        keys_t = kt[b, :, pl.ds(offset, count)]
        at = pl.ds(pl.multiple_of(i * bq, bq), bq)
        if masked:
            k_pos = (lax.broadcasted_iota(jnp.int32, (count, bq), 0) + offset) ^ flip
            q_pos = (lax.broadcasted_iota(jnp.int32, (count, bq), 1) + i * bq) ^ flip
            visible = k_pos <= q_pos
        for h in range(HEADS):
            query, grad = q_pad[h, at, :], do_pad[h, at, :]
            s = mm(keys, query, NT)
            p = jnp.exp2(s * scale - lse_ref[pl.ds(h, 1), at])
            if masked:
                p = jnp.where(visible, p, 0.0)
            dp = mm(keys, grad, NT)
            ds = (p * (dp - delta[pl.ds(h, 1), at])).astype(bf16)
            dkv = dkv + mm(p.astype(bf16), grad, NN) + mm(ds, query, NN)
            dqt[h * HD : (h + 1) * HD, at] += mm(keys_t, ds, NN)
        return dkv

    lane = lax.broadcasted_iota(jnp.int32, (1, 128), 1)
    out_scale = jnp.where(lane < HD, HD**-0.5, 1.0)
    per = rows // bk

    def far(j, _):
        b, offset = 1 + j // per, pl.multiple_of((j % per) * bk, bk)
        dkv = lax.fori_loop(
            0,
            rows // bq,
            lambda i, st: tile(b, offset, i, False, bk, st),
            jnp.zeros((bk, 128), f32),
        )
        dkv_ref[b, pl.ds(offset, bk), :] = (dkv * out_scale).astype(bf16)
        return 0

    lax.fori_loop(0, depth * per, far, 0)

    def clear(b, _):
        dkv_ref[b] = jnp.zeros(dkv_ref.shape[1:], bf16)
        return 0

    lax.fori_loop(1 + depth, dkv_ref.shape[0], clear, 0)

    def near(j, _):
        offset = pl.multiple_of(j * bq, bq)
        dkv = tile(0, offset, j, True, bq, jnp.zeros((bq, 128), f32))
        dkv = lax.fori_loop(
            (j ^ pair) + 1,
            rows // bq,
            lambda i, st: tile(0, offset, i ^ pair, False, bq, st),
            dkv,
        )
        dkv_ref[0, pl.ds(offset, bq), :] = (dkv * out_scale).astype(bf16)
        return 0

    lax.fori_loop(0, rows // bq, near, 0)
    dq_ref[...] = dqt[...].T * HD**-0.5


def attn_bwd(at, q, kv, do, ot, lse):
    rows = q.shape[0]
    return pl.pallas_call(
        functools.partial(attn_bwd_kernel, bq=512, bk=512),
        out_shape=(
            jax.ShapeDtypeStruct((rows, HEADS * HD), f32),
            jax.ShapeDtypeStruct(kv.shape, bf16),
        ),
        in_specs=[SMEM] + [VMEM] * 5,
        out_specs=(VMEM, VMEM),
        scratch_shapes=[
            pltpu.VMEM((HEADS, rows, 128), bf16),
            pltpu.VMEM((HEADS, rows, 128), bf16),
            pltpu.VMEM((4, HD, rows), bf16),
            pltpu.VMEM((HEADS * HD, rows), f32),
            pltpu.VMEM((HEADS, rows), f32),
        ],
        cost_estimate=pl.CostEstimate(
            flops=50 * 10**9, bytes_accessed=8 * 2**20, transcendentals=12 * 10**6
        ),
        compiler_params=BIG,
        name="attn_bwd",
    )(at, q, kv, do, ot, lse)


def ffn_kernel(hn_ref, cot_ref, w_ref, hid_ref, dgu_ref, y_ref, dn_ref):
    hn, cot = hn_ref[...], cot_ref[...]
    w_gate = w_ref[:, :FF_PAD]
    w_up = w_ref[:, FF_PAD : 2 * FF_PAD]
    w_down = w_ref[:, 2 * FF_PAD :]
    gate = mm(hn, w_gate, NN)
    up = mm(hn, w_up, NN)
    dhid = mm(cot, w_down, NN)
    sg = 1.0 / (1.0 + jnp.exp(-gate))
    act = gate * sg
    hid = (act * up).astype(bf16)
    dgate = (dhid * up * sg * (1.0 + gate * (1.0 - sg))).astype(bf16)
    dup = (dhid * act).astype(bf16)
    hid_ref[...] = hid
    dgu_ref[:, :FF_PAD] = dgate
    dgu_ref[:, FF_PAD:] = dup
    dn_ref[...] = (mm(dgate, w_gate, NT) + mm(dup, w_up, NT)).astype(bf16)
    y_ref[...] = mm(hid, w_down, NT).astype(bf16)


def ffn(hn, cot, w):
    rows, depth = hn.shape
    block = 256
    rowwise = lambda width: pl.BlockSpec((block, width), lambda i: (i, 0))
    return pl.pallas_call(
        ffn_kernel,
        grid=(rows // block,),
        in_specs=[
            rowwise(depth),
            rowwise(depth),
            pl.BlockSpec(w.shape, lambda i: (0, 0), pipeline_mode=pl.Buffered(1)),
        ],
        out_specs=(rowwise(FF_PAD), rowwise(2 * FF_PAD), rowwise(depth), rowwise(depth)),
        out_shape=(
            jax.ShapeDtypeStruct((rows, FF_PAD), bf16),
            jax.ShapeDtypeStruct((rows, 2 * FF_PAD), bf16),
            jax.ShapeDtypeStruct((rows, depth), bf16),
            jax.ShapeDtypeStruct((rows, depth), bf16),
        ),
        cost_estimate=pl.CostEstimate(
            flops=12 * rows * depth * FF_PAD,
            bytes_accessed=30 * 2**20,
            transcendentals=rows * FF_PAD,
        ),
        compiler_params=BIG,
        name="ffn",
    )(hn, cot, w)


def ffn_grad_kernel(hn_ref, cot_ref, dgu_ref, hid_ref, out_ref):
    out_ref[:, : 2 * FF_PAD] = mm(hn_ref[...], dgu_ref[...], TN).astype(bf16)
    out_ref[:, 2 * FF_PAD :] = mm(cot_ref[...], hid_ref[...], TN).astype(bf16)


def ffn_grad(hn, cot, dgu, hid):
    rows, depth = hn.shape
    block = 256
    return pl.pallas_call(
        ffn_grad_kernel,
        grid=(depth // block,),
        in_specs=[
            pl.BlockSpec((rows, block), lambda i: (0, i)),
            pl.BlockSpec((rows, block), lambda i: (0, i)),
            pl.BlockSpec((rows, 2 * FF_PAD), lambda i: (0, 0)),
            pl.BlockSpec((rows, FF_PAD), lambda i: (0, 0)),
        ],
        out_specs=pl.BlockSpec((block, 3 * FF_PAD), lambda i: (i, 0)),
        out_shape=jax.ShapeDtypeStruct((depth, 3 * FF_PAD), bf16),
        cost_estimate=pl.CostEstimate(
            flops=6 * rows * depth * FF_PAD, bytes_accessed=24 * 2**20, transcendentals=0
        ),
        compiler_params=BIG,
        name="ffn_grad",
    )(hn, cot, dgu, hid)


def dqkv_kernel(at_ref, dq_ref, dkv_ref, w_ref, cos_ref, sin_ref, dqkv_ref, dn_ref):
    cosine, sine = cos_ref[...], -sin_ref[...]
    core = at_ref[2]
    for part in range(2):
        cols = slice(part * 128, part * 128 + 128)
        dqkv_ref[:, cols] = turn(dq_ref[:, cols], cosine, sine).astype(bf16)
    dkv = dkv_ref[...]
    lane = lax.broadcasted_iota(jnp.int32, dkv.shape, 1)
    is_key = lane < HD
    turned = jnp.where(is_key, turn(dkv, cosine, sine), dkv)
    mine = jnp.where(is_key, 1 - core, core) > 0
    dqkv_ref[:, 256:] = jnp.where(mine, turned, 0.0).astype(bf16)
    dn_ref[...] = mm(dqkv_ref[...], w_ref[...], NT).astype(bf16)


def dqkv_project(at, dq, dkv, w, cosine, sine):
    rows, depth = dq.shape[0], w.shape[0]
    block = 256
    rowwise = lambda width: pl.BlockSpec((block, width), lambda i: (i, 0))
    return pl.pallas_call(
        dqkv_kernel,
        grid=(rows // block,),
        in_specs=[
            SMEM,
            rowwise(256),
            rowwise(128),
            pl.BlockSpec(w.shape, lambda i: (0, 0)),
            rowwise(128),
            rowwise(128),
        ],
        out_specs=(rowwise(384), rowwise(depth)),
        out_shape=(
            jax.ShapeDtypeStruct((rows, 384), bf16),
            jax.ShapeDtypeStruct((rows, depth), bf16),
        ),
        cost_estimate=pl.CostEstimate(
            flops=2 * rows * depth * 384, bytes_accessed=8 * 2**20, transcendentals=0
        ),
        compiler_params=BIG,
        name="dqkv_project",
    )(at, dq, dkv, w, cosine, sine)


def swap(value, axes):
    count = 2 ** len(axes)
    return lax.ppermute(value, axes, [(i, count - 1 - i) for i in range(count)])


def shifted(value, steps):
    first, last = max(0, -steps), min(4, 4 - steps)
    return lax.ppermute(value, "z", [(i, i + steps) for i in range(first, last)])


def gather_group(own):
    by_l = swap(own, ("yl",))
    by_d = swap(own, ("yh", "yl"))
    by_h = swap(own, ("yh",))
    by_c = swap(own, ("c",))
    return jnp.concatenate(
        [own, by_l, by_c, swap(by_l, ("c",)), by_h, by_d, swap(by_h, ("c",)), swap(by_d, ("c",))], 0
    )


def scatter_group(partial):
    n = partial.shape[0] // 8
    near = swap(partial[2 * n : 4 * n], ("c",))
    far = swap(partial[6 * n : 8 * n], ("c",))
    low = partial[: 2 * n].astype(f32) + near.astype(f32)
    high = (partial[4 * n : 6 * n].astype(f32) + far.astype(f32)).astype(bf16)
    by_l = swap(low[n:].astype(bf16), ("yl",))
    by_d = swap(high[n:], ("yh", "yl"))
    by_h = swap(high[:n], ("yh",))
    return low[:n] + by_l.astype(f32) + by_d.astype(f32) + by_h.astype(f32)


def gather_pieces(own):
    by_c = swap(own, ("c",))
    by_h = swap(own, ("yh",))
    return jnp.concatenate([own, by_c, by_h, swap(by_h, ("c",))], 0)


def to_owners(grad, width):
    parts = lax.all_to_all(grad.reshape(64, 32, width), ALL, 0, 0)
    return jnp.sum(parts.reshape(16, 4, 32, width).astype(f32), 0)


def both_halves(own, other, yl):
    rows = own.shape[0]
    whole = jnp.concatenate([own, other, own], 0)
    return lax.dynamic_slice_in_dim(whole, yl * rows, 2 * rows, 0)


def on_device(
    tokens, w_query, w_key, w_value, w_output, w_gate, w_up, w_down, norm_attn, norm_ffn, cotangent
):
    z, yh = lax.axis_index("z"), lax.axis_index("yh")
    core, yl = lax.axis_index("c"), lax.axis_index("yl")
    gain_one = norm_attn.astype(f32)[:, None]
    gain_two = norm_ffn.astype(f32)[:, None]
    flip = (yh * 4 + core * 2 + yl) * 128
    at = jnp.stack([z, flip, core]).astype(jnp.int32)

    def by_model(w):
        return w.reshape(32, 4, -1).transpose(1, 0, 2)

    def by_head(w):
        return jnp.repeat(w.reshape(32, 2, HD).transpose(1, 0, 2), 2, axis=0)

    scaled = lambda w, gain: (w.astype(f32) * gain).astype(bf16)
    qkv_rows = jnp.concatenate(
        [
            by_model(scaled(w_query, gain_one)),
            by_head(scaled(w_key, gain_one)),
            by_head(scaled(w_value, gain_one)),
        ],
        -1,
    )
    w_qkv = lax.all_to_all(
        jnp.broadcast_to(qkv_rows[None], (16, 4, 32, 384)).reshape(64, 32, 384), ALL, 0, 0
    ).reshape(2048, 384)

    def padded(w):
        return jnp.pad(by_model(w), ((0, 0), (0, 0), (0, FF_PAD - FF_BLOCK)))

    other_rows = jnp.concatenate(
        [
            by_model(w_output.T),
            padded(scaled(w_gate, gain_two)),
            padded(scaled(w_up, gain_two)),
            padded(w_down.T),
        ],
        -1,
    )
    other_rows = lax.all_to_all(other_rows, MODEL, 0, 0).reshape(128, 256 + 3 * FF_PAD)
    w_out = lax.all_gather(other_rows[:, :256], ("x", "z"), axis=0, tiled=True)
    w_ffn = lax.all_gather(other_rows[:, 256:], ("x", "z"), axis=0, tiled=True)

    both = lambda a: lax.dynamic_slice_in_dim(jnp.concatenate([a, a], 0), yl * 128, 256, 0)
    inputs = both(tokens[0]).astype(f32)
    inverse_one = lax.rsqrt(jnp.mean(inputs * inputs, axis=-1, keepdims=True) + epsilon)
    xh = gather_pieces((inputs * inverse_one).astype(bf16))
    inputs, inverse_one = inputs[:128], inverse_one[:128]
    cot_here = both(cotangent[0])
    cot = gather_pieces(cot_here)
    grad_top = cot_here[:128].astype(f32)

    positions = (z * 1024 + (jnp.arange(1024, dtype=jnp.int32) ^ flip)).astype(f32)
    freqs = rope_base ** (-2.0 * jnp.arange(HD // 2, dtype=f32) / HD)
    angles = positions[:, None] * freqs[None, :]
    cosine, sine = jnp.cos(angles), jnp.sin(angles)
    cosine = jnp.concatenate([cosine] * 4, -1)
    sine = jnp.concatenate([-sine, sine, -sine, sine], -1)

    q, kv = qkv_project(xh, w_qkv, cosine, sine)
    kv = jnp.stack([kv, shifted(kv, 1), shifted(kv, 2), shifted(kv, 3)])
    ob, o_t, lse = attn_fwd(at, q, kv)
    branch_one = scatter_group(mm(ob, w_out, NT).astype(bf16))
    middle = inputs + branch_one
    inverse_two = lax.rsqrt(jnp.mean(middle * middle, axis=-1, keepdims=True) + epsilon)
    hn = gather_group((middle * inverse_two).astype(bf16))

    hid, dgu, y, dn2 = ffn(hn, cot, w_ffn)
    dn2 = scatter_group(dn2)
    grad_ffn = ffn_grad(hn, cot, dgu, hid)
    grad_ffn = lax.psum_scatter(grad_ffn, ("x", "z"), scatter_dimension=0, tiled=True)
    grad_ffn = lax.all_to_all(grad_ffn.reshape(4, 32, 3 * FF_PAD), MODEL, 0, 0)
    dh = (
        grad_top
        + inverse_two * dn2
        - middle * inverse_two**3 * jnp.mean(dn2 * middle, axis=-1, keepdims=True)
    )
    gain_grad_two = jnp.sum(dn2 * middle * inverse_two, axis=0)
    dh_all = gather_group(dh.astype(bf16))
    block_out = (middle + scatter_group(y)).astype(bf16)
    block_out = both_halves(block_out, swap(block_out, ("yl",)), yl)

    do = mm(dh_all, w_out, NN).astype(bf16)
    grad_out = to_owners(mm(dh_all, ob, TN).astype(bf16), 256)
    dq, dkv = attn_bwd(at, q, kv, do, o_t, lse)
    dkv = (
        dkv[0].astype(f32)
        + shifted(dkv[1], -1).astype(f32)
        + shifted(dkv[2], -2).astype(f32)
        + shifted(dkv[3], -3).astype(f32)
    )
    other = swap(dkv, ("c",)).reshape(2, 2, 256, 2 * HD)[:, ::-1].reshape(1024, 2 * HD)
    dkv = dkv + other
    dqkv, dn1 = dqkv_project(at, dq, dkv, w_qkv, cosine, sine)
    grad_qkv = to_owners(mm(xh, dqkv, TN).astype(bf16), 384)
    dn1 = scatter_group(dn1)
    input_grad = (
        dh
        + inverse_one * dn1
        - inputs * inverse_one**3 * jnp.mean(dn1 * inputs, axis=-1, keepdims=True)
    )
    gain_grad_one = jnp.sum(dn1 * inputs * inverse_one, axis=0)
    input_grad = both_halves(input_grad, swap(input_grad, ("yl",)), yl)

    gains = jnp.stack([gain_grad_one.reshape(64, 32), gain_grad_two.reshape(64, 32)], 1)
    gains = jnp.sum(lax.all_to_all(gains.reshape(64, 64), ALL, 0, 0, tiled=True), 0)
    gains = gains + swap(gains, ("yl",))

    def joined(parts):
        return parts.transpose(1, 0, 2).reshape(32, -1)

    grad_ffn = grad_ffn.astype(f32)
    ffn_part = lambda k: joined(grad_ffn[:, :, k * FF_PAD : k * FF_PAD + FF_BLOCK])
    by_core = grad_qkv[:, :, 256:].reshape(2, 2, 32, 2 * HD).sum(1)
    return (
        block_out[None],
        input_grad[None],
        joined(grad_qkv[:, :, :256]) * gain_one,
        joined(by_core[:, :, :HD]) * gain_one,
        joined(by_core[:, :, HD:]) * gain_one,
        joined(grad_out).T,
        ffn_part(0) * gain_two,
        ffn_part(1) * gain_two,
        ffn_part(2).T,
        gains[:32] / gain_one[:, 0],
        gains[32:] / gain_two[:, 0],
    )


def solution(mesh):
    mesh = Mesh(mesh.devices.reshape(4, 4, 2, 2, 2), ("x", "z", "yh", "c", "yl"))
    ctx = ("z", "yh", "c")
    rows, cols = P(ALL, "yl"), P("yl", ALL)
    seq = P("x", ctx, None)
    vec = P(ALL)
    in_specs = (seq, rows, rows, rows, cols, rows, rows, cols, vec, vec, seq)
    out_specs = (seq, seq, rows, rows, rows, cols, rows, rows, cols, vec, vec)
    return jax.shard_map(
        on_device, mesh=mesh, in_specs=in_specs, out_specs=out_specs, check_vma=False
    )
```

```python
import functools

import jax
import jax.numpy as jnp
from jax import lax
from jax.experimental import pallas as pl
from jax.experimental.pallas import tpu as pltpu
from jax.sharding import Mesh, PartitionSpec as P

HD = 64
HEADS = 4
FF_BLOCK = 704
FF_PAD = 768
OUT = 256
LOG2E = 1.4426950408889634
epsilon = 1e-05
rope_base = 10000.0
masked_low = -1e30
f32 = jnp.float32
bf16 = jnp.bfloat16

ALL = ("x", "z", "yh", "c")
MODEL = ("yh", "c")

NN = (((1,), (0,)), ((), ()))
NT = (((1,), (1,)), ((), ()))
TN = (((0,), (0,)), ((), ()))

VMEM = pl.BlockSpec(memory_space=pltpu.VMEM)
SMEM = pl.BlockSpec(memory_space=pltpu.SMEM)
BIG = pltpu.CompilerParams(vmem_limit_bytes=56 * 2**20)


def mm(a, b, dims):
    return lax.dot_general(a, b, dims, preferred_element_type=f32)


def turn(u, cosine, sine_signed):
    width = u.shape[-1]
    lane = lax.broadcasted_iota(jnp.int32, u.shape, 1)
    turned = jnp.where(
        lane % HD < HD // 2, pltpu.roll(u, width - HD // 2, 1), pltpu.roll(u, HD // 2, 1)
    )
    return u * cosine + turned * sine_signed


def qkv_kernel(x0, x1, x2, x3, w_ref, cos_ref, sin_ref, q_ref, kv_ref):
    scale = HD**-0.5 * LOG2E
    for part, x_ref in enumerate((x0, x1, x2, x3)):
        rows = slice(part * 256, part * 256 + 256)
        lin = mm(x_ref[...], w_ref[...], NN)
        cosine, sine = cos_ref[rows], sin_ref[rows]
        for half in range(2):
            cols = slice(half * 128, half * 128 + 128)
            q_ref[rows, cols] = (turn(lin[:, cols], cosine, sine) * scale).astype(bf16)
        kv = lin[:, 256:384]
        lane = lax.broadcasted_iota(jnp.int32, kv.shape, 1)
        kv_ref[rows, :] = jnp.where(lane < HD, turn(kv, cosine, sine), kv).astype(bf16)


def qkv_project(xs, w, cosine, sine):
    return pl.pallas_call(
        qkv_kernel,
        in_specs=[VMEM] * 7,
        out_specs=(VMEM, VMEM),
        out_shape=(
            jax.ShapeDtypeStruct((1024, 256), bf16),
            jax.ShapeDtypeStruct((1024, 128), bf16),
        ),
        cost_estimate=pl.CostEstimate(
            flops=2 * 1024 * 2048 * 384, bytes_accessed=6 * 2**20, transcendentals=0
        ),
        compiler_params=BIG,
        name="qkv_project",
    )(*xs, w, cosine, sine)


def attn_fwd_kernel(
    at_ref, q_ref, kv0, kv1, kv2, kv3, o_ref, ot_ref, lse_ref, q_pad, keys_all, values_t, *, bq, bk
):
    rows = q_ref.shape[0]
    depth, flip = at_ref[0], at_ref[1]
    for h in range(HEADS):
        q_pad[h, :, :HD] = q_ref[:, h * HD : (h + 1) * HD]
        q_pad[h, :, HD:] = jnp.zeros((rows, HD), bf16)
    for b, kv_ref in enumerate((kv0, kv1, kv2, kv3)):

        @pl.when(depth >= b)
        def _():
            keys_all[b] = kv_ref[...]
            values_t[b, :HD] = kv_ref[...].T[HD:]
            values_t[b, HD:] = jnp.ones((16, rows), bf16)

    pair = flip // bq

    def q_step(i, _):
        cols = pl.ds(pl.multiple_of(i * bq, bq), bq)
        queries = [q_pad[h, cols, :] for h in range(HEADS)]

        def block(b, offset, state, masked, count):
            keys = keys_all[b, pl.ds(offset, count), :]
            values = values_t[b, :, pl.ds(offset, count)]
            scores = [mm(keys, queries[h], NT) for h in range(HEADS)]
            if masked:
                k_pos = (lax.broadcasted_iota(jnp.int32, (count, bq), 0) + offset) ^ flip
                q_pos = (lax.broadcasted_iota(jnp.int32, (count, bq), 1) + i * bq) ^ flip
                visible = k_pos <= q_pos
                scores = [jnp.where(visible, s, masked_low) for s in scores]
            out = []
            for h in range(HEADS):
                top, acc = state[h]
                s = scores[h]
                new_top = jnp.maximum(top, jnp.max(s, axis=0, keepdims=True))
                p = jnp.exp2(s - new_top).astype(bf16)
                acc = acc * jnp.exp2(top - new_top) + mm(values, p, NN)
                out.append((new_top, acc))
            return tuple(out)

        state = tuple(
            (jnp.full((1, bq), masked_low, f32), jnp.zeros((HD + 16, bq), f32))
            for _ in range(HEADS)
        )
        state = block(0, pl.multiple_of(i * bq, bq), state, True, bq)
        state = lax.fori_loop(
            0,
            i ^ pair,
            lambda j, st: block(0, pl.multiple_of((j ^ pair) * bq, bq), st, False, bq),
            state,
        )
        per = rows // bk
        state = lax.fori_loop(
            0,
            depth * per,
            lambda j, st: block(
                1 + j // per, pl.multiple_of((j % per) * bk, bk), st, False, bk
            ),
            state,
        )
        outs = []
        for h in range(HEADS):
            top, acc = state[h]
            total = acc[HD : HD + 1]
            lse_ref[pl.ds(h, 1), cols] = top + jnp.log2(total)
            outs.append(acc[:HD] * (1.0 / total))
        o_t = jnp.concatenate(outs, 0)
        ot_ref[:, cols] = o_t
        o_ref[cols, :] = o_t.T.astype(bf16)
        return 0

    lax.fori_loop(0, rows // bq, q_step, 0)


def attn_fwd(at, q, kvs):
    rows = q.shape[0]
    return pl.pallas_call(
        functools.partial(attn_fwd_kernel, bq=512, bk=512),
        out_shape=(
            jax.ShapeDtypeStruct((rows, HEADS * HD), bf16),
            jax.ShapeDtypeStruct((HEADS * HD, rows), f32),
            jax.ShapeDtypeStruct((HEADS, rows), f32),
        ),
        in_specs=[SMEM] + [VMEM] * 5,
        out_specs=(VMEM,) * 3,
        scratch_shapes=[
            pltpu.VMEM((HEADS, rows, 128), bf16),
            pltpu.VMEM((4, rows, 128), bf16),
            pltpu.VMEM((4, HD + 16, rows), bf16),
        ],
        cost_estimate=pl.CostEstimate(
            flops=25 * 10**9, bytes_accessed=6 * 2**20, transcendentals=12 * 10**6
        ),
        compiler_params=BIG,
        name="attn_fwd",
    )(at, q, *kvs)


def branch_kernel(o_ref, w_ref, a0, a1, a2, a3):
    for k, out_ref in enumerate((a0, a1, a2, a3)):
        @pl.when(pl.program_id(0) == k)
        def _():
            out_ref[...] = mm(o_ref[...], w_ref[...], NT).astype(bf16)


def branch_project(o, w):
    depth = w.shape[0]
    part = jax.ShapeDtypeStruct((256, depth), bf16)
    return pl.pallas_call(
        branch_kernel,
        grid=(4,),
        in_specs=[pl.BlockSpec((256, OUT), lambda i: (i, 0)), VMEM],
        out_specs=(pl.BlockSpec((256, depth), lambda i: (0, 0)),) * 4,
        out_shape=(part,) * 4,
        cost_estimate=pl.CostEstimate(
            flops=2 * 1024 * depth * OUT, bytes_accessed=6 * 2**20, transcendentals=0
        ),
        compiler_params=BIG,
        name="branch_project",
    )(o, w)


def attn_bwd_kernel(
    at_ref, q_ref, kv0, kv1, kv2, kv3, do_ref, ot_ref, lse_ref,
    dq_ref, dkv0, dkv1, dkv2, dkv3,
    q_pad, do_pad, keys_all, keys_t, dkv_all, dqt, delta, *, bq, bk,
):
    rows = q_ref.shape[0]
    depth, flip = at_ref[0], at_ref[1]
    nothing = jnp.zeros((rows, HD), bf16)
    for h in range(HEADS):
        cols = slice(h * HD, (h + 1) * HD)
        q_pad[h, :, :HD] = q_ref[:, cols]
        q_pad[h, :, HD:] = nothing
        do_pad[h, :, :HD] = nothing
        do_pad[h, :, HD:] = do_ref[:, cols]
    do_t = do_ref[...].astype(f32).T
    for h in range(HEADS):
        cols = slice(h * HD, (h + 1) * HD)
        delta[pl.ds(h, 1), :] = jnp.sum(do_t[cols] * ot_ref[cols, :], axis=0, keepdims=True)
    for b, kv_ref in enumerate((kv0, kv1, kv2, kv3)):

        @pl.when(depth >= b)
        def _():
            keys_all[b] = kv_ref[...]
            keys_t[b] = kv_ref[...].T[:HD]

    dqt[...] = jnp.zeros_like(dqt)
    pair = flip // bq

    def tile(b, offset, i, masked, count, dkv):
        keys = keys_all[b, pl.ds(offset, count), :]
        turned = keys_t[b, :, pl.ds(offset, count)]
        at = pl.ds(pl.multiple_of(i * bq, bq), bq)
        if masked:
            k_pos = (lax.broadcasted_iota(jnp.int32, (count, bq), 0) + offset) ^ flip
            q_pos = (lax.broadcasted_iota(jnp.int32, (count, bq), 1) + i * bq) ^ flip
            visible = k_pos <= q_pos
        for h in range(HEADS):
            query, grad = q_pad[h, at, :], do_pad[h, at, :]
            p = jnp.exp2(mm(keys, query, NT) - lse_ref[pl.ds(h, 1), at])
            if masked:
                p = jnp.where(visible, p, 0.0)
            dp = mm(keys, grad, NT)
            ds = (p * (dp - delta[pl.ds(h, 1), at])).astype(bf16)
            dkv = dkv + mm(p.astype(bf16), grad, NN) + mm(ds, query, NN)
            dqt[h * HD : (h + 1) * HD, at] += mm(turned, ds, NN)
        return dkv

    lane = lax.broadcasted_iota(jnp.int32, (1, 128), 1)
    out_scale = jnp.where(lane < HD, 1.0 / LOG2E, 1.0)
    per = rows // bk

    def far(j, _):
        b, offset = 1 + j // per, pl.multiple_of((j % per) * bk, bk)
        dkv = lax.fori_loop(
            0,
            rows // bq,
            lambda i, st: tile(b, offset, i, False, bk, st),
            jnp.zeros((bk, 128), f32),
        )
        dkv_all[b, pl.ds(offset, bk), :] = (dkv * out_scale).astype(bf16)
        return 0

    lax.fori_loop(0, depth * per, far, 0)

    def near(j, _):
        offset = pl.multiple_of(j * bq, bq)
        dkv = tile(0, offset, j, True, bq, jnp.zeros((bq, 128), f32))
        dkv = lax.fori_loop(
            (j ^ pair) + 1,
            rows // bq,
            lambda i, st: tile(0, offset, i ^ pair, False, bq, st),
            dkv,
        )
        dkv_all[0, pl.ds(offset, bq), :] = (dkv * out_scale).astype(bf16)
        return 0

    lax.fori_loop(0, rows // bq, near, 0)
    dq_ref[...] = dqt[...].T * HD**-0.5
    for b, out_ref in enumerate((dkv0, dkv1, dkv2, dkv3)):
        out_ref[...] = dkv_all[b]


def attn_bwd(at, q, kvs, do, ot, lse):
    rows = q.shape[0]
    block = jax.ShapeDtypeStruct(kvs[0].shape, bf16)
    return pl.pallas_call(
        functools.partial(attn_bwd_kernel, bq=512, bk=512),
        out_shape=(jax.ShapeDtypeStruct((rows, HEADS * HD), f32), block, block, block, block),
        in_specs=[SMEM] + [VMEM] * 8,
        out_specs=(VMEM,) * 5,
        scratch_shapes=[
            pltpu.VMEM((HEADS, rows, 128), bf16),
            pltpu.VMEM((HEADS, rows, 128), bf16),
            pltpu.VMEM((4, rows, 128), bf16),
            pltpu.VMEM((4, HD, rows), bf16),
            pltpu.VMEM((4, rows, 128), bf16),
            pltpu.VMEM((HEADS * HD, rows), f32),
            pltpu.VMEM((HEADS, rows), f32),
        ],
        cost_estimate=pl.CostEstimate(
            flops=50 * 10**9, bytes_accessed=8 * 2**20, transcendentals=12 * 10**6
        ),
        compiler_params=BIG,
        name="attn_bwd",
    )(at, q, *kvs, do, ot, lse)


def ffn_kernel(*refs):
    hns, cots, w_hbm = refs[:8], refs[8:12], refs[12]
    hid_ref, dgu_ref = refs[13:15]
    ys, dns = refs[15:19], refs[19:23]
    hn_buf, cot_buf, y_buf, dn_buf, w_ref, w_sems, in_sems, out_sems = refs[23:]
    step = pl.program_id(0)
    slot = lax.rem(step, 2)
    parts = [slice(k * FF_PAD, (k + 1) * FF_PAD) for k in range(3)]
    weights = [
        pltpu.make_async_copy(w_hbm.at[:, parts[k]], w_ref.at[:, parts[k]], w_sems.at[k])
        for k in range(3)
    ]

    def fetch(k):
        b = k % 2
        return [
            pltpu.make_async_copy(hns[2 * k], hn_buf.at[b, :128], in_sems.at[b, 0]),
            pltpu.make_async_copy(hns[2 * k + 1], hn_buf.at[b, 128:], in_sems.at[b, 1]),
            pltpu.make_async_copy(cots[k], cot_buf.at[b], in_sems.at[b, 2]),
        ]

    def flush(k):
        b = k % 2
        return [
            pltpu.make_async_copy(y_buf.at[b], ys[k], out_sems.at[b, 0]),
            pltpu.make_async_copy(dn_buf.at[b], dns[k], out_sems.at[b, 1]),
        ]

    def start(copies):
        for copy in copies:
            copy.start()

    def wait(copies):
        for copy in copies:
            copy.wait()

    def arrived(k):
        @pl.when(step == 0)
        def _():
            weights[k].wait()

    for k in range(4):

        @pl.when(step == k)
        def _():
            if k == 0:
                start(fetch(0))
                start(weights)
            if k < 3:
                start(fetch(k + 1))
            wait(fetch(k))

    hn, cot = hn_buf[slot], cot_buf[slot]
    arrived(0)
    gate = mm(hn, w_ref[:, parts[0]], NN)
    arrived(1)
    up = mm(hn, w_ref[:, parts[1]], NN)
    arrived(2)
    dhid = mm(cot, w_ref[:, parts[2]], NN)
    sg = 1.0 / (1.0 + jnp.exp(-gate))
    act = gate * sg
    hid = (act * up).astype(bf16)
    dgate = (dhid * up * sg * (1.0 + gate * (1.0 - sg))).astype(bf16)
    dup = (dhid * act).astype(bf16)
    hid_ref[...] = hid
    dgu_ref[:, parts[0]] = dgate
    dgu_ref[:, parts[1]] = dup
    for k in (2, 3):

        @pl.when(step == k)
        def _():
            wait(flush(k - 2))

    dn_buf[slot] = (mm(dgate, w_ref[:, parts[0]], NT) + mm(dup, w_ref[:, parts[1]], NT)).astype(
        bf16
    )
    y_buf[slot] = mm(hid, w_ref[:, parts[2]], NT).astype(bf16)
    for k in range(4):

        @pl.when(step == k)
        def _():
            start(flush(k))
            if k == 3:
                wait(flush(2))
                wait(flush(3))


def ffn(hns, cots, w):
    depth = w.shape[0]
    rowwise = lambda width: pl.BlockSpec((256, width), lambda i: (i, 0))
    hbm = pl.BlockSpec(memory_space=pl.ANY)
    quarter = jax.ShapeDtypeStruct((256, depth), bf16)
    outs = pl.pallas_call(
        ffn_kernel,
        grid=(4,),
        in_specs=[hbm] * 13,
        out_specs=(rowwise(FF_PAD), rowwise(2 * FF_PAD)) + (hbm,) * 8,
        out_shape=(
            jax.ShapeDtypeStruct((1024, FF_PAD), bf16),
            jax.ShapeDtypeStruct((1024, 2 * FF_PAD), bf16),
        )
        + (quarter,) * 8,
        scratch_shapes=[pltpu.VMEM((2, 256, depth), bf16)] * 4
        + [
            pltpu.VMEM((depth, 3 * FF_PAD), bf16),
            pltpu.SemaphoreType.DMA((3,)),
            pltpu.SemaphoreType.DMA((2, 3)),
            pltpu.SemaphoreType.DMA((2, 2)),
        ],
        cost_estimate=pl.CostEstimate(
            flops=12 * 1024 * depth * FF_PAD,
            bytes_accessed=35 * 2**20,
            transcendentals=1024 * FF_PAD,
        ),
        compiler_params=BIG,
        name="ffn",
    )(*hns, *cots, w)
    return outs[0], outs[1], outs[2:6], outs[6:10]


def ffn_grad_kernel(*refs):
    hn = jnp.concatenate([r[...] for r in refs[:8]], 0)
    cot = jnp.concatenate([r[...] for r in refs[8:12]], 0)
    dgu_ref, hid_ref, out_ref = refs[12:]
    out_ref[:, : 2 * FF_PAD] = mm(hn, dgu_ref[...], TN).astype(bf16)
    out_ref[:, 2 * FF_PAD :] = mm(cot, hid_ref[...], TN).astype(bf16)


def ffn_grad(hns, cots, dgu, hid):
    depth = hns[0].shape[1]
    block = 256
    return pl.pallas_call(
        ffn_grad_kernel,
        grid=(depth // block,),
        in_specs=[pl.BlockSpec((128, block), lambda i: (0, i))] * 8
        + [pl.BlockSpec((256, block), lambda i: (0, i))] * 4
        + [VMEM] * 2,
        out_specs=pl.BlockSpec((block, 3 * FF_PAD), lambda i: (i, 0)),
        out_shape=jax.ShapeDtypeStruct((depth, 3 * FF_PAD + OUT), bf16),
        cost_estimate=pl.CostEstimate(
            flops=6 * 1024 * depth * FF_PAD, bytes_accessed=24 * 2**20, transcendentals=0
        ),
        compiler_params=BIG,
        name="ffn_grad",
    )(*hns, *cots, dgu, hid)


def dh_kernel(*refs):
    pieces, w_ref, ob_ref, _ = refs[:8], refs[8], refs[9], refs[10]
    do_ref, grads_hbm, part, sem = refs[11:]
    for k in range(4):
        cols = slice(k * 512, k * 512 + 512)
        dh = jnp.concatenate([r[:, cols] for r in pieces], 0)
        part[cols, :] = mm(dh, ob_ref[...], TN).astype(bf16)
    copy = pltpu.make_async_copy(part, grads_hbm.at[:, 3 * FF_PAD :], sem)
    copy.start()
    for k in range(4):
        dh = jnp.concatenate([pieces[2 * k][...], pieces[2 * k + 1][...]], 0)
        do_ref[k * 256 : k * 256 + 256, :] = mm(dh, w_ref[...], NN).astype(bf16)
    copy.wait()


def dh_project(pieces, w, ob, grads):
    depth = w.shape[0]
    hbm = pl.BlockSpec(memory_space=pl.ANY)
    return pl.pallas_call(
        dh_kernel,
        in_specs=[VMEM] * 10 + [hbm],
        out_specs=(VMEM, hbm),
        out_shape=(
            jax.ShapeDtypeStruct((1024, OUT), bf16),
            jax.ShapeDtypeStruct(grads.shape, bf16),
        ),
        scratch_shapes=[pltpu.VMEM((depth, OUT), bf16), pltpu.SemaphoreType.DMA(())],
        input_output_aliases={10: 1},
        cost_estimate=pl.CostEstimate(
            flops=4 * 1024 * depth * OUT, bytes_accessed=8 * 2**20, transcendentals=0
        ),
        compiler_params=BIG,
        name="dh_project",
    )(*pieces, w, ob, grads)


def qkv_grad_kernel(x0, x1, x2, x3, near_ref, far_ref, out_ref):
    xh = jnp.concatenate([r[...] for r in (x0, x1, x2, x3)], 0)
    out_ref[...] = mm(xh, jnp.concatenate([near_ref[...], far_ref[...]], 0), TN).astype(bf16)


def qkv_grad(xs, dqkvs):
    depth = xs[0].shape[1]
    block = 512
    return pl.pallas_call(
        qkv_grad_kernel,
        grid=(depth // block,),
        in_specs=[pl.BlockSpec((256, block), lambda i: (0, i))] * 4 + [VMEM] * 2,
        out_specs=pl.BlockSpec((block, 384), lambda i: (i, 0)),
        out_shape=jax.ShapeDtypeStruct((depth, 384), bf16),
        cost_estimate=pl.CostEstimate(
            flops=2 * 1024 * depth * 384, bytes_accessed=8 * 2**20, transcendentals=0
        ),
        compiler_params=BIG,
        name="qkv_grad",
    )(*xs, *dqkvs)


def dqkv_kernel(at_ref, dq_ref, *refs):
    parts, (w_ref, cos_ref, sin_ref, dqkv_ref, keep_ref, send_ref) = refs[:8], refs[8:]
    cosine, sine = cos_ref[...], -sin_ref[...]
    core = at_ref[2]
    for part in range(2):
        cols = slice(part * 128, part * 128 + 128)
        dqkv_ref[:, cols] = turn(dq_ref[:, cols], cosine, sine).astype(bf16)
    dkv = sum(part[...].astype(f32) for part in parts)
    lane = lax.broadcasted_iota(jnp.int32, dkv.shape, 1)
    is_key = lane < HD
    turned = jnp.where(is_key, turn(dkv, cosine, sine), dkv)
    mine = jnp.where(is_key, 1 - core, core) > 0
    dqkv_ref[:, 256:] = jnp.where(mine, turned, 0.0).astype(bf16)
    dn = mm(dqkv_ref[...], w_ref[...], NT).astype(bf16)

    @pl.when(pl.program_id(0) == 0)
    def _():
        send_ref[...] = dn

    @pl.when(pl.program_id(0) == 1)
    def _():
        keep_ref[...] = dn


def dqkv_project(half, at, dq, dkvs, others, w, cosine, sine):
    depth = w.shape[0]
    turned = pl.BlockSpec((256, 128), lambda i: (2 * half + i, 0))
    rowwise = lambda width: pl.BlockSpec((256, width), lambda i: (2 * half + 1 - i, 0))
    whole = pl.BlockSpec((256, depth), lambda i: (0, 0))
    return pl.pallas_call(
        dqkv_kernel,
        grid=(2,),
        in_specs=[SMEM, rowwise(256)]
        + [rowwise(128)] * 4
        + [turned] * 4
        + [VMEM, rowwise(128), rowwise(128)],
        out_specs=(pl.BlockSpec((256, 384), lambda i: (1 - i, 0)), whole, whole),
        out_shape=(
            jax.ShapeDtypeStruct((512, 384), bf16),
            jax.ShapeDtypeStruct((256, depth), bf16),
            jax.ShapeDtypeStruct((256, depth), bf16),
        ),
        cost_estimate=pl.CostEstimate(
            flops=2 * 512 * depth * 384, bytes_accessed=6 * 2**20, transcendentals=0
        ),
        compiler_params=BIG,
        name="dqkv_project",
    )(at, dq, *dkvs, *others, w, cosine, sine)


def swap(value, axes):
    count = 2 ** len(axes)
    return lax.ppermute(value, axes, [(i, count - 1 - i) for i in range(count)])


def shifted(value, steps):
    first, last = max(0, -steps), min(4, 4 - steps)
    return lax.ppermute(value, "z", [(i, i + steps) for i in range(first, last)])


def gather_group(own):
    by_l, by_c = swap(own, ("yl",)), swap(own, ("c",))
    by_d, by_h = swap(own, ("yh", "yl")), swap(own, ("yh",))
    near = [own, by_l, by_c, swap(by_l, ("c",))]
    return near + [by_h, by_d, swap(by_h, ("c",)), swap(by_d, ("c",))]


def sum_cores(keep, send):
    return keep.astype(f32) + swap(send, ("c",)).astype(f32)


def from_chips(near, far):
    far = far.astype(bf16)
    by_h = swap(far[:128], ("yh",))
    by_d = swap(far[128:], ("yh", "yl"))
    by_l = swap(near[128:].astype(bf16), ("yl",))
    return by_l, by_d, by_h


def sum_chips(near, received):
    by_l, by_d, by_h = received
    return near[:128] + by_l.astype(f32) + by_d.astype(f32) + by_h.astype(f32)


def pick(parts, index):
    return lax.dynamic_index_in_dim(parts, index, 0, False)


def trade_cores(parts, core):
    parts = parts.reshape(2, 2, *parts.shape[1:]).swapaxes(0, 1)
    mine, got = pick(parts, core), swap(pick(parts, 1 - core), ("c",))
    return jnp.where(core == 0, jnp.stack([mine, got], 1), jnp.stack([got, mine], 1))


def trade_chips(parts, yh):
    mine, got = pick(parts, yh), swap(pick(parts, 1 - yh), ("yh",))
    parts = jnp.where(yh == 0, jnp.stack([mine, got]), jnp.stack([got, mine]))
    return parts.reshape(4, *parts.shape[2:])


def both_halves(own, other, yl):
    return jnp.where(yl == 0, jnp.concatenate([own, other], 0), jnp.concatenate([other, own], 0))


def on_device(
    tokens, w_query, w_key, w_value, w_output, w_gate, w_up, w_down, norm_attn, norm_ffn, cotangent
):
    together = lax.optimization_barrier
    z, yh = lax.axis_index("z"), lax.axis_index("yh")
    core, yl = lax.axis_index("c"), lax.axis_index("yl")
    gain_one = norm_attn.astype(f32)[:, None]
    gain_two = norm_ffn.astype(f32)[:, None]
    flip = (yh * 4 + core * 2 + yl) * 128
    at = jnp.stack([z, flip, core]).astype(jnp.int32)

    both = lambda a: jnp.where(yl == 0, a, jnp.concatenate([a[128:], a[:128]], 0))
    inputs = both(tokens[0]).astype(f32)
    inverse_one = lax.rsqrt(jnp.mean(inputs * inputs, axis=-1, keepdims=True) + epsilon)
    xh = (inputs * inverse_one).astype(bf16)
    inputs, inverse_one = inputs[:128], inverse_one[:128]
    cot_here = both(cotangent[0])

    def by_model(w):
        return w.reshape(32, 4, -1).transpose(1, 0, 2)

    def by_head(w):
        return jnp.repeat(w.reshape(32, 2, HD).transpose(1, 0, 2), 2, axis=0)

    scaled = lambda w, gain: (w.astype(f32) * gain).astype(bf16)

    def padded(w):
        return jnp.pad(by_model(w), ((0, 0), (0, 0), (0, FF_PAD - FF_BLOCK)))

    qkv_rows = jnp.concatenate(
        [
            by_model(scaled(w_query, gain_one)),
            by_head(scaled(w_key, gain_one)),
            by_head(scaled(w_value, gain_one)),
        ],
        -1,
    )
    ffn_rows = jnp.concatenate(
        [padded(scaled(w_gate, gain_two)), padded(scaled(w_up, gain_two)), padded(w_down.T)], -1
    )

    def spread(rows):
        copies = jnp.broadcast_to(rows[None], (16,) + rows.shape).reshape(64, 32, -1)
        return lax.all_to_all(copies, ALL, 0, 0).reshape(2048, -1)

    w_qkv = spread(qkv_rows)
    positions = (z * 1024 + (jnp.arange(1024, dtype=jnp.int32) ^ flip)).astype(f32)
    freqs = rope_base ** (-2.0 * jnp.arange(HD // 2, dtype=f32) / HD)
    angles = positions[:, None] * freqs[None, :]
    cosine, sine = jnp.cos(angles), jnp.sin(angles)
    cosine = jnp.concatenate([cosine] * 4, -1)
    sine = jnp.concatenate([-sine, sine, -sine, sine], -1)

    xh_c, xh_h = swap(xh, ("c",)), swap(xh, ("yh",))
    ffn_rows = trade_chips(trade_cores(ffn_rows, core), yh).reshape(128, -1)
    out_rows = by_model(w_output.T)
    xh_h, w_qkv, cosine, sine, cot_here, ffn_rows, out_rows = together(
        (xh_h, w_qkv, cosine, sine, cot_here, ffn_rows, out_rows)
    )
    xhs = [xh, xh_c, xh_h, swap(xh_h, ("c",))]

    q, kv = qkv_project(xhs, w_qkv, cosine, sine)
    cot_c, cot_h = swap(cot_here, ("c",)), swap(cot_here, ("yh",))
    kvs = [kv] + [shifted(kv, by) for by in (1, 2, 3)]
    kvs, cot_h, ffn_rows, out_rows = together((kvs, cot_h, ffn_rows, out_rows))
    w_ffn = lax.all_gather(ffn_rows, ("x", "z"), axis=0, tiled=True)
    w_out = spread(out_rows)
    cots = [cot_here, cot_c, cot_h, swap(cot_h, ("c",))]
    ob, o_t, lse = attn_fwd(at, q, kvs)
    branch = branch_project(ob, w_out)
    near, far = sum_cores(*branch[:2]), sum_cores(*branch[2:])
    middle = inputs + sum_chips(near, from_chips(near, far))
    inverse_two = lax.rsqrt(jnp.mean(middle * middle, axis=-1, keepdims=True) + epsilon)
    hns = gather_group((middle * inverse_two).astype(bf16))

    hid, dgu, ys, dns = ffn(hns, cots, w_ffn)
    near, far = sum_cores(*dns[:2]), sum_cores(*dns[2:])
    received = from_chips(near, far)
    grads = ffn_grad(hns, cots, dgu, hid)
    received, grads = together((received, grads))
    dn2 = sum_chips(near, received)
    dh = (
        cots[0][:128].astype(f32)
        + inverse_two * dn2
        - middle * inverse_two**3 * jnp.mean(dn2 * middle, axis=-1, keepdims=True)
    )
    dh_low, ys = together((dh.astype(bf16), ys))
    dhs = gather_group(dh_low)
    y_near, y_far = sum_cores(*ys[:2]), sum_cores(*ys[2:])
    dhs, y_near, y_far = together((dhs, y_near, y_far))

    do, grads = dh_project(dhs, w_out, ob, grads)
    grads = lax.psum_scatter(grads, ("x", "z"), scatter_dimension=0, tiled=True)
    do, y_near, y_far = together((do, y_near, y_far))
    received = from_chips(y_near, y_far)
    dq, *dkvs = attn_bwd(at, q, kvs, do, o_t, lse)
    received, dkvs = together((received, dkvs))
    block_out = (middle + sum_chips(y_near, received)).astype(bf16)
    block_out, dkvs = together((block_out, dkvs))
    block_other = swap(block_out, ("yl",))
    dkvs = dkvs[:1] + [shifted(dkvs[by], -by) for by in (1, 2, 3)]
    dkvs, block_other = together((dkvs, block_other))
    block_out = both_halves(block_out, block_other, yl)
    others = [swap(part, ("c",)) for part in dkvs]
    dqkv_far, dn_far, dn_far_c = dqkv_project(1, at, dq, dkvs, others, w_qkv, cosine, sine)
    dqkv_near, dn_near, dn_near_c = dqkv_project(0, at, dq, dkvs, others, w_qkv, cosine, sine)
    near, far = sum_cores(dn_near, dn_near_c), sum_cores(dn_far, dn_far_c)
    near, far, dqkv_near, dqkv_far = together((near, far, dqkv_near, dqkv_far))
    received = from_chips(near, far)
    dn1 = sum_chips(near, received)
    grad_qkv = qkv_grad(xhs, (dqkv_near, dqkv_far))
    grad_qkv = lax.all_to_all(grad_qkv.reshape(16, 128, 384), ("x", "z"), 0, 0)
    grads = trade_cores(grads.reshape(4, 32, 3 * FF_PAD + OUT), core)
    input_grad = (
        dh
        + inverse_one * dn1
        - inputs * inverse_one**3 * jnp.mean(dn1 * inputs, axis=-1, keepdims=True)
    )
    input_grad, grad_qkv, grads = together((input_grad, grad_qkv, grads))
    other = swap(input_grad.astype(bf16), ("yl",)).astype(f32)
    input_grad = both_halves(input_grad, other, yl)
    grads = trade_chips(grads, yh).astype(f32)
    grad_qkv = jnp.sum(grad_qkv.astype(f32), 0).astype(bf16).reshape(4, 32, 384)
    grad_qkv = trade_chips(trade_cores(grad_qkv, core), yh).astype(f32)

    def joined(parts):
        return parts.transpose(1, 0, 2).reshape(32, -1)

    ffn_part = lambda k: joined(grads[:, :, k * FF_PAD : k * FF_PAD + FF_BLOCK])
    grad_gate, grad_up, grad_down = ffn_part(0), ffn_part(1), ffn_part(2).T
    grad_query = joined(grad_qkv[:, :, :256])
    by_core = grad_qkv[:, :, 256:].reshape(2, 2, 32, 2 * HD).sum(1)
    grad_key, grad_value = joined(by_core[:, :, :HD]), joined(by_core[:, :, HD:])

    def gain_grad(*pairs):
        return sum(jnp.sum(w.astype(f32) * grad, 1) for w, grad in pairs)

    gains = jnp.stack(
        [
            gain_grad((w_query, grad_query), (w_key, grad_key), (w_value, grad_value)),
            gain_grad((w_gate, grad_gate), (w_up, grad_up)),
        ]
    )
    gains = gains + swap(gains, ("yl",))
    return (
        block_out[None],
        input_grad[None],
        grad_query * gain_one,
        grad_key * gain_one,
        grad_value * gain_one,
        joined(grads[:, :, 3 * FF_PAD :]).T,
        grad_gate * gain_two,
        grad_up * gain_two,
        grad_down,
        gains[0],
        gains[1],
    )


def solution(mesh):
    mesh = Mesh(mesh.devices.reshape(4, 4, 2, 2, 2), ("x", "z", "yh", "c", "yl"))
    ctx = ("z", "yh", "c")
    rows, cols = P(ALL, "yl"), P("yl", ALL)
    seq = P("x", ctx, None)
    vec = P(ALL)
    in_specs = (seq, rows, rows, rows, cols, rows, rows, cols, vec, vec, seq)
    out_specs = (seq, seq, rows, rows, rows, cols, rows, rows, cols, vec, vec)
    return jax.shard_map(
        on_device, mesh=mesh, in_specs=in_specs, out_specs=out_specs, check_vma=False
    )
```

```python
import functools

import jax
import jax.numpy as jnp
from jax import lax
from jax.experimental import pallas as pl
from jax.experimental.pallas import tpu as pltpu
from jax.sharding import Mesh, PartitionSpec as P

HD = 64
HEADS = 4
FF_BLOCK = 704
FF_PAD = 768
OUT = 256
LOG2E = 1.4426950408889634
epsilon = 1e-05
rope_base = 10000.0
masked_low = -1e30
f32 = jnp.float32
bf16 = jnp.bfloat16

ALL = ("x", "z", "yh", "c")
MODEL = ("yh", "c")

NN = (((1,), (0,)), ((), ()))
NT = (((1,), (1,)), ((), ()))
TN = (((0,), (0,)), ((), ()))

VMEM = pl.BlockSpec(memory_space=pltpu.VMEM)
SMEM = pl.BlockSpec(memory_space=pltpu.SMEM)
BIG = pltpu.CompilerParams(vmem_limit_bytes=56 * 2**20)


def mm(a, b, dims):
    return lax.dot_general(a, b, dims, preferred_element_type=f32)


def turn(u, cosine, sine_signed):
    width = u.shape[-1]
    lane = lax.broadcasted_iota(jnp.int32, u.shape, 1)
    turned = jnp.where(
        lane % HD < HD // 2, pltpu.roll(u, width - HD // 2, 1), pltpu.roll(u, HD // 2, 1)
    )
    return u * cosine + turned * sine_signed


def order_kernel(at_ref, x_ref, cot_ref, xh_ref, inv_ref, cot_out):
    for half in range(2):
        first = pl.multiple_of((at_ref[3] ^ half) * 128, 128)
        rows = slice(half * 128, half * 128 + 128)
        x = x_ref[pl.ds(first, 128), :].astype(f32)
        inverse = lax.rsqrt(jnp.mean(x * x, axis=-1, keepdims=True) + epsilon)
        xh_ref[rows, :] = (x * inverse).astype(bf16)
        cot_out[rows, :] = cot_ref[pl.ds(first, 128), :]
        if half == 0:
            inv_ref[...] = inverse


def order(at, x, cot):
    low = jax.ShapeDtypeStruct(x.shape, bf16)
    return pl.pallas_call(
        order_kernel,
        in_specs=[SMEM, VMEM, VMEM],
        out_specs=(VMEM,) * 3,
        out_shape=(low, jax.ShapeDtypeStruct((128, 1), f32), low),
        cost_estimate=pl.CostEstimate(flops=2**20, bytes_accessed=4 * 2**20, transcendentals=0),
        compiler_params=BIG,
        name="order",
    )(at, x, cot)


def prepare_kernel(wq, wk, wv, wo_t, wg, wu, wd_t, g_one, g_two, qkv_ref, rest_ref, out_ref):
    g_one, g_two = g_one[...], g_two[...]
    scaled = lambda ref, gain: (ref[...].astype(f32) * gain).astype(bf16)
    query, key, value = scaled(wq, g_one), scaled(wk, g_one), scaled(wv, g_one)
    for part in range(4):
        head = slice(part // 2 * HD, part // 2 * HD + HD)
        rows = jnp.concatenate(
            [query[:, part * 256 : part * 256 + 256], key[:, head], value[:, head]], 1
        )
        for copy in range(16):
            qkv_ref[copy * 4 + part] = rows
    lane = lax.broadcasted_iota(jnp.int32, (32, FF_PAD), 1)
    for k, (ref, gain) in enumerate(((wg, g_two), (wu, g_two), (wd_t, None))):
        w = ref[...].astype(f32)
        w = w if gain is None else w * gain
        for part in range(4):
            shift = (w.shape[1] - part * FF_BLOCK) % w.shape[1]
            block = pltpu.roll(w, shift, 1)[:, :FF_PAD] if shift else w[:, :FF_PAD]
            block = jnp.where(lane < FF_BLOCK, block, 0.0)
            rest_ref[part, :, k * FF_PAD : (k + 1) * FF_PAD] = block.astype(bf16)
    for part in range(4):
        out_ref[part] = wo_t[:, part * OUT : part * OUT + OUT]


def prepare(*args):
    return pl.pallas_call(
        prepare_kernel,
        in_specs=[VMEM] * 9,
        out_specs=(VMEM,) * 3,
        out_shape=(
            jax.ShapeDtypeStruct((64, 32, 384), bf16),
            jax.ShapeDtypeStruct((4, 32, 3 * FF_PAD), bf16),
            jax.ShapeDtypeStruct((4, 32, OUT), bf16),
        ),
        cost_estimate=pl.CostEstimate(flops=2**20, bytes_accessed=3 * 2**20, transcendentals=0),
        compiler_params=BIG,
        name="prepare",
    )(*args)


def finish_ffn_kernel(parts, wg, wu, g_two, gate_ref, up_ref, down_ref, out_ref, gain_ref):
    def joined(first):
        total = jnp.zeros(gate_ref.shape, f32)
        for part in range(4):
            block = parts[part, :, first : first + FF_PAD].astype(f32)
            block = jnp.concatenate(
                [block, jnp.zeros((32, total.shape[1] - FF_PAD), f32)], 1
            )
            total = total + (pltpu.roll(block, part * FF_BLOCK, 1) if part else block)
        return total

    gate, up = joined(0), joined(FF_PAD)
    gain_ref[...] = jnp.sum(
        wg[...].astype(f32) * gate + wu[...].astype(f32) * up, axis=1, keepdims=True
    )
    gate_ref[...] = gate * g_two[...]
    up_ref[...] = up * g_two[...]
    down_ref[...] = joined(2 * FF_PAD)
    for part in range(4):
        out_ref[:, part * OUT : part * OUT + OUT] = parts[part, :, 3 * FF_PAD :].astype(f32)


def finish_ffn(parts, wg, wu, g_two):
    wide = jax.ShapeDtypeStruct(wg.shape, f32)
    return pl.pallas_call(
        finish_ffn_kernel,
        in_specs=[VMEM] * 4,
        out_specs=(VMEM,) * 5,
        out_shape=(
            wide,
            wide,
            wide,
            jax.ShapeDtypeStruct((32, 4 * OUT), f32),
            jax.ShapeDtypeStruct((32, 1), f32),
        ),
        cost_estimate=pl.CostEstimate(flops=2**20, bytes_accessed=3 * 2**20, transcendentals=0),
        compiler_params=BIG,
        name="finish_ffn",
    )(parts, wg, wu, g_two)


def finish_qkv_kernel(parts, wq, wk, wv, g_one, q_ref, k_ref, v_ref, gain_ref):
    grads = [parts[part].astype(f32) for part in range(4)]
    query = jnp.concatenate([grad[:, :256] for grad in grads], 1)
    both = [grads[0] + grads[1], grads[2] + grads[3]]
    key = jnp.concatenate([grad[:, 256:320] for grad in both], 1)
    value = jnp.concatenate([grad[:, 320:] for grad in both], 1)
    total = jnp.sum(wq[...].astype(f32) * query, axis=1, keepdims=True)
    total = total + jnp.sum(
        wk[...].astype(f32) * key + wv[...].astype(f32) * value, axis=1, keepdims=True
    )
    gain_ref[...] = total
    q_ref[...] = query * g_one[...]
    k_ref[...] = key * g_one[...]
    v_ref[...] = value * g_one[...]


def finish_qkv(parts, wq, wk, wv, g_one):
    shapes = [w.shape for w in (wq, wk, wv)] + [(32, 1)]
    return pl.pallas_call(
        finish_qkv_kernel,
        in_specs=[VMEM] * 5,
        out_specs=(VMEM,) * 4,
        out_shape=tuple(jax.ShapeDtypeStruct(shape, f32) for shape in shapes),
        cost_estimate=pl.CostEstimate(flops=2**18, bytes_accessed=2**19, transcendentals=0),
        compiler_params=BIG,
        name="finish_qkv",
    )(parts, wq, wk, wv, g_one)


def qkv_kernel(*refs):
    w_ref, cos_ref, sin_ref, q_ref, kv_ref = refs[4:]
    scale = HD**-0.5 * LOG2E
    for part, x_ref in enumerate(refs[:4]):
        rows = slice(part * 256, part * 256 + 256)
        lin = mm(x_ref[...], w_ref[...], NN)
        cosine, sine = cos_ref[rows], sin_ref[rows]
        for half in range(2):
            cols = slice(half * 128, half * 128 + 128)
            q_ref[rows, cols] = (turn(lin[:, cols], cosine, sine) * scale).astype(bf16)
        kv = lin[:, 256:384]
        lane = lax.broadcasted_iota(jnp.int32, kv.shape, 1)
        kv_ref[rows, :] = jnp.where(lane < HD, turn(kv, cosine, sine), kv).astype(bf16)


def qkv_project(xs, w, cosine, sine):
    return pl.pallas_call(
        qkv_kernel,
        in_specs=[VMEM] * 7,
        out_specs=(VMEM, VMEM),
        out_shape=(
            jax.ShapeDtypeStruct((1024, 256), bf16),
            jax.ShapeDtypeStruct((1024, 128), bf16),
        ),
        cost_estimate=pl.CostEstimate(
            flops=2 * 1024 * 2048 * 384, bytes_accessed=6 * 2**20, transcendentals=0
        ),
        compiler_params=BIG,
        name="qkv_project",
    )(*xs, w, cosine, sine)


def attn_fwd_kernel(
    at_ref, q_ref, kv0, kv1, kv2, kv3, o_ref, ot_ref, lse_ref, q_pad, keys_all, values_t, *, bq, bk
):
    rows = q_ref.shape[0]
    depth, flip = at_ref[0], at_ref[1]
    for h in range(HEADS):
        q_pad[h, :, :HD] = q_ref[:, h * HD : (h + 1) * HD]
        q_pad[h, :, HD:] = jnp.zeros((rows, HD), bf16)
    for b, kv_ref in enumerate((kv0, kv1, kv2, kv3)):

        @pl.when(depth >= b)
        def _():
            keys_all[b] = kv_ref[...]
            values_t[b, :HD] = kv_ref[...].T[HD:]
            values_t[b, HD:] = jnp.ones((16, rows), bf16)

    pair = flip // bq

    def q_step(i, _):
        cols = pl.ds(pl.multiple_of(i * bq, bq), bq)
        queries = [q_pad[h, cols, :] for h in range(HEADS)]

        def block(b, offset, state, masked, count):
            keys = keys_all[b, pl.ds(offset, count), :]
            values = values_t[b, :, pl.ds(offset, count)]
            scores = [mm(keys, queries[h], NT) for h in range(HEADS)]
            if masked:
                k_pos = (lax.broadcasted_iota(jnp.int32, (count, bq), 0) + offset) ^ flip
                q_pos = (lax.broadcasted_iota(jnp.int32, (count, bq), 1) + i * bq) ^ flip
                visible = k_pos <= q_pos
                scores = [jnp.where(visible, s, masked_low) for s in scores]
            out = []
            for h in range(HEADS):
                top, acc = state[h]
                s = scores[h]
                new_top = jnp.maximum(top, jnp.max(s, axis=0, keepdims=True))
                p = jnp.exp2(s - new_top).astype(bf16)
                acc = acc * jnp.exp2(top - new_top) + mm(values, p, NN)
                out.append((new_top, acc))
            return tuple(out)

        state = tuple(
            (jnp.full((1, bq), masked_low, f32), jnp.zeros((HD + 16, bq), f32))
            for _ in range(HEADS)
        )
        state = block(0, pl.multiple_of(i * bq, bq), state, True, bq)
        state = lax.fori_loop(
            0,
            i ^ pair,
            lambda j, st: block(0, pl.multiple_of((j ^ pair) * bq, bq), st, False, bq),
            state,
        )
        per = rows // bk
        state = lax.fori_loop(
            0,
            depth * per,
            lambda j, st: block(
                1 + j // per, pl.multiple_of((j % per) * bk, bk), st, False, bk
            ),
            state,
        )
        outs = []
        for h in range(HEADS):
            top, acc = state[h]
            total = acc[HD : HD + 1]
            lse_ref[pl.ds(h, 1), cols] = top + jnp.log2(total)
            outs.append(acc[:HD] * (1.0 / total))
        o_t = jnp.concatenate(outs, 0)
        ot_ref[:, cols] = o_t
        o_ref[cols, :] = o_t.T.astype(bf16)
        return 0

    lax.fori_loop(0, rows // bq, q_step, 0)


def attn_fwd(at, q, kvs):
    rows = q.shape[0]
    return pl.pallas_call(
        functools.partial(attn_fwd_kernel, bq=512, bk=512),
        out_shape=(
            jax.ShapeDtypeStruct((rows, HEADS * HD), bf16),
            jax.ShapeDtypeStruct((HEADS * HD, rows), f32),
            jax.ShapeDtypeStruct((HEADS, rows), f32),
        ),
        in_specs=[SMEM] + [VMEM] * 5,
        out_specs=(VMEM,) * 3,
        scratch_shapes=[
            pltpu.VMEM((HEADS, rows, 128), bf16),
            pltpu.VMEM((4, rows, 128), bf16),
            pltpu.VMEM((4, HD + 16, rows), bf16),
        ],
        cost_estimate=pl.CostEstimate(
            flops=25 * 10**9, bytes_accessed=6 * 2**20, transcendentals=12 * 10**6
        ),
        compiler_params=BIG,
        name="attn_fwd",
    )(at, q, *kvs)


def branch_kernel(at_ref, o_ref, w0, w1, w2, w3, a0, a1, a2, a3, w_ref):
    @pl.when(pl.program_id(0) == 0)
    def _():
        for i, piece in enumerate((w0, w1, w2, w3)):
            for j in range(4):
                first = ((at_ref[4] ^ j) * 4 + (at_ref[0] ^ i)) * 128
                w_ref[pl.ds(pl.multiple_of(first, 128), 128), :] = piece[j * 128 : j * 128 + 128]

    for k, out_ref in enumerate((a0, a1, a2, a3)):

        @pl.when(pl.program_id(0) == k)
        def _():
            out_ref[...] = mm(o_ref[...], w_ref[...], NT).astype(bf16)


def branch_project(at, o, ws):
    depth = 4 * ws[0].shape[0]
    part = jax.ShapeDtypeStruct((256, depth), bf16)
    outs = pl.pallas_call(
        branch_kernel,
        grid=(4,),
        in_specs=[SMEM, pl.BlockSpec((256, OUT), lambda i: (i, 0))] + [VMEM] * 4,
        out_specs=(pl.BlockSpec((256, depth), lambda i: (0, 0)),) * 4 + (VMEM,),
        out_shape=(part,) * 4 + (jax.ShapeDtypeStruct((depth, OUT), bf16),),
        cost_estimate=pl.CostEstimate(
            flops=2 * 1024 * depth * OUT, bytes_accessed=6 * 2**20, transcendentals=0
        ),
        compiler_params=BIG,
        name="branch_project",
    )(at, o, *ws)
    return outs[:4], outs[4]


def attn_bwd_kernel(
    at_ref, q_ref, kv0, kv1, kv2, kv3, do_ref, ot_ref, lse_ref,
    dq_ref, dkv0, dkv1, dkv2, dkv3,
    q_pad, do_pad, keys_all, keys_t, dkv_all, dqt, delta, *, bq, bk,
):
    rows = q_ref.shape[0]
    depth, flip = at_ref[0], at_ref[1]
    nothing = jnp.zeros((rows, HD), bf16)
    for h in range(HEADS):
        cols = slice(h * HD, (h + 1) * HD)
        q_pad[h, :, :HD] = q_ref[:, cols]
        q_pad[h, :, HD:] = nothing
        do_pad[h, :, :HD] = nothing
        do_pad[h, :, HD:] = do_ref[:, cols]
    do_t = do_ref[...].astype(f32).T
    for h in range(HEADS):
        cols = slice(h * HD, (h + 1) * HD)
        delta[pl.ds(h, 1), :] = jnp.sum(do_t[cols] * ot_ref[cols, :], axis=0, keepdims=True)
    for b, kv_ref in enumerate((kv0, kv1, kv2, kv3)):

        @pl.when(depth >= b)
        def _():
            keys_all[b] = kv_ref[...]
            keys_t[b] = kv_ref[...].T[:HD]

    dqt[...] = jnp.zeros_like(dqt)
    pair = flip // bq

    def tile(b, offset, i, masked, count, dkv):
        keys = keys_all[b, pl.ds(offset, count), :]
        turned = keys_t[b, :, pl.ds(offset, count)]
        at = pl.ds(pl.multiple_of(i * bq, bq), bq)
        if masked:
            k_pos = (lax.broadcasted_iota(jnp.int32, (count, bq), 0) + offset) ^ flip
            q_pos = (lax.broadcasted_iota(jnp.int32, (count, bq), 1) + i * bq) ^ flip
            visible = k_pos <= q_pos
        for h in range(HEADS):
            query, grad = q_pad[h, at, :], do_pad[h, at, :]
            p = jnp.exp2(mm(keys, query, NT) - lse_ref[pl.ds(h, 1), at])
            if masked:
                p = jnp.where(visible, p, 0.0)
            dp = mm(keys, grad, NT)
            ds = (p * (dp - delta[pl.ds(h, 1), at])).astype(bf16)
            dkv = dkv + mm(p.astype(bf16), grad, NN) + mm(ds, query, NN)
            dqt[h * HD : (h + 1) * HD, at] += mm(turned, ds, NN)
        return dkv

    lane = lax.broadcasted_iota(jnp.int32, (1, 128), 1)
    out_scale = jnp.where(lane < HD, 1.0 / LOG2E, 1.0)
    per = rows // bk

    def far(j, _):
        b, offset = 1 + j // per, pl.multiple_of((j % per) * bk, bk)
        dkv = lax.fori_loop(
            0,
            rows // bq,
            lambda i, st: tile(b, offset, i, False, bk, st),
            jnp.zeros((bk, 128), f32),
        )
        dkv_all[b, pl.ds(offset, bk), :] = (dkv * out_scale).astype(bf16)
        return 0

    lax.fori_loop(0, depth * per, far, 0)

    def near(j, _):
        offset = pl.multiple_of(j * bq, bq)
        dkv = tile(0, offset, j, True, bq, jnp.zeros((bq, 128), f32))
        dkv = lax.fori_loop(
            (j ^ pair) + 1,
            rows // bq,
            lambda i, st: tile(0, offset, i ^ pair, False, bq, st),
            dkv,
        )
        dkv_all[0, pl.ds(offset, bq), :] = (dkv * out_scale).astype(bf16)
        return 0

    lax.fori_loop(0, rows // bq, near, 0)
    dq_ref[...] = dqt[...].T * HD**-0.5
    for b, out_ref in enumerate((dkv0, dkv1, dkv2, dkv3)):
        out_ref[...] = dkv_all[b]


def attn_bwd(at, q, kvs, do, ot, lse):
    rows = q.shape[0]
    block = jax.ShapeDtypeStruct(kvs[0].shape, bf16)
    return pl.pallas_call(
        functools.partial(attn_bwd_kernel, bq=512, bk=1024),
        out_shape=(jax.ShapeDtypeStruct((rows, HEADS * HD), f32), block, block, block, block),
        in_specs=[SMEM] + [VMEM] * 8,
        out_specs=(VMEM,) * 5,
        scratch_shapes=[
            pltpu.VMEM((HEADS, rows, 128), bf16),
            pltpu.VMEM((HEADS, rows, 128), bf16),
            pltpu.VMEM((4, rows, 128), bf16),
            pltpu.VMEM((4, HD, rows), bf16),
            pltpu.VMEM((4, rows, 128), bf16),
            pltpu.VMEM((HEADS * HD, rows), f32),
            pltpu.VMEM((HEADS, rows), f32),
        ],
        cost_estimate=pl.CostEstimate(
            flops=50 * 10**9, bytes_accessed=8 * 2**20, transcendentals=12 * 10**6
        ),
        compiler_params=BIG,
        name="attn_bwd",
    )(at, q, *kvs, do, ot, lse)


def dhid_kernel(*refs):
    w_ref, out_ref = refs[4:]
    for part, cot_ref in enumerate(refs[:4]):
        out_ref[part * 256 : part * 256 + 256, :] = mm(cot_ref[...], w_ref[...], NN)


def dhid_project(cots, w):
    depth = w.shape[0]
    return pl.pallas_call(
        dhid_kernel,
        grid=(1,),
        in_specs=[VMEM] * 4 + [pl.BlockSpec((depth, FF_PAD), lambda i: (0, 2))],
        out_specs=VMEM,
        out_shape=jax.ShapeDtypeStruct((1024, FF_PAD), f32),
        cost_estimate=pl.CostEstimate(
            flops=2 * 1024 * depth * FF_PAD, bytes_accessed=10 * 2**20, transcendentals=0
        ),
        compiler_params=BIG,
        name="dhid_project",
    )(*cots, w)


def ffn_kernel(*refs):
    hns, dhid_ref, w_hbm = refs[:8], refs[8], refs[9]
    hid_ref, dgu_ref = refs[10:12]
    dns = refs[12:16]
    hn_buf, dn_buf, w_ref, w_sems, in_sems, out_sems = refs[16:]
    step = pl.program_id(0)
    parts = [slice(k * FF_PAD, (k + 1) * FF_PAD) for k in range(2)]
    weights = [
        pltpu.make_async_copy(w_hbm.at[:, parts[k]], w_ref.at[:, parts[k]], w_sems.at[k])
        for k in range(2)
    ]

    def fetch(s):
        return [
            pltpu.make_async_copy(
                hns[4 * s + k], hn_buf.at[s, k * 128 : k * 128 + 128], in_sems.at[s, k]
            )
            for k in range(4)
        ]

    def flush(s):
        return [
            pltpu.make_async_copy(
                dn_buf.at[s, k * 256 : k * 256 + 256], dns[2 * s + k], out_sems.at[s, k]
            )
            for k in range(2)
        ]

    def at(s, action, copies):
        @pl.when(step == s)
        def _():
            for copy in copies:
                action(copy)

    start = lambda copy: copy.start()
    wait = lambda copy: copy.wait()
    at(0, start, fetch(0) + weights + fetch(1))
    for s in range(2):
        at(s, wait, fetch(s))
    at(0, wait, weights[:1])
    hn = hn_buf[step]
    gate = mm(hn, w_ref[:, parts[0]], NN)
    at(0, wait, weights[1:])
    up = mm(hn, w_ref[:, parts[1]], NN)
    dhid = dhid_ref[...]
    sg = 1.0 / (1.0 + jnp.exp(-gate))
    act = gate * sg
    hid_ref[...] = (act * up).astype(bf16)
    dgu_ref[:, parts[0]] = (dhid * up * sg * (1.0 + gate * (1.0 - sg))).astype(bf16)
    dgu_ref[:, parts[1]] = (dhid * act).astype(bf16)
    dn_buf[step] = mm(dgu_ref[...], w_ref[...], NT).astype(bf16)
    for s in range(2):
        at(s, start, flush(s))
    at(1, wait, flush(0) + flush(1))


def ffn(hns, dhid, w):
    depth = w.shape[0]
    rowwise = lambda width: pl.BlockSpec((512, width), lambda i: (i, 0))
    hbm = pl.BlockSpec(memory_space=pl.ANY)
    quarter = jax.ShapeDtypeStruct((256, depth), bf16)
    outs = pl.pallas_call(
        ffn_kernel,
        grid=(2,),
        in_specs=[hbm] * 8 + [rowwise(FF_PAD), hbm],
        out_specs=(rowwise(FF_PAD), rowwise(2 * FF_PAD)) + (hbm,) * 4,
        out_shape=(
            jax.ShapeDtypeStruct((1024, FF_PAD), bf16),
            jax.ShapeDtypeStruct((1024, 2 * FF_PAD), bf16),
        )
        + (quarter,) * 4,
        scratch_shapes=[
            pltpu.VMEM((2, 512, depth), bf16),
            pltpu.VMEM((2, 512, depth), bf16),
            pltpu.VMEM((depth, 2 * FF_PAD), bf16),
            pltpu.SemaphoreType.DMA((2,)),
            pltpu.SemaphoreType.DMA((2, 4)),
            pltpu.SemaphoreType.DMA((2, 2)),
        ],
        cost_estimate=pl.CostEstimate(
            flops=8 * 1024 * depth * FF_PAD,
            bytes_accessed=25 * 2**20,
            transcendentals=1024 * FF_PAD,
        ),
        compiler_params=BIG,
        name="ffn",
    )(*hns, dhid, w)
    return outs[0], outs[1], outs[2:]


def ffn_grad_kernel(*refs):
    hn = jnp.concatenate([r[...] for r in refs[:8]], 0)
    cot = jnp.concatenate([r[...] for r in refs[8:12]], 0)
    dgu_ref, hid_ref, w_ref, out_ref = refs[12:16]
    hid = hid_ref[...]
    out_ref[:, : 2 * FF_PAD] = mm(hn, dgu_ref[...], TN).astype(bf16)
    out_ref[:, 2 * FF_PAD :] = mm(cot, hid, TN).astype(bf16)
    for part, y_ref in enumerate(refs[16:]):
        y_ref[...] = mm(hid[part * 256 : part * 256 + 256], w_ref[...], NT).astype(bf16)


def ffn_grad(hns, cots, dgu, hid, w):
    depth = hns[0].shape[1]
    block = 256
    piece = lambda rows: pl.BlockSpec((rows, block), lambda i: (0, i))
    outs = pl.pallas_call(
        ffn_grad_kernel,
        grid=(depth // block,),
        in_specs=[piece(a.shape[0]) for a in hns + cots]
        + [VMEM] * 2
        + [pl.BlockSpec((block, FF_PAD), lambda i: (i, 2))],
        out_specs=(pl.BlockSpec((block, 3 * FF_PAD), lambda i: (i, 0)),) + (piece(256),) * 4,
        out_shape=(jax.ShapeDtypeStruct((depth, 3 * FF_PAD + OUT), bf16),)
        + (jax.ShapeDtypeStruct((256, depth), bf16),) * 4,
        cost_estimate=pl.CostEstimate(
            flops=8 * 1024 * depth * FF_PAD, bytes_accessed=30 * 2**20, transcendentals=0
        ),
        compiler_params=BIG,
        name="ffn_grad",
    )(*hns, *cots, dgu, hid, w)
    return outs[0], outs[1:]


def dh_kernel(*refs):
    pieces, w_ref, ob_ref, _ = refs[:8], refs[8], refs[9], refs[10]
    do_ref, grads_hbm, part, sem = refs[11:]
    for k in range(4):
        cols = slice(k * 512, k * 512 + 512)
        dh = jnp.concatenate([r[:, cols] for r in pieces], 0)
        part[cols, :] = mm(dh, ob_ref[...], TN).astype(bf16)
    copy = pltpu.make_async_copy(part, grads_hbm.at[:, 3 * FF_PAD :], sem)
    copy.start()
    for k in range(4):
        dh = jnp.concatenate([pieces[2 * k][...], pieces[2 * k + 1][...]], 0)
        do_ref[k * 256 : k * 256 + 256, :] = mm(dh, w_ref[...], NN).astype(bf16)
    copy.wait()


def dh_project(pieces, w, ob, grads):
    depth = w.shape[0]
    hbm = pl.BlockSpec(memory_space=pl.ANY)
    return pl.pallas_call(
        dh_kernel,
        in_specs=[VMEM] * 10 + [hbm],
        out_specs=(VMEM, hbm),
        out_shape=(
            jax.ShapeDtypeStruct((1024, OUT), bf16),
            jax.ShapeDtypeStruct(grads.shape, bf16),
        ),
        scratch_shapes=[pltpu.VMEM((depth, OUT), bf16), pltpu.SemaphoreType.DMA(())],
        input_output_aliases={10: 1},
        cost_estimate=pl.CostEstimate(
            flops=4 * 1024 * depth * OUT, bytes_accessed=8 * 2**20, transcendentals=0
        ),
        compiler_params=BIG,
        name="dh_project",
    )(*pieces, w, ob, grads)


def qkv_grad_kernel(*refs):
    xh = jnp.concatenate([r[...] for r in refs[:4]], 0)
    dqkv_ref, out_ref = refs[4:]
    out_ref[...] = mm(xh, dqkv_ref[...], TN).astype(bf16)


def qkv_grad(xs, dqkv):
    depth = xs[0].shape[1]
    block = 512
    return pl.pallas_call(
        qkv_grad_kernel,
        grid=(depth // block,),
        in_specs=[pl.BlockSpec((x.shape[0], block), lambda i: (0, i)) for x in xs] + [VMEM],
        out_specs=pl.BlockSpec((block, 384), lambda i: (i, 0)),
        out_shape=jax.ShapeDtypeStruct((depth, 384), bf16),
        cost_estimate=pl.CostEstimate(
            flops=2 * 1024 * depth * 384, bytes_accessed=8 * 2**20, transcendentals=0
        ),
        compiler_params=BIG,
        name="qkv_grad",
    )(*xs, dqkv)


def dqkv_kernel(at_ref, dq_ref, *refs):
    parts, (w_ref, cos_ref, sin_ref, dqkv_ref) = refs[:8], refs[8:12]
    far_send, near_send, far_keep, near_keep = refs[12:]
    cosine, sine = cos_ref[...], -sin_ref[...]
    core = at_ref[2]
    for part in range(2):
        cols = slice(part * 128, part * 128 + 128)
        dqkv_ref[:, cols] = turn(dq_ref[:, cols], cosine, sine).astype(bf16)
    dkv = sum(part[...].astype(f32) for part in parts)
    lane = lax.broadcasted_iota(jnp.int32, dkv.shape, 1)
    is_key = lane < HD
    turned = jnp.where(is_key, turn(dkv, cosine, sine), dkv)
    mine = jnp.where(is_key, 1 - core, core) > 0
    dqkv_ref[:, 256:] = jnp.where(mine, turned, 0.0).astype(bf16)
    dn = mm(dqkv_ref[...], w_ref[...], NT).astype(bf16)
    for step, out_ref in enumerate((far_send, near_send, far_keep, near_keep)):

        @pl.when(pl.program_id(0) == step)
        def _():
            out_ref[...] = dn


def dqkv_project(at, dq, dkvs, others, w, cosine, sine):
    depth = w.shape[0]
    own = lambda i: jnp.where(i < 2, 3 - 2 * i, 6 - 2 * i)
    rowwise = lambda width: pl.BlockSpec((256, width), lambda i: (own(i), 0))
    turned = pl.BlockSpec((256, 128), lambda i: (own(i) ^ 1, 0))
    whole = pl.BlockSpec((256, depth), lambda i: (0, 0))
    return pl.pallas_call(
        dqkv_kernel,
        grid=(4,),
        in_specs=[SMEM, rowwise(256)]
        + [rowwise(128)] * 4
        + [turned] * 4
        + [VMEM, rowwise(128), rowwise(128)],
        out_specs=(rowwise(384),) + (whole,) * 4,
        out_shape=(jax.ShapeDtypeStruct((1024, 384), bf16),)
        + (jax.ShapeDtypeStruct((256, depth), bf16),) * 4,
        cost_estimate=pl.CostEstimate(
            flops=2 * 1024 * depth * 384, bytes_accessed=10 * 2**20, transcendentals=0
        ),
        compiler_params=BIG,
        name="dqkv_project",
    )(at, dq, *dkvs, *others, w, cosine, sine)


def swap(value, axes):
    count = 2 ** len(axes)
    return lax.ppermute(value, axes, [(i, count - 1 - i) for i in range(count)])


def crossed(value, axis, mask):
    return lax.ppermute(value, axis, [(i, i ^ mask) for i in range(4)])


def shifted(value, steps):
    first, last = max(0, -steps), min(4, 4 - steps)
    return lax.ppermute(value, "z", [(i, i + steps) for i in range(first, last)])


def gather_chips(own):
    return swap(own, ("yl",)), swap(own, ("yh", "yl")), swap(own, ("yh",))


def gather_cores(own, received):
    by_l, by_d, by_h = received
    near = [own, by_l, swap(own, ("c",)), swap(by_l, ("c",))]
    return near + [by_h, by_d, swap(by_h, ("c",)), swap(by_d, ("c",))]


def sum_cores(keep, send):
    return keep.astype(f32) + swap(send, ("c",)).astype(f32)


def from_chips(near, far):
    far = far.astype(bf16)
    by_h = swap(far[:128], ("yh",))
    by_d = swap(far[128:], ("yh", "yl"))
    by_l = swap(near[128:].astype(bf16), ("yl",))
    return by_l, by_d, by_h


def sum_chips(near, received):
    by_l, by_d, by_h = received
    return near[:128] + by_l.astype(f32) + by_d.astype(f32) + by_h.astype(f32)


def pick(parts, index):
    return lax.dynamic_index_in_dim(parts, index, 0, False)


def trade_cores(parts, core):
    parts = parts.reshape(2, 2, *parts.shape[1:]).swapaxes(0, 1)
    mine, got = pick(parts, core), swap(pick(parts, 1 - core), ("c",))
    return jnp.where(core == 0, jnp.stack([mine, got], 1), jnp.stack([got, mine], 1))


def trade_chips(parts, yh):
    mine, got = pick(parts, yh), swap(pick(parts, 1 - yh), ("yh",))
    parts = jnp.where(yh == 0, jnp.stack([mine, got]), jnp.stack([got, mine]))
    return parts.reshape(4, *parts.shape[2:])


def both_halves(own, other, yl):
    return jnp.where(yl == 0, jnp.concatenate([own, other], 0), jnp.concatenate([other, own], 0))


def on_device(
    tokens, w_query, w_key, w_value, w_output, w_gate, w_up, w_down, norm_attn, norm_ffn, cotangent
):
    together = lax.optimization_barrier
    z, yh = lax.axis_index("z"), lax.axis_index("yh")
    core, yl = lax.axis_index("c"), lax.axis_index("yl")
    gain_one = norm_attn.astype(f32)[:, None]
    gain_two = norm_ffn.astype(f32)[:, None]
    flip = (yh * 4 + core * 2 + yl) * 128
    at = jnp.stack([z, flip, core, yl, lax.axis_index("x")]).astype(jnp.int32)

    xh, inverse_one, cot_here = order(at, tokens[0], cotangent[0])
    inputs = lax.dynamic_slice_in_dim(tokens[0], yl * 128, 128, 0).astype(f32)

    xh_c, xh_h = swap(xh, ("c",)), swap(xh, ("yh",))
    copies, rest, out_rows = prepare(
        w_query, w_key, w_value, w_output.T, w_gate, w_up, w_down.T, gain_one, gain_two
    )
    w_qkv = lax.all_to_all(copies, ALL, 0, 0).reshape(2048, 384)
    rest = trade_chips(trade_cores(rest, core), yh)
    out_rows = trade_chips(trade_cores(out_rows, core), yh).reshape(128, OUT)

    positions = (z * 1024 + (jnp.arange(1024, dtype=jnp.int32) ^ flip)).astype(f32)
    freqs = rope_base ** (-2.0 * jnp.arange(HD // 2, dtype=f32) / HD)
    angles = positions[:, None] * freqs[None, :]
    cosine, sine = jnp.cos(angles), jnp.sin(angles)
    cosine = jnp.concatenate([cosine] * 4, -1)
    sine = jnp.concatenate([-sine, sine, -sine, sine], -1)

    xh_h, w_qkv, cosine, sine, rest, out_rows = together(
        (xh_h, w_qkv, cosine, sine, rest, out_rows)
    )
    xhs = [xh, xh_c, xh_h, swap(xh_h, ("c",))]

    q, kv = qkv_project(xhs, w_qkv, cosine, sine)
    kv, out_rows = together((kv, out_rows))
    kvs = [kv] + [shifted(kv, by) for by in (1, 2, 3)]
    ws = jnp.concatenate([out_rows] + [crossed(out_rows, "x", mask) for mask in (1, 2, 3)], 0)
    kvs, rest, ws, cot_here = together((kvs, rest, ws, cot_here))
    w_ffn = lax.all_gather(rest.reshape(128, -1), ("x", "z"), axis=0, tiled=True)
    ws = [ws] + [crossed(ws, "z", mask) for mask in (1, 2, 3)]
    cot_c, cot_h = swap(cot_here, ("c",)), swap(cot_here, ("yh",))
    ob, o_t, lse = attn_fwd(at, q, kvs)
    ob, cot_h, ws = together((ob, cot_h, ws))
    cots = [cot_here, cot_c, cot_h, swap(cot_h, ("c",))]
    branch, w_out = branch_project(at, ob, ws)
    near, far = sum_cores(*branch[:2]), sum_cores(*branch[2:])
    middle = inputs + sum_chips(near, from_chips(near, far))
    inverse_two = lax.rsqrt(jnp.mean(middle * middle, axis=-1, keepdims=True) + epsilon)
    hn = (middle * inverse_two).astype(bf16)

    received = gather_chips(hn)
    dhid = dhid_project(cots, w_ffn)
    received, dhid = together((received, dhid))
    hns = gather_cores(hn, received)
    hid, dgu, dns = ffn(hns, dhid, w_ffn)
    near, far = sum_cores(*dns[:2]), sum_cores(*dns[2:])
    received = from_chips(near, far)
    grads, ys = ffn_grad(hns, cots, dgu, hid, w_ffn)
    received, grads = together((received, grads))
    dn2 = sum_chips(near, received)
    dh = (
        cots[0][:128].astype(f32)
        + inverse_two * dn2
        - middle * inverse_two**3 * jnp.mean(dn2 * middle, axis=-1, keepdims=True)
    )
    dh_low, ys = together((dh.astype(bf16), ys))
    received = gather_chips(dh_low)
    y_near, y_far = sum_cores(*ys[:2]), sum_cores(*ys[2:])
    received, y_near, y_far = together((received, y_near, y_far))
    dhs = gather_cores(dh_low, received)

    do, grads = dh_project(dhs, w_out, ob, grads)
    grads = lax.psum_scatter(grads, ("x", "z"), scatter_dimension=0, tiled=True)
    do, y_near, y_far = together((do, y_near, y_far))
    received = from_chips(y_near, y_far)
    dq, *dkvs = attn_bwd(at, q, kvs, do, o_t, lse)
    received, dkvs = together((received, dkvs))
    block_out = (middle + sum_chips(y_near, received)).astype(bf16)
    block_out, dkvs = together((block_out, dkvs))
    block_other = swap(block_out, ("yl",))
    dkvs = dkvs[:1] + [shifted(dkvs[by], -by) for by in (1, 2, 3)]
    dkvs, block_other = together((dkvs, block_other))
    block_out = both_halves(block_out, block_other, yl)
    others = [swap(part, ("c",)) for part in dkvs]
    dqkv, far_send, near_send, far_keep, near_keep = dqkv_project(
        at, dq, dkvs, others, w_qkv, cosine, sine
    )
    near, far = sum_cores(near_keep, near_send), sum_cores(far_keep, far_send)
    near, far, dqkv = together((near, far, dqkv))
    received = from_chips(near, far)
    dn1 = sum_chips(near, received)
    grad_qkv = qkv_grad(xhs, dqkv)
    grad_qkv = lax.all_to_all(grad_qkv.reshape(16, 128, 384), ("x", "z"), 0, 0)
    grads = trade_cores(grads.reshape(4, 32, 3 * FF_PAD + OUT), core)
    input_grad = (
        dh
        + inverse_one * dn1
        - inputs * inverse_one**3 * jnp.mean(dn1 * inputs, axis=-1, keepdims=True)
    )
    input_grad, grad_qkv, grads = together((input_grad, grad_qkv, grads))
    other = swap(input_grad.astype(bf16), ("yl",)).astype(f32)
    input_grad = both_halves(input_grad, other, yl)
    grad_qkv = jnp.sum(grad_qkv.astype(f32), 0).astype(bf16).reshape(4, 32, 384)
    grad_qkv = trade_chips(trade_cores(grad_qkv, core), yh)
    grad_gate, grad_up, grad_down, grad_out, gain_grad_two = finish_ffn(
        trade_chips(grads, yh), w_gate, w_up, gain_two
    )
    grad_query, grad_key, grad_value, gain_grad_one = finish_qkv(
        grad_qkv, w_query, w_key, w_value, gain_one
    )
    gain_grad_one = gain_grad_one + swap(gain_grad_one, ("yl",))
    gain_grad_two = gain_grad_two + swap(gain_grad_two, ("yl",))
    return (
        block_out[None],
        input_grad[None],
        grad_query,
        grad_key,
        grad_value,
        grad_out.T,
        grad_gate,
        grad_up,
        grad_down.T,
        gain_grad_one[:, 0],
        gain_grad_two[:, 0],
    )


def solution(mesh):
    mesh = Mesh(mesh.devices.reshape(4, 4, 2, 2, 2), ("x", "z", "yh", "c", "yl"))
    ctx = ("z", "yh", "c")
    rows, cols = P(ALL, "yl"), P("yl", ALL)
    seq = P("x", ctx, None)
    vec = P(ALL)
    in_specs = (seq, rows, rows, rows, cols, rows, rows, cols, vec, vec, seq)
    out_specs = (seq, seq, rows, rows, rows, cols, rows, rows, cols, vec, vec)
    return jax.shard_map(
        on_device, mesh=mesh, in_specs=in_specs, out_specs=out_specs, check_vma=False
    )
```

```python
import functools

import jax
import jax.numpy as jnp
from jax import lax
from jax.experimental import pallas as pl
from jax.experimental.pallas import tpu as pltpu
from jax.sharding import Mesh, PartitionSpec as P

HD = 64
HEADS = 8
FF_BLOCK = 704
FF_PAD = 768
OUT = HEADS * HD
QKV = OUT + 2 * HD
REST = 3 * FF_PAD
ROWS = 512
LOG2E = 1.4426950408889634
epsilon = 1e-05
rope_base = 10000.0
masked_low = -1e30
f32 = jnp.float32
bf16 = jnp.bfloat16

ALL = ("x", "z", "yh", "c")

NN = (((1,), (0,)), ((), ()))
NT = (((1,), (1,)), ((), ()))
TN = (((0,), (0,)), ((), ()))

VMEM = pl.BlockSpec(memory_space=pltpu.VMEM)
SMEM = pl.BlockSpec(memory_space=pltpu.SMEM)
BIG = pltpu.CompilerParams(vmem_limit_bytes=56 * 2**20)


def mm(a, b, dims):
    return lax.dot_general(a, b, dims, preferred_element_type=f32)


def turn(u, cosine, sine_signed):
    width = u.shape[-1]
    lane = lax.broadcasted_iota(jnp.int32, u.shape, 1)
    turned = jnp.where(
        lane % HD < HD // 2, pltpu.roll(u, width - HD // 2, 1), pltpu.roll(u, HD // 2, 1)
    )
    return u * cosine + turned * sine_signed


def order_kernel(at_ref, x_ref, cot_ref, xh_ref, inv_ref, cot_out):
    for half in range(2):
        first = pl.multiple_of((at_ref[3] ^ half) * 128, 128)
        rows = slice(half * 128, half * 128 + 128)
        x = x_ref[pl.ds(first, 128), :].astype(f32)
        inverse = lax.rsqrt(jnp.mean(x * x, axis=-1, keepdims=True) + epsilon)
        xh_ref[rows, :] = (x * inverse).astype(bf16)
        cot_out[rows, :] = cot_ref[pl.ds(first, 128), :]
        if half == 0:
            inv_ref[...] = inverse


def order(at, x, cot):
    low = jax.ShapeDtypeStruct(x.shape, bf16)
    return pl.pallas_call(
        order_kernel,
        in_specs=[SMEM, VMEM, VMEM],
        out_specs=(VMEM,) * 3,
        out_shape=(low, jax.ShapeDtypeStruct((128, 1), f32), low),
        cost_estimate=pl.CostEstimate(flops=2**20, bytes_accessed=4 * 2**20, transcendentals=0),
        compiler_params=BIG,
        name="order",
    )(at, x, cot)


def prepare_kernel(wq, wk, wv, wo_t, wg, wu, wd_t, g_one, g_two, qkv_ref, rest_ref, out_ref):
    g_one, g_two = g_one[...], g_two[...]
    scaled = lambda ref, gain: (ref[...].astype(f32) * gain).astype(bf16)
    query, key, value = scaled(wq, g_one), scaled(wk, g_one), scaled(wv, g_one)
    for core in range(2):
        head = slice(core * HD, core * HD + HD)
        rows = jnp.concatenate([query[:, core * OUT : core * OUT + OUT], key[:, head], value[:, head]], 1)
        for copy in range(32):
            qkv_ref[copy * 2 + core] = rows
        out_ref[core] = wo_t[:, core * OUT : core * OUT + OUT]
    lane = lax.broadcasted_iota(jnp.int32, (32, FF_PAD), 1)
    for k, (ref, gain) in enumerate(((wg, g_two), (wu, g_two), (wd_t, None))):
        w = ref[...].astype(f32)
        w = w if gain is None else w * gain
        for part in range(4):
            shift = (w.shape[1] - part * FF_BLOCK) % w.shape[1]
            block = pltpu.roll(w, shift, 1)[:, :FF_PAD] if shift else w[:, :FF_PAD]
            block = jnp.where(lane < FF_BLOCK, block, 0.0)
            rest_ref[part, :, k * FF_PAD : (k + 1) * FF_PAD] = block.astype(bf16)


def prepare(*args):
    return pl.pallas_call(
        prepare_kernel,
        in_specs=[VMEM] * 9,
        out_specs=(VMEM,) * 3,
        out_shape=(
            jax.ShapeDtypeStruct((64, 32, QKV), bf16),
            jax.ShapeDtypeStruct((4, 32, REST), bf16),
            jax.ShapeDtypeStruct((2, 32, OUT), bf16),
        ),
        cost_estimate=pl.CostEstimate(flops=2**20, bytes_accessed=3 * 2**20, transcendentals=0),
        compiler_params=BIG,
        name="prepare",
    )(*args)


def finish_ffn_kernel(parts, out_parts, wg, wu, g_two, gate_ref, up_ref, down_ref, out_ref, gain_ref):
    def joined(first):
        total = jnp.zeros(gate_ref.shape, f32)
        for part in range(4):
            block = parts[part, :, first : first + FF_PAD].astype(f32)
            block = jnp.concatenate(
                [block, jnp.zeros((32, total.shape[1] - FF_PAD), f32)], 1
            )
            total = total + (pltpu.roll(block, part * FF_BLOCK, 1) if part else block)
        return total

    gate, up = joined(0), joined(FF_PAD)
    gain_ref[...] = jnp.sum(
        wg[...].astype(f32) * gate + wu[...].astype(f32) * up, axis=1, keepdims=True
    )
    gate_ref[...] = gate * g_two[...]
    up_ref[...] = up * g_two[...]
    down_ref[...] = joined(2 * FF_PAD)
    out_ref[...] = jnp.concatenate([out_parts[0], out_parts[1]], 1)


def finish_ffn(parts, out_parts, wg, wu, g_two):
    wide = jax.ShapeDtypeStruct(wg.shape, f32)
    return pl.pallas_call(
        finish_ffn_kernel,
        in_specs=[VMEM] * 5,
        out_specs=(VMEM,) * 5,
        out_shape=(
            wide,
            wide,
            wide,
            jax.ShapeDtypeStruct((32, 2 * OUT), f32),
            jax.ShapeDtypeStruct((32, 1), f32),
        ),
        cost_estimate=pl.CostEstimate(flops=2**20, bytes_accessed=3 * 2**20, transcendentals=0),
        compiler_params=BIG,
        name="finish_ffn",
    )(parts, out_parts, wg, wu, g_two)


def finish_qkv_kernel(parts, wq, wk, wv, g_one, q_ref, k_ref, v_ref, gain_ref):
    joined = lambda first, width: jnp.concatenate(
        [parts[core, :, first : first + width] for core in range(2)], 1
    )
    query, key, value = joined(0, OUT), joined(OUT, HD), joined(OUT + HD, HD)
    total = jnp.sum(wq[...].astype(f32) * query, axis=1, keepdims=True)
    total = total + jnp.sum(
        wk[...].astype(f32) * key + wv[...].astype(f32) * value, axis=1, keepdims=True
    )
    gain_ref[...] = total
    q_ref[...] = query * g_one[...]
    k_ref[...] = key * g_one[...]
    v_ref[...] = value * g_one[...]


def finish_qkv(parts, wq, wk, wv, g_one):
    shapes = [w.shape for w in (wq, wk, wv)] + [(32, 1)]
    return pl.pallas_call(
        finish_qkv_kernel,
        in_specs=[VMEM] * 5,
        out_specs=(VMEM,) * 4,
        out_shape=tuple(jax.ShapeDtypeStruct(shape, f32) for shape in shapes),
        cost_estimate=pl.CostEstimate(flops=2**18, bytes_accessed=2**19, transcendentals=0),
        compiler_params=BIG,
        name="finish_qkv",
    )(parts, wq, wk, wv, g_one)


def qkv_kernel(x0, x1, w_ref, cos_ref, sin_ref, q_ref, kv_ref):
    scale = HD**-0.5 * LOG2E
    for part, x_ref in enumerate((x0, x1)):
        rows = slice(part * 256, part * 256 + 256)
        lin = mm(x_ref[...], w_ref[...], NN)
        cosine, sine = cos_ref[rows], sin_ref[rows]
        for k in range(OUT // 128):
            cols = slice(k * 128, k * 128 + 128)
            q_ref[rows, cols] = (turn(lin[:, cols], cosine, sine) * scale).astype(bf16)
        kv = lin[:, OUT:]
        lane = lax.broadcasted_iota(jnp.int32, kv.shape, 1)
        kv_ref[rows, :] = jnp.where(lane < HD, turn(kv, cosine, sine), kv).astype(bf16)


def qkv_project(xs, w, cosine, sine):
    return pl.pallas_call(
        qkv_kernel,
        in_specs=[VMEM] * 5,
        out_specs=(VMEM, VMEM),
        out_shape=(
            jax.ShapeDtypeStruct((ROWS, OUT), bf16),
            jax.ShapeDtypeStruct((ROWS, 2 * HD), bf16),
        ),
        cost_estimate=pl.CostEstimate(
            flops=2 * ROWS * 2048 * QKV, bytes_accessed=6 * 2**20, transcendentals=0
        ),
        compiler_params=BIG,
        name="qkv_project",
    )(*xs, w, cosine, sine)


def attn_fwd_kernel(
    at_ref, q_ref, kv0, kv1, kv2, kv3, o_ref, ot_ref, lse_ref, q_pad, keys_all, values_t
):
    depth, flip, later = at_ref[0], at_ref[1], at_ref[5]
    for h in range(HEADS):
        q_pad[h, :, :HD] = q_ref[:, h * HD : (h + 1) * HD]
        q_pad[h, :, HD:] = jnp.zeros((ROWS, HD), bf16)
    for b, kv_ref in enumerate((kv0, kv1, kv2, kv3)):

        @pl.when(depth >= b)
        def _():
            keys_all[b] = kv_ref[...]
            values_t[b, :HD] = kv_ref[...].T[HD:]
            values_t[b, HD:] = jnp.ones((16, 2 * ROWS), bf16)

    outs = []
    for first in range(0, HEADS, 4):
        heads = range(first, first + 4)

        def block(b, offset, state, masked):
            keys = keys_all[b, pl.ds(offset, ROWS), :]
            values = values_t[b, :, pl.ds(offset, ROWS)]
            scores = [mm(keys, q_pad[h], NT) for h in heads]
            if masked:
                k_pos = lax.broadcasted_iota(jnp.int32, (ROWS, ROWS), 0) ^ flip
                q_pos = lax.broadcasted_iota(jnp.int32, (ROWS, ROWS), 1) ^ flip
                scores = [jnp.where(k_pos <= q_pos, s, masked_low) for s in scores]
            out = []
            for (top, acc), s in zip(state, scores):
                new_top = jnp.maximum(top, jnp.max(s, axis=0, keepdims=True))
                p = jnp.exp2(s - new_top).astype(bf16)
                acc = acc * jnp.exp2(top - new_top) + mm(values, p, NN)
                out.append((new_top, acc))
            return tuple(out)

        state = tuple(
            (jnp.full((1, ROWS), masked_low, f32), jnp.zeros((HD + 16, ROWS), f32)) for _ in heads
        )
        state = block(0, 0, state, True)
        state = lax.fori_loop(0, later, lambda j, st: block(0, ROWS, st, False), state)
        state = lax.fori_loop(
            0,
            2 * depth,
            lambda j, st: block(1 + j // 2, pl.multiple_of((j % 2) * ROWS, ROWS), st, False),
            state,
        )
        for h, (top, acc) in zip(heads, state):
            total = acc[HD : HD + 1]
            lse_ref[pl.ds(h, 1), :] = top + jnp.log2(total)
            outs.append(acc[:HD] * (1.0 / total))
    o_t = jnp.concatenate(outs, 0)
    ot_ref[...] = o_t
    o_ref[...] = o_t.T.astype(bf16)


def attn_fwd(at, q, kvs):
    return pl.pallas_call(
        attn_fwd_kernel,
        out_shape=(
            jax.ShapeDtypeStruct((ROWS, OUT), bf16),
            jax.ShapeDtypeStruct((OUT, ROWS), f32),
            jax.ShapeDtypeStruct((HEADS, ROWS), f32),
        ),
        in_specs=[SMEM] + [VMEM] * 5,
        out_specs=(VMEM,) * 3,
        scratch_shapes=[
            pltpu.VMEM((HEADS, ROWS, 128), bf16),
            pltpu.VMEM((4, 2 * ROWS, 128), bf16),
            pltpu.VMEM((4, HD + 16, 2 * ROWS), bf16),
        ],
        cost_estimate=pl.CostEstimate(
            flops=25 * 10**9, bytes_accessed=6 * 2**20, transcendentals=12 * 10**6
        ),
        compiler_params=BIG,
        name="attn_fwd",
    )(at, q, *kvs)


def branch_kernel(at_ref, o_ref, w0, w1, w2, w3, keep, send, w_ref):
    for i, piece in enumerate((w0, w1, w2, w3)):
        for j in range(4):
            first = ((at_ref[4] ^ j) * 4 + (at_ref[0] ^ i)) * 128
            w_ref[pl.ds(pl.multiple_of(first, 128), 128), :] = piece[j * 128 : j * 128 + 128]
    send[...] = mm(o_ref[256:], w_ref[...], NT).astype(bf16)
    keep[...] = mm(o_ref[:256], w_ref[...], NT).astype(bf16)


def branch_project(at, o, ws):
    depth = 4 * ws[0].shape[0]
    part = jax.ShapeDtypeStruct((256, depth), bf16)
    return pl.pallas_call(
        branch_kernel,
        in_specs=[SMEM] + [VMEM] * 5,
        out_specs=(VMEM,) * 3,
        out_shape=(part, part, jax.ShapeDtypeStruct((depth, OUT), bf16)),
        cost_estimate=pl.CostEstimate(
            flops=2 * ROWS * depth * OUT, bytes_accessed=6 * 2**20, transcendentals=0
        ),
        compiler_params=BIG,
        name="branch_project",
    )(at, o, *ws)


def attn_bwd_kernel(
    at_ref, q_ref, kv0, kv1, kv2, kv3, do_ref, ot_ref, lse_ref,
    dq_ref, dkv0, dkv1, dkv2, dkv3,
    q_pad, do_pad, keys_all, keys_t, dkv_all, dqt, delta,
):
    depth, flip, later = at_ref[0], at_ref[1], at_ref[5]
    nothing = jnp.zeros((ROWS, HD), bf16)
    do_t = do_ref[...].astype(f32).T
    for h in range(HEADS):
        cols = slice(h * HD, (h + 1) * HD)
        q_pad[h, :, :HD] = q_ref[:, cols]
        q_pad[h, :, HD:] = nothing
        do_pad[h, :, :HD] = nothing
        do_pad[h, :, HD:] = do_ref[:, cols]
        delta[pl.ds(h, 1), :] = jnp.sum(do_t[cols] * ot_ref[cols, :], axis=0, keepdims=True)
    for b, kv_ref in enumerate((kv0, kv1, kv2, kv3)):

        @pl.when(depth >= b)
        def _():
            keys_all[b] = kv_ref[...]
            keys_t[b] = kv_ref[...].T[:HD]

    dqt[...] = jnp.zeros_like(dqt)
    lane = lax.broadcasted_iota(jnp.int32, (1, 128), 1)
    out_scale = jnp.where(lane < HD, 1.0 / LOG2E, 1.0)

    def part(b, first, count, masked):
        at = slice(first, first + count)
        keys, turned = keys_all[b, at, :], keys_t[b, :, at]
        if masked:
            k_pos = lax.broadcasted_iota(jnp.int32, (count, ROWS), 0) ^ flip
            q_pos = lax.broadcasted_iota(jnp.int32, (count, ROWS), 1) ^ flip
            visible = k_pos <= q_pos
        dkv = jnp.zeros((count, 128), f32)
        for h in range(HEADS):
            query, grad = q_pad[h], do_pad[h]
            p = jnp.exp2(mm(keys, query, NT) - lse_ref[pl.ds(h, 1), :])
            if masked:
                p = jnp.where(visible, p, 0.0)
            dp = mm(keys, grad, NT)
            ds = (p * (dp - delta[pl.ds(h, 1), :])).astype(bf16)
            dkv = dkv + mm(p.astype(bf16), grad, NN) + mm(ds, query, NN)
            dqt[h * HD : (h + 1) * HD, :] += mm(turned, ds, NN)
        dkv_all[b, at, :] = (dkv * out_scale).astype(bf16)

    def far(j, _):
        part(1 + j, 0, 2 * ROWS, False)
        return 0

    lax.fori_loop(0, depth, far, 0)
    part(0, 0, ROWS, True)

    @pl.when(later == 1)
    def _():
        part(0, ROWS, ROWS, False)

    @pl.when(later == 0)
    def _():
        dkv_all[0, ROWS:, :] = jnp.zeros((ROWS, 128), bf16)

    dq_ref[...] = dqt[...].T * HD**-0.5
    for b, out_ref in enumerate((dkv0, dkv1, dkv2, dkv3)):
        out_ref[...] = dkv_all[b]


def attn_bwd(at, q, kvs, do, ot, lse):
    block = jax.ShapeDtypeStruct(kvs[0].shape, bf16)
    return pl.pallas_call(
        attn_bwd_kernel,
        out_shape=(jax.ShapeDtypeStruct((ROWS, OUT), f32), block, block, block, block),
        in_specs=[SMEM] + [VMEM] * 8,
        out_specs=(VMEM,) * 5,
        scratch_shapes=[
            pltpu.VMEM((HEADS, ROWS, 128), bf16),
            pltpu.VMEM((HEADS, ROWS, 128), bf16),
            pltpu.VMEM((4, 2 * ROWS, 128), bf16),
            pltpu.VMEM((4, HD, 2 * ROWS), bf16),
            pltpu.VMEM((4, 2 * ROWS, 128), bf16),
            pltpu.VMEM((OUT, ROWS), f32),
            pltpu.VMEM((HEADS, ROWS), f32),
        ],
        cost_estimate=pl.CostEstimate(
            flops=50 * 10**9, bytes_accessed=8 * 2**20, transcendentals=12 * 10**6
        ),
        compiler_params=BIG,
        name="attn_bwd",
    )(at, q, *kvs, do, ot, lse)


def dhid_kernel(*refs):
    w_ref, out_ref = refs[4:]
    for part, cot_ref in enumerate(refs[:4]):
        out_ref[part * 256 : part * 256 + 256, :] = mm(cot_ref[...], w_ref[...], NN)


def dhid_project(cots, w):
    depth = w.shape[0]
    return pl.pallas_call(
        dhid_kernel,
        grid=(1,),
        in_specs=[VMEM] * 4 + [pl.BlockSpec((depth, FF_PAD), lambda i: (0, 2))],
        out_specs=VMEM,
        out_shape=jax.ShapeDtypeStruct((1024, FF_PAD), f32),
        cost_estimate=pl.CostEstimate(
            flops=2 * 1024 * depth * FF_PAD, bytes_accessed=10 * 2**20, transcendentals=0
        ),
        compiler_params=BIG,
        name="dhid_project",
    )(*cots, w)


def ffn_kernel(*refs):
    hns, dhid_ref, w_hbm = refs[:8], refs[8], refs[9]
    hid_ref, dgu_ref = refs[10:12]
    dns = refs[12:16]
    hn_buf, dn_buf, w_ref, w_sems, in_sems, out_sems = refs[16:]
    step = pl.program_id(0)
    parts = [slice(k * FF_PAD, (k + 1) * FF_PAD) for k in range(2)]
    weights = [
        pltpu.make_async_copy(w_hbm.at[:, parts[k]], w_ref.at[:, parts[k]], w_sems.at[k])
        for k in range(2)
    ]

    def fetch(s):
        return [
            pltpu.make_async_copy(
                hns[4 * s + k], hn_buf.at[s, k * 128 : k * 128 + 128], in_sems.at[s, k]
            )
            for k in range(4)
        ]

    def flush(s):
        return [
            pltpu.make_async_copy(
                dn_buf.at[s, k * 256 : k * 256 + 256], dns[2 * s + k], out_sems.at[s, k]
            )
            for k in range(2)
        ]

    def at(s, action, copies):
        @pl.when(step == s)
        def _():
            for copy in copies:
                action(copy)

    start = lambda copy: copy.start()
    wait = lambda copy: copy.wait()
    at(0, start, fetch(0) + weights + fetch(1))
    for s in range(2):
        at(s, wait, fetch(s))
    at(0, wait, weights[:1])
    hn = hn_buf[step]
    gate = mm(hn, w_ref[:, parts[0]], NN)
    at(0, wait, weights[1:])
    up = mm(hn, w_ref[:, parts[1]], NN)
    dhid = dhid_ref[...]
    sg = 1.0 / (1.0 + jnp.exp(-gate))
    act = gate * sg
    hid_ref[...] = (act * up).astype(bf16)
    dgu_ref[:, parts[0]] = (dhid * up * sg * (1.0 + gate * (1.0 - sg))).astype(bf16)
    dgu_ref[:, parts[1]] = (dhid * act).astype(bf16)
    dn_buf[step] = mm(dgu_ref[...], w_ref[...], NT).astype(bf16)
    for s in range(2):
        at(s, start, flush(s))
    at(1, wait, flush(0) + flush(1))


def ffn(hns, dhid, w):
    depth = w.shape[0]
    rowwise = lambda width: pl.BlockSpec((512, width), lambda i: (i, 0))
    hbm = pl.BlockSpec(memory_space=pl.ANY)
    quarter = jax.ShapeDtypeStruct((256, depth), bf16)
    outs = pl.pallas_call(
        ffn_kernel,
        grid=(2,),
        in_specs=[hbm] * 8 + [rowwise(FF_PAD), hbm],
        out_specs=(rowwise(FF_PAD), rowwise(2 * FF_PAD)) + (hbm,) * 4,
        out_shape=(
            jax.ShapeDtypeStruct((1024, FF_PAD), bf16),
            jax.ShapeDtypeStruct((1024, 2 * FF_PAD), bf16),
        )
        + (quarter,) * 4,
        scratch_shapes=[
            pltpu.VMEM((2, 512, depth), bf16),
            pltpu.VMEM((2, 512, depth), bf16),
            pltpu.VMEM((depth, 2 * FF_PAD), bf16),
            pltpu.SemaphoreType.DMA((2,)),
            pltpu.SemaphoreType.DMA((2, 4)),
            pltpu.SemaphoreType.DMA((2, 2)),
        ],
        cost_estimate=pl.CostEstimate(
            flops=8 * 1024 * depth * FF_PAD,
            bytes_accessed=25 * 2**20,
            transcendentals=1024 * FF_PAD,
        ),
        compiler_params=BIG,
        name="ffn",
    )(*hns, dhid, w)
    return outs[0], outs[1], outs[2:]


def ffn_grad_kernel(*refs):
    hn = jnp.concatenate([r[...] for r in refs[:8]], 0)
    cot = jnp.concatenate([r[...] for r in refs[8:12]], 0)
    dgu_ref, hid_ref, w_ref, out_ref = refs[12:16]
    hid = hid_ref[...]
    out_ref[:, : 2 * FF_PAD] = mm(hn, dgu_ref[...], TN).astype(bf16)
    out_ref[:, 2 * FF_PAD :] = mm(cot, hid, TN).astype(bf16)
    for part, y_ref in enumerate(refs[16:]):
        y_ref[...] = mm(hid[part * 256 : part * 256 + 256], w_ref[...], NT).astype(bf16)


def ffn_grad(hns, cots, dgu, hid, w):
    depth = hns[0].shape[1]
    block = 256
    piece = lambda rows: pl.BlockSpec((rows, block), lambda i: (0, i))
    outs = pl.pallas_call(
        ffn_grad_kernel,
        grid=(depth // block,),
        in_specs=[piece(a.shape[0]) for a in hns + cots]
        + [VMEM] * 2
        + [pl.BlockSpec((block, FF_PAD), lambda i: (i, 2))],
        out_specs=(pl.BlockSpec((block, 3 * FF_PAD), lambda i: (i, 0)),) + (piece(256),) * 4,
        out_shape=(jax.ShapeDtypeStruct((depth, REST + OUT), bf16),)
        + (jax.ShapeDtypeStruct((256, depth), bf16),) * 4,
        cost_estimate=pl.CostEstimate(
            flops=8 * 1024 * depth * FF_PAD, bytes_accessed=30 * 2**20, transcendentals=0
        ),
        compiler_params=BIG,
        name="ffn_grad",
    )(*hns, *cots, dgu, hid, w)
    return outs[0], outs[1:]


def dh_kernel(p0, p1, p2, p3, w_ref, ob_ref, _, do_ref, grads_hbm, part, sem):
    for k in range(4):
        cols = slice(k * 512, k * 512 + 512)
        dh = jnp.concatenate([r[:, cols] for r in (p0, p1, p2, p3)], 0)
        part[cols, :] = mm(dh, ob_ref[...], TN).astype(bf16)
    copy = pltpu.make_async_copy(part, grads_hbm.at[:, REST:], sem)
    copy.start()
    for k, pieces in enumerate(((p0, p1), (p2, p3))):
        dh = jnp.concatenate([r[...] for r in pieces], 0)
        do_ref[k * 256 : k * 256 + 256, :] = mm(dh, w_ref[...], NN).astype(bf16)
    copy.wait()


def dh_project(pieces, w, ob, grads):
    depth = w.shape[0]
    hbm = pl.BlockSpec(memory_space=pl.ANY)
    return pl.pallas_call(
        dh_kernel,
        in_specs=[VMEM] * 6 + [hbm],
        out_specs=(VMEM, hbm),
        out_shape=(
            jax.ShapeDtypeStruct((ROWS, OUT), bf16),
            jax.ShapeDtypeStruct(grads.shape, bf16),
        ),
        scratch_shapes=[pltpu.VMEM((depth, OUT), bf16), pltpu.SemaphoreType.DMA(())],
        input_output_aliases={6: 1},
        cost_estimate=pl.CostEstimate(
            flops=4 * ROWS * depth * OUT, bytes_accessed=8 * 2**20, transcendentals=0
        ),
        compiler_params=BIG,
        name="dh_project",
    )(*pieces, w, ob, grads)


def dq_kernel(dq_ref, cos_ref, sin_ref, x0, x1, dqr_ref, grad_ref):
    @pl.when(pl.program_id(0) == 0)
    def _():
        cosine, sine = cos_ref[...], -sin_ref[...]
        for part in range(OUT // 128):
            cols = slice(part * 128, part * 128 + 128)
            dqr_ref[:, cols] = turn(dq_ref[:, cols], cosine, sine).astype(bf16)

    xh = jnp.concatenate([x0[...], x1[...]], 0)
    grad_ref[...] = mm(xh, dqr_ref[...], TN).astype(bf16)


def dq_project(dq, cosine, sine, xs):
    depth = xs[0].shape[1]
    block = 512
    return pl.pallas_call(
        dq_kernel,
        grid=(depth // block,),
        in_specs=[VMEM] * 3 + [pl.BlockSpec((256, block), lambda i: (0, i))] * 2,
        out_specs=(VMEM, pl.BlockSpec((block, OUT), lambda i: (i, 0))),
        out_shape=(
            jax.ShapeDtypeStruct((ROWS, OUT), bf16),
            jax.ShapeDtypeStruct((depth, OUT), bf16),
        ),
        cost_estimate=pl.CostEstimate(
            flops=2 * ROWS * depth * OUT, bytes_accessed=8 * 2**20, transcendentals=0
        ),
        compiler_params=BIG,
        name="dq_project",
    )(dq, cosine, sine, *xs)


def kv_grad_kernel(x0, x1, dkv_ref, out_ref):
    xh = jnp.concatenate([x0[...], x1[...]], 0)
    out_ref[...] = mm(xh, dkv_ref[...], TN).astype(bf16)


def kv_grad(xs, dkv):
    depth = xs[0].shape[1]
    block = 512
    return pl.pallas_call(
        kv_grad_kernel,
        grid=(depth // block,),
        in_specs=[pl.BlockSpec((256, block), lambda i: (0, i))] * 2 + [VMEM],
        out_specs=pl.BlockSpec((block, 2 * HD), lambda i: (i, 0)),
        out_shape=jax.ShapeDtypeStruct((depth, 2 * HD), bf16),
        cost_estimate=pl.CostEstimate(
            flops=4 * ROWS * depth * HD, bytes_accessed=6 * 2**20, transcendentals=0
        ),
        compiler_params=BIG,
        name="kv_grad",
    )(*xs, dkv)


def dqkv_kernel(dqr_ref, dkv_ref, other_ref, w_ref, cos_ref, sin_ref, dkvr_ref, send, keep):
    dkv = dkv_ref[...] + other_ref[...].astype(f32)
    lane = lax.broadcasted_iota(jnp.int32, dkv.shape, 1)
    dkvr = jnp.where(lane < HD, turn(dkv, cos_ref[...], -sin_ref[...]), dkv).astype(bf16)
    dkvr_ref[...] = dkvr
    dn = mm(jnp.concatenate([dqr_ref[...], dkvr], 1), w_ref[...], NT).astype(bf16)
    for step, out_ref in enumerate((send, keep)):

        @pl.when(pl.program_id(0) == step)
        def _():
            out_ref[...] = dn


def dqkv_project(dqr, dkv, other, w, cosine, sine):
    depth = w.shape[0]
    rowwise = lambda width: pl.BlockSpec((256, width), lambda i: (1 - i, 0))
    whole = pl.BlockSpec((256, depth), lambda i: (0, 0))
    return pl.pallas_call(
        dqkv_kernel,
        grid=(2,),
        in_specs=[rowwise(OUT), rowwise(128), rowwise(128), VMEM, rowwise(128), rowwise(128)],
        out_specs=(rowwise(128), whole, whole),
        out_shape=(jax.ShapeDtypeStruct((ROWS, 2 * HD), bf16),)
        + (jax.ShapeDtypeStruct((256, depth), bf16),) * 2,
        cost_estimate=pl.CostEstimate(
            flops=2 * ROWS * depth * QKV, bytes_accessed=10 * 2**20, transcendentals=0
        ),
        compiler_params=BIG,
        name="dqkv_project",
    )(dqr, dkv, other, w, cosine, sine)


def swap(value, axes):
    count = 2 ** len(axes)
    return lax.ppermute(value, axes, [(i, count - 1 - i) for i in range(count)])


def crossed(value, axis, mask):
    return lax.ppermute(value, axis, [(i, i ^ mask) for i in range(4)])


def shifted(value, steps):
    first, last = max(0, -steps), min(4, 4 - steps)
    return lax.ppermute(value, "z", [(i, i + steps) for i in range(first, last)])


def gather_chips(own):
    return swap(own, ("yl",)), swap(own, ("yh", "yl")), swap(own, ("yh",))


def gather_cores(own, by_l):
    return [own, by_l, swap(own, ("c",)), swap(by_l, ("c",))]


def sum_cores(keep, send):
    return keep.astype(f32) + swap(send, ("c",)).astype(f32)


def from_chip(total):
    return swap(total[128:].astype(bf16), ("yl",))


def from_chips(near, far):
    far = far.astype(bf16)
    return from_chip(near), swap(far[128:], ("yh", "yl")), swap(far[:128], ("yh",))


def sum_chips(near, *received):
    return near[:128] + sum(part.astype(f32) for part in received)


def pick(parts, index):
    return lax.dynamic_index_in_dim(parts, index, 0, False)


def in_order(which, mine, got, axis=0):
    return jnp.where(which == 0, jnp.stack([mine, got], axis), jnp.stack([got, mine], axis))


def trade_cores(parts, core):
    parts = jnp.moveaxis(parts, -3, 0)
    return in_order(core, pick(parts, core), swap(pick(parts, 1 - core), ("c",)), -3)


def both_halves(own, other, yl):
    return jnp.where(yl == 0, jnp.concatenate([own, other], 0), jnp.concatenate([other, own], 0))


def on_device(
    tokens, w_query, w_key, w_value, w_output, w_gate, w_up, w_down, norm_attn, norm_ffn, cotangent
):
    together = lax.optimization_barrier
    z, yh = lax.axis_index("z"), lax.axis_index("yh")
    core, yl = lax.axis_index("c"), lax.axis_index("yl")
    gain_one = norm_attn.astype(f32)[:, None]
    gain_two = norm_ffn.astype(f32)[:, None]
    flip = (core * 2 + yl) * 128
    at = jnp.stack([z, flip, core, yl, lax.axis_index("x"), yh]).astype(jnp.int32)

    xh, inverse_one, cot_here = order(at, tokens[0], cotangent[0])
    inputs = lax.dynamic_slice_in_dim(tokens[0], yl * 128, 128, 0).astype(f32)

    xhs = [xh, swap(xh, ("c",))]
    copies, rest, out_rows = prepare(
        w_query, w_key, w_value, w_output.T, w_gate, w_up, w_down.T, gain_one, gain_two
    )

    w_qkv = lax.all_to_all(copies, ALL, 0, 0).reshape(2048, QKV)
    out_rows = trade_cores(out_rows, core).reshape(64, OUT)
    out_rows = in_order(yh, out_rows, swap(out_rows, ("yh",))).reshape(128, OUT)
    rest = trade_cores(rest.reshape(2, 2, 32, REST), core)

    positions = ((z * 2 + yh) * ROWS + (jnp.arange(ROWS, dtype=jnp.int32) ^ flip)).astype(f32)
    freqs = rope_base ** (-2.0 * jnp.arange(HD // 2, dtype=f32) / HD)
    angles = positions[:, None] * freqs[None, :]
    cosine, sine = jnp.cos(angles), jnp.sin(angles)
    cosine = jnp.concatenate([cosine] * 4, -1)
    sine = jnp.concatenate([-sine, sine, -sine, sine], -1)

    w_qkv, cosine, sine, rest, out_rows, xhs = together(
        (w_qkv, cosine, sine, rest, out_rows, xhs)
    )

    q, kv = qkv_project(xhs, w_qkv, cosine, sine)
    kv, out_rows = together((kv, out_rows))
    kv_other = swap(kv, ("yh",))
    rest = in_order(yh, pick(rest, yh), swap(pick(rest, 1 - yh), ("yh",))).reshape(128, REST)
    ws = jnp.concatenate([out_rows] + [crossed(out_rows, "x", mask) for mask in (1, 2, 3)], 0)
    kv = jnp.concatenate([kv, kv_other], 0)
    kvs = [kv] + [shifted(kv, by) for by in (1, 2, 3)]
    kvs, ws, cot_here, rest = together((kvs, ws, cot_here, rest))
    w_ffn = lax.all_gather(rest, ("x", "z"), axis=0, tiled=True)
    ws = [ws] + [crossed(ws, "z", mask) for mask in (1, 2, 3)]
    cot_c, cot_h = swap(cot_here, ("c",)), swap(cot_here, ("yh",))
    ob, o_t, lse = attn_fwd(at, q, kvs)
    ob, ws, cot_h = together((ob, ws, cot_h))
    cots = [cot_here, cot_c, cot_h, swap(cot_h, ("c",))]
    keep, send, w_out = branch_project(at, ob, ws)
    total = sum_cores(keep, send)
    middle = inputs + sum_chips(total, from_chip(total))
    inverse_two = lax.rsqrt(jnp.mean(middle * middle, axis=-1, keepdims=True) + epsilon)
    hn = (middle * inverse_two).astype(bf16)

    received = gather_chips(hn)
    dhid = dhid_project(cots, w_ffn)
    (by_l, by_d, by_h), dhid = together((received, dhid))
    hns = gather_cores(hn, by_l) + [by_h, by_d, swap(by_h, ("c",)), swap(by_d, ("c",))]
    hid, dgu, dns = ffn(hns, dhid, w_ffn)
    near, far = sum_cores(*dns[:2]), sum_cores(*dns[2:])
    received = from_chips(near, far)
    grads, ys = ffn_grad(hns, cots, dgu, hid, w_ffn)
    received, grads = together((received, grads))
    dn2 = sum_chips(near, *received)
    dh = (
        cots[0][:128].astype(f32)
        + inverse_two * dn2
        - middle * inverse_two**3 * jnp.mean(dn2 * middle, axis=-1, keepdims=True)
    )
    dh_low, ys = together((dh.astype(bf16), ys))
    by_l, y_near, y_far = swap(dh_low, ("yl",)), sum_cores(*ys[:2]), sum_cores(*ys[2:])
    by_l, y_near, y_far = together((by_l, y_near, y_far))
    dhs = gather_cores(dh_low, by_l)

    do, grads = dh_project(dhs, w_out, ob, grads)
    grads = lax.psum_scatter(grads, ("x", "z"), scatter_dimension=0, tiled=True)
    do, y_near, y_far = together((do, y_near, y_far))
    received = from_chips(y_near, y_far)
    dq, *dkvs = attn_bwd(at, q, kvs, do, o_t, lse)
    received, dkvs = together((received, dkvs))
    block_out = (middle + sum_chips(y_near, *received)).astype(bf16)
    block_out, dkvs, dq = together((block_out, dkvs, dq))
    block_other = swap(block_out, ("yl",))
    dkvs = dkvs[:1] + [shifted(dkvs[by], -by) for by in (1, 2, 3)]

    def to_owners(grad, axis):
        parts = grad.reshape(4, grad.shape[0] // 4, -1)
        mine = lax.axis_index(axis)
        return [pick(parts, mine)] + [crossed(pick(parts, mine ^ m), axis, m) for m in (1, 2, 3)]

    added = lambda parts: sum(part.astype(f32) for part in parts).astype(bf16)
    dqr, grad_q = dq_project(dq, cosine, sine, xhs)
    grad_q = lax.all_to_all(grad_q.reshape(4, ROWS, OUT), "x", 0, 0)
    dkvs, block_other, dqr, grad_q = together((dkvs, block_other, dqr, grad_q))
    block_out = both_halves(block_out, block_other, yl)
    dkv = sum(part.astype(f32) for part in dkvs)
    other = swap(dkv[ROWS:].astype(bf16), ("yh",))
    dkvr, send, keep = dqkv_project(dqr, dkv[:ROWS], other, w_qkv, cosine, sine)
    total, dkvr, grad_q = together((sum_cores(keep, send), dkvr, added(grad_q)))
    received, grad_kv, grad_q = together(
        (from_chip(total), kv_grad(xhs, dkvr), to_owners(grad_q, "z"))
    )
    grad_kv = lax.all_to_all(grad_kv.reshape(16, 128, 2 * HD), ("x", "z"), 0, 0)
    dn1 = sum_chips(total, received)
    input_grad = (
        dh
        + inverse_one * dn1
        - inputs * inverse_one**3 * jnp.mean(dn1 * inputs, axis=-1, keepdims=True)
    )
    other, grad_kv = together((swap(input_grad.astype(bf16), ("yl",)), grad_kv))
    input_grad = both_halves(input_grad, other.astype(f32), yl)
    grad_kv = jnp.sum(grad_kv.astype(f32), 0).astype(bf16)
    grads = jnp.concatenate([grads, added(grad_q), grad_kv], -1)
    grads = trade_cores(grads.reshape(2, 2, 32, REST + OUT + QKV), core)
    mine, got = pick(grads, yh), swap(pick(grads, 1 - yh), ("yh",))
    attn_grads = mine[..., REST:].astype(f32) + got[..., REST:].astype(f32)
    grad_qkv = attn_grads[..., OUT:]
    grad_gate, grad_up, grad_down, grad_out, gain_grad_two = finish_ffn(
        in_order(yh, mine[..., :REST], got[..., :REST]).reshape(4, 32, REST),
        attn_grads[..., :OUT],
        w_gate,
        w_up,
        gain_two,
    )
    grad_query, grad_key, grad_value, gain_grad_one = finish_qkv(
        grad_qkv, w_query, w_key, w_value, gain_one
    )
    gain_grad_one = gain_grad_one + swap(gain_grad_one, ("yl",))
    gain_grad_two = gain_grad_two + swap(gain_grad_two, ("yl",))
    return (
        block_out[None],
        input_grad[None],
        grad_query,
        grad_key,
        grad_value,
        grad_out.T,
        grad_gate,
        grad_up,
        grad_down.T,
        gain_grad_one[:, 0],
        gain_grad_two[:, 0],
    )


def solution(mesh):
    mesh = Mesh(mesh.devices.reshape(4, 4, 2, 2, 2), ("x", "z", "yh", "c", "yl"))
    ctx = ("z", "yh", "c")
    rows, cols = P(ALL, "yl"), P("yl", ALL)
    seq = P("x", ctx, None)
    vec = P(ALL)
    in_specs = (seq, rows, rows, rows, cols, rows, rows, cols, vec, vec, seq)
    out_specs = (seq, seq, rows, rows, rows, cols, rows, rows, cols, vec, vec)
    return jax.shard_map(
        on_device, mesh=mesh, in_specs=in_specs, out_specs=out_specs, check_vma=False
    )
```

```python
import functools

import jax
import jax.numpy as jnp
from jax import lax
from jax.experimental import pallas as pl
from jax.experimental.pallas import tpu as pltpu
from jax.sharding import Mesh, PartitionSpec as P

HD = 64
HEADS = 8
FF_BLOCK = 704
FF_PAD = 768
OUT = HEADS * HD
QKV = OUT + 2 * HD
REST = 3 * FF_PAD
ROWS = 512
LOG2E = 1.4426950408889634
epsilon = 1e-05
rope_base = 10000.0
masked_low = -1e30
f32 = jnp.float32
bf16 = jnp.bfloat16

ALL = ("x", "z", "yh", "c")

NN = (((1,), (0,)), ((), ()))
NT = (((1,), (1,)), ((), ()))
TN = (((0,), (0,)), ((), ()))

VMEM = pl.BlockSpec(memory_space=pltpu.VMEM)
SMEM = pl.BlockSpec(memory_space=pltpu.SMEM)
BIG = pltpu.CompilerParams(vmem_limit_bytes=56 * 2**20)


def mm(a, b, dims):
    return lax.dot_general(a, b, dims, preferred_element_type=f32)


def turn(u, cosine, sine_signed):
    width = u.shape[-1]
    lane = lax.broadcasted_iota(jnp.int32, u.shape, 1)
    turned = jnp.where(
        lane % HD < HD // 2, pltpu.roll(u, width - HD // 2, 1), pltpu.roll(u, HD // 2, 1)
    )
    return u * cosine + turned * sine_signed


def order_kernel(at_ref, x_ref, cot_ref, xh_ref, inv_ref, cot_out):
    for half in range(2):
        first = pl.multiple_of((at_ref[3] ^ half) * 128, 128)
        rows = slice(half * 128, half * 128 + 128)
        x = x_ref[pl.ds(first, 128), :].astype(f32)
        inverse = lax.rsqrt(jnp.mean(x * x, axis=-1, keepdims=True) + epsilon)
        xh_ref[rows, :] = (x * inverse).astype(bf16)
        cot_out[rows, :] = cot_ref[pl.ds(first, 128), :]
        if half == 0:
            inv_ref[...] = inverse


def order(at, x, cot):
    low = jax.ShapeDtypeStruct(x.shape, bf16)
    return pl.pallas_call(
        order_kernel,
        in_specs=[SMEM, VMEM, VMEM],
        out_specs=(VMEM,) * 3,
        out_shape=(low, jax.ShapeDtypeStruct((128, 1), f32), low),
        cost_estimate=pl.CostEstimate(flops=2**20, bytes_accessed=4 * 2**20, transcendentals=0),
        compiler_params=BIG,
        name="order",
    )(at, x, cot)


def prepare_kernel(wq, wk, wv, wo_t, wg, wu, wd_t, g_one, g_two, qkv_ref, rest_ref, out_ref):
    g_one, g_two = g_one[...], g_two[...]
    scaled = lambda ref, gain: (ref[...].astype(f32) * gain).astype(bf16)
    query, key, value = scaled(wq, g_one), scaled(wk, g_one), scaled(wv, g_one)
    for core in range(2):
        head = slice(core * HD, core * HD + HD)
        rows = jnp.concatenate([query[:, core * OUT : core * OUT + OUT], key[:, head], value[:, head]], 1)
        for copy in range(32):
            qkv_ref[copy * 2 + core] = rows
        out_ref[core] = wo_t[:, core * OUT : core * OUT + OUT]
    lane = lax.broadcasted_iota(jnp.int32, (32, FF_PAD), 1)
    for k, (ref, gain) in enumerate(((wg, g_two), (wu, g_two), (wd_t, None))):
        w = ref[...].astype(f32)
        w = w if gain is None else w * gain
        for part in range(4):
            shift = (w.shape[1] - part * FF_BLOCK) % w.shape[1]
            block = pltpu.roll(w, shift, 1)[:, :FF_PAD] if shift else w[:, :FF_PAD]
            block = jnp.where(lane < FF_BLOCK, block, 0.0)
            rest_ref[part, :, k * FF_PAD : (k + 1) * FF_PAD] = block.astype(bf16)


def prepare(*args):
    return pl.pallas_call(
        prepare_kernel,
        in_specs=[VMEM] * 9,
        out_specs=(VMEM,) * 3,
        out_shape=(
            jax.ShapeDtypeStruct((64, 32, QKV), bf16),
            jax.ShapeDtypeStruct((4, 32, REST), bf16),
            jax.ShapeDtypeStruct((2, 32, OUT), bf16),
        ),
        cost_estimate=pl.CostEstimate(flops=2**20, bytes_accessed=3 * 2**20, transcendentals=0),
        compiler_params=BIG,
        name="prepare",
    )(*args)


def finish_ffn_kernel(parts, out_parts, wg, wu, g_two, gate_ref, up_ref, down_ref, out_ref, gain_ref):
    def joined(first):
        total = jnp.zeros(gate_ref.shape, f32)
        for part in range(4):
            block = parts[part, :, first : first + FF_PAD].astype(f32)
            block = jnp.concatenate(
                [block, jnp.zeros((32, total.shape[1] - FF_PAD), f32)], 1
            )
            total = total + (pltpu.roll(block, part * FF_BLOCK, 1) if part else block)
        return total

    gate, up = joined(0), joined(FF_PAD)
    gain_ref[...] = jnp.sum(
        wg[...].astype(f32) * gate + wu[...].astype(f32) * up, axis=1, keepdims=True
    )
    gate_ref[...] = gate * g_two[...]
    up_ref[...] = up * g_two[...]
    down_ref[...] = joined(2 * FF_PAD)
    out_ref[...] = jnp.concatenate([out_parts[0], out_parts[1]], 1)


def finish_ffn(parts, out_parts, wg, wu, g_two):
    wide = jax.ShapeDtypeStruct(wg.shape, f32)
    return pl.pallas_call(
        finish_ffn_kernel,
        in_specs=[VMEM] * 5,
        out_specs=(VMEM,) * 5,
        out_shape=(
            wide,
            wide,
            wide,
            jax.ShapeDtypeStruct((32, 2 * OUT), f32),
            jax.ShapeDtypeStruct((32, 1), f32),
        ),
        cost_estimate=pl.CostEstimate(flops=2**20, bytes_accessed=3 * 2**20, transcendentals=0),
        compiler_params=BIG,
        name="finish_ffn",
    )(parts, out_parts, wg, wu, g_two)


def finish_qkv_kernel(parts, wq, wk, wv, g_one, q_ref, k_ref, v_ref, gain_ref):
    joined = lambda first, width: jnp.concatenate(
        [parts[core, :, first : first + width] for core in range(2)], 1
    )
    query, key, value = joined(0, OUT), joined(OUT, HD), joined(OUT + HD, HD)
    total = jnp.sum(wq[...].astype(f32) * query, axis=1, keepdims=True)
    total = total + jnp.sum(
        wk[...].astype(f32) * key + wv[...].astype(f32) * value, axis=1, keepdims=True
    )
    gain_ref[...] = total
    q_ref[...] = query * g_one[...]
    k_ref[...] = key * g_one[...]
    v_ref[...] = value * g_one[...]


def finish_qkv(parts, wq, wk, wv, g_one):
    shapes = [w.shape for w in (wq, wk, wv)] + [(32, 1)]
    return pl.pallas_call(
        finish_qkv_kernel,
        in_specs=[VMEM] * 5,
        out_specs=(VMEM,) * 4,
        out_shape=tuple(jax.ShapeDtypeStruct(shape, f32) for shape in shapes),
        cost_estimate=pl.CostEstimate(flops=2**18, bytes_accessed=2**19, transcendentals=0),
        compiler_params=BIG,
        name="finish_qkv",
    )(parts, wq, wk, wv, g_one)


def qkv_kernel(x0, x1, w_ref, cos_ref, sin_ref, q_ref, kv_ref):
    scale = HD**-0.5 * LOG2E
    for part, x_ref in enumerate((x0, x1)):
        rows = slice(part * 256, part * 256 + 256)
        lin = mm(x_ref[...], w_ref[...], NN)
        cosine, sine = cos_ref[rows], sin_ref[rows]
        for k in range(OUT // 128):
            cols = slice(k * 128, k * 128 + 128)
            q_ref[rows, cols] = (turn(lin[:, cols], cosine, sine) * scale).astype(bf16)
        kv = lin[:, OUT:]
        lane = lax.broadcasted_iota(jnp.int32, kv.shape, 1)
        kv_ref[rows, :] = jnp.where(lane < HD, turn(kv, cosine, sine), kv).astype(bf16)


def qkv_project(xs, w, cosine, sine):
    return pl.pallas_call(
        qkv_kernel,
        in_specs=[VMEM] * 5,
        out_specs=(VMEM, VMEM),
        out_shape=(
            jax.ShapeDtypeStruct((ROWS, OUT), bf16),
            jax.ShapeDtypeStruct((ROWS, 2 * HD), bf16),
        ),
        cost_estimate=pl.CostEstimate(
            flops=2 * ROWS * 2048 * QKV, bytes_accessed=6 * 2**20, transcendentals=0
        ),
        compiler_params=BIG,
        name="qkv_project",
    )(*xs, w, cosine, sine)


def attn_fwd_kernel(
    at_ref, q_ref, kv0, kv1, kv2, kv3, o_ref, ot_ref, lse_ref, q_pad, keys_all, values_t
):
    depth, flip, later = at_ref[0], at_ref[1], at_ref[5]
    for h in range(HEADS):
        q_pad[h, :, :HD] = q_ref[:, h * HD : (h + 1) * HD]
        q_pad[h, :, HD:] = jnp.zeros((ROWS, HD), bf16)
    for b, kv_ref in enumerate((kv0, kv1, kv2, kv3)):

        @pl.when(depth >= b)
        def _():
            keys_all[b] = kv_ref[...]
            values_t[b, :HD] = kv_ref[...].T[HD:]
            values_t[b, HD:] = jnp.ones((16, 2 * ROWS), bf16)

    outs = []
    for first in range(0, HEADS, 4):
        heads = range(first, first + 4)

        def block(b, offset, state, masked):
            keys = keys_all[b, pl.ds(offset, ROWS), :]
            values = values_t[b, :, pl.ds(offset, ROWS)]
            scores = [mm(keys, q_pad[h], NT) for h in heads]
            if masked:
                k_pos = lax.broadcasted_iota(jnp.int32, (ROWS, ROWS), 0) ^ flip
                q_pos = lax.broadcasted_iota(jnp.int32, (ROWS, ROWS), 1) ^ flip
                scores = [jnp.where(k_pos <= q_pos, s, masked_low) for s in scores]
            out = []
            for (top, acc), s in zip(state, scores):
                new_top = jnp.maximum(top, jnp.max(s, axis=0, keepdims=True))
                p = jnp.exp2(s - new_top).astype(bf16)
                acc = acc * jnp.exp2(top - new_top) + mm(values, p, NN)
                out.append((new_top, acc))
            return tuple(out)

        state = tuple(
            (jnp.full((1, ROWS), masked_low, f32), jnp.zeros((HD + 16, ROWS), f32)) for _ in heads
        )
        state = block(0, 0, state, True)
        state = lax.fori_loop(0, later, lambda j, st: block(0, ROWS, st, False), state)
        state = lax.fori_loop(
            0,
            2 * depth,
            lambda j, st: block(1 + j // 2, pl.multiple_of((j % 2) * ROWS, ROWS), st, False),
            state,
        )
        for h, (top, acc) in zip(heads, state):
            total = acc[HD : HD + 1]
            lse_ref[pl.ds(h, 1), :] = top + jnp.log2(total)
            outs.append(acc[:HD] * (1.0 / total))
    o_t = jnp.concatenate(outs, 0)
    ot_ref[...] = o_t
    o_ref[...] = o_t.T.astype(bf16)


def attn_fwd(at, q, kvs):
    return pl.pallas_call(
        attn_fwd_kernel,
        out_shape=(
            jax.ShapeDtypeStruct((ROWS, OUT), bf16),
            jax.ShapeDtypeStruct((OUT, ROWS), f32),
            jax.ShapeDtypeStruct((HEADS, ROWS), f32),
        ),
        in_specs=[SMEM] + [VMEM] * 5,
        out_specs=(VMEM,) * 3,
        scratch_shapes=[
            pltpu.VMEM((HEADS, ROWS, 128), bf16),
            pltpu.VMEM((4, 2 * ROWS, 128), bf16),
            pltpu.VMEM((4, HD + 16, 2 * ROWS), bf16),
        ],
        cost_estimate=pl.CostEstimate(
            flops=25 * 10**9, bytes_accessed=6 * 2**20, transcendentals=12 * 10**6
        ),
        compiler_params=BIG,
        name="attn_fwd",
    )(at, q, *kvs)


def branch_kernel(at_ref, o_ref, w0, w1, w2, w3, keep, send, w_ref):
    for i, piece in enumerate((w0, w1, w2, w3)):
        for j in range(4):
            first = ((at_ref[4] ^ j) * 4 + (at_ref[0] ^ i)) * 128
            w_ref[pl.ds(pl.multiple_of(first, 128), 128), :] = piece[j * 128 : j * 128 + 128]
    send[...] = mm(o_ref[256:], w_ref[...], NT).astype(bf16)
    keep[...] = mm(o_ref[:256], w_ref[...], NT).astype(bf16)


def branch_project(at, o, ws):
    depth = 4 * ws[0].shape[0]
    part = jax.ShapeDtypeStruct((256, depth), bf16)
    return pl.pallas_call(
        branch_kernel,
        in_specs=[SMEM] + [VMEM] * 5,
        out_specs=(VMEM,) * 3,
        out_shape=(part, part, jax.ShapeDtypeStruct((depth, OUT), bf16)),
        cost_estimate=pl.CostEstimate(
            flops=2 * ROWS * depth * OUT, bytes_accessed=6 * 2**20, transcendentals=0
        ),
        compiler_params=BIG,
        name="branch_project",
    )(at, o, *ws)


def attn_bwd_kernel(
    at_ref, q_ref, kv0, kv1, kv2, kv3, do_ref, ot_ref, lse_ref,
    dq_ref, dkv0, dkv1, dkv2, dkv3,
    q_pad, do_pad, keys_all, keys_t, dkv_all, dqt, delta,
):
    depth, flip, later = at_ref[0], at_ref[1], at_ref[5]
    nothing = jnp.zeros((ROWS, HD), bf16)
    do_t = do_ref[...].astype(f32).T
    for h in range(HEADS):
        cols = slice(h * HD, (h + 1) * HD)
        q_pad[h, :, :HD] = q_ref[:, cols]
        q_pad[h, :, HD:] = nothing
        do_pad[h, :, :HD] = nothing
        do_pad[h, :, HD:] = do_ref[:, cols]
        delta[pl.ds(h, 1), :] = jnp.sum(do_t[cols] * ot_ref[cols, :], axis=0, keepdims=True)
    for b, kv_ref in enumerate((kv0, kv1, kv2, kv3)):

        @pl.when(depth >= b)
        def _():
            keys_all[b] = kv_ref[...]
            keys_t[b] = kv_ref[...].T[:HD]

    dqt[...] = jnp.zeros_like(dqt)
    lane = lax.broadcasted_iota(jnp.int32, (1, 128), 1)
    out_scale = jnp.where(lane < HD, 1.0 / LOG2E, 1.0)

    def part(b, first, count, masked):
        at = slice(first, first + count)
        keys, turned = keys_all[b, at, :], keys_t[b, :, at]
        if masked:
            k_pos = lax.broadcasted_iota(jnp.int32, (count, ROWS), 0) ^ flip
            q_pos = lax.broadcasted_iota(jnp.int32, (count, ROWS), 1) ^ flip
            visible = k_pos <= q_pos
        dkv = jnp.zeros((count, 128), f32)
        for h in range(HEADS):
            query, grad = q_pad[h], do_pad[h]
            p = jnp.exp2(mm(keys, query, NT) - lse_ref[pl.ds(h, 1), :])
            if masked:
                p = jnp.where(visible, p, 0.0)
            dp = mm(keys, grad, NT)
            ds = (p * (dp - delta[pl.ds(h, 1), :])).astype(bf16)
            dkv = dkv + mm(p.astype(bf16), grad, NN) + mm(ds, query, NN)
            dqt[h * HD : (h + 1) * HD, :] += mm(turned, ds, NN)
        dkv_all[b, at, :] = (dkv * out_scale).astype(bf16)

    def far(j, _):
        part(1 + j, 0, 2 * ROWS, False)
        return 0

    lax.fori_loop(0, depth, far, 0)
    part(0, 0, ROWS, True)

    @pl.when(later == 1)
    def _():
        part(0, ROWS, ROWS, False)

    @pl.when(later == 0)
    def _():
        dkv_all[0, ROWS:, :] = jnp.zeros((ROWS, 128), bf16)

    dq_ref[...] = dqt[...].T * HD**-0.5
    for b, out_ref in enumerate((dkv0, dkv1, dkv2, dkv3)):
        out_ref[...] = dkv_all[b]


def attn_bwd(at, q, kvs, do, ot, lse):
    block = jax.ShapeDtypeStruct(kvs[0].shape, bf16)
    return pl.pallas_call(
        attn_bwd_kernel,
        out_shape=(jax.ShapeDtypeStruct((ROWS, OUT), f32), block, block, block, block),
        in_specs=[SMEM] + [VMEM] * 8,
        out_specs=(VMEM,) * 5,
        scratch_shapes=[
            pltpu.VMEM((HEADS, ROWS, 128), bf16),
            pltpu.VMEM((HEADS, ROWS, 128), bf16),
            pltpu.VMEM((4, 2 * ROWS, 128), bf16),
            pltpu.VMEM((4, HD, 2 * ROWS), bf16),
            pltpu.VMEM((4, 2 * ROWS, 128), bf16),
            pltpu.VMEM((OUT, ROWS), f32),
            pltpu.VMEM((HEADS, ROWS), f32),
        ],
        cost_estimate=pl.CostEstimate(
            flops=50 * 10**9, bytes_accessed=8 * 2**20, transcendentals=12 * 10**6
        ),
        compiler_params=BIG,
        name="attn_bwd",
    )(at, q, *kvs, do, ot, lse)


def dhid_kernel(*refs):
    w_ref, out_ref = refs[4:]
    for part, cot_ref in enumerate(refs[:4]):
        out_ref[part * 256 : part * 256 + 256, :] = mm(cot_ref[...], w_ref[...], NN)


def dhid_project(cots, w):
    depth = w.shape[0]
    return pl.pallas_call(
        dhid_kernel,
        grid=(1,),
        in_specs=[VMEM] * 4 + [pl.BlockSpec((depth, FF_PAD), lambda i: (0, 2))],
        out_specs=VMEM,
        out_shape=jax.ShapeDtypeStruct((1024, FF_PAD), f32),
        cost_estimate=pl.CostEstimate(
            flops=2 * 1024 * depth * FF_PAD, bytes_accessed=10 * 2**20, transcendentals=0
        ),
        compiler_params=BIG,
        name="dhid_project",
    )(*cots, w)


def ffn_kernel(*refs):
    hns, dhid_ref, w_hbm = refs[:8], refs[8], refs[9]
    hid_ref, dgu_ref = refs[10:12]
    dns = refs[12:16]
    hn_buf, dn_buf, w_ref, w_sems, in_sems, out_sems = refs[16:]
    step = pl.program_id(0)
    parts = [slice(k * FF_PAD, (k + 1) * FF_PAD) for k in range(2)]
    weights = [
        pltpu.make_async_copy(w_hbm.at[:, parts[k]], w_ref.at[:, parts[k]], w_sems.at[k])
        for k in range(2)
    ]

    def fetch(s):
        return [
            pltpu.make_async_copy(
                hns[4 * s + k], hn_buf.at[s, k * 128 : k * 128 + 128], in_sems.at[s, k]
            )
            for k in range(4)
        ]

    def flush(s):
        return [
            pltpu.make_async_copy(
                dn_buf.at[s, k * 256 : k * 256 + 256], dns[2 * s + k], out_sems.at[s, k]
            )
            for k in range(2)
        ]

    def at(s, action, copies):
        @pl.when(step == s)
        def _():
            for copy in copies:
                action(copy)

    start = lambda copy: copy.start()
    wait = lambda copy: copy.wait()
    at(0, start, fetch(0) + weights + fetch(1))
    for s in range(2):
        at(s, wait, fetch(s))
    at(0, wait, weights[:1])
    hn = hn_buf[step]
    gate = mm(hn, w_ref[:, parts[0]], NN)
    at(0, wait, weights[1:])
    up = mm(hn, w_ref[:, parts[1]], NN)
    dhid = dhid_ref[...]
    sg = 1.0 / (1.0 + jnp.exp(-gate))
    act = gate * sg
    hid_ref[...] = (act * up).astype(bf16)
    dgu_ref[:, parts[0]] = (dhid * up * sg * (1.0 + gate * (1.0 - sg))).astype(bf16)
    dgu_ref[:, parts[1]] = (dhid * act).astype(bf16)
    dn_buf[step] = mm(dgu_ref[...], w_ref[...], NT).astype(bf16)
    for s in range(2):
        at(s, start, flush(s))
    at(1, wait, flush(0) + flush(1))


def ffn(hns, dhid, w):
    depth = w.shape[0]
    rowwise = lambda width: pl.BlockSpec((512, width), lambda i: (i, 0))
    hbm = pl.BlockSpec(memory_space=pl.ANY)
    quarter = jax.ShapeDtypeStruct((256, depth), bf16)
    outs = pl.pallas_call(
        ffn_kernel,
        grid=(2,),
        in_specs=[hbm] * 8 + [rowwise(FF_PAD), hbm],
        out_specs=(rowwise(FF_PAD), rowwise(2 * FF_PAD)) + (hbm,) * 4,
        out_shape=(
            jax.ShapeDtypeStruct((1024, FF_PAD), bf16),
            jax.ShapeDtypeStruct((1024, 2 * FF_PAD), bf16),
        )
        + (quarter,) * 4,
        scratch_shapes=[
            pltpu.VMEM((2, 512, depth), bf16),
            pltpu.VMEM((2, 512, depth), bf16),
            pltpu.VMEM((depth, 2 * FF_PAD), bf16),
            pltpu.SemaphoreType.DMA((2,)),
            pltpu.SemaphoreType.DMA((2, 4)),
            pltpu.SemaphoreType.DMA((2, 2)),
        ],
        cost_estimate=pl.CostEstimate(
            flops=8 * 1024 * depth * FF_PAD,
            bytes_accessed=25 * 2**20,
            transcendentals=1024 * FF_PAD,
        ),
        compiler_params=BIG,
        name="ffn",
    )(*hns, dhid, w)
    return outs[0], outs[1], outs[2:]


def ffn_grad_kernel(*refs):
    hn = jnp.concatenate([r[...] for r in refs[:8]], 0)
    cot = jnp.concatenate([r[...] for r in refs[8:12]], 0)
    dgu_ref, hid_ref, w_ref, out_ref = refs[12:16]
    hid = hid_ref[...]
    out_ref[:, : 2 * FF_PAD] = mm(hn, dgu_ref[...], TN).astype(bf16)
    out_ref[:, 2 * FF_PAD :] = mm(cot, hid, TN).astype(bf16)
    for part, y_ref in enumerate(refs[16:]):
        y_ref[...] = mm(hid[part * 256 : part * 256 + 256], w_ref[...], NT).astype(bf16)


def ffn_grad(hns, cots, dgu, hid, w):
    depth = hns[0].shape[1]
    block = 256
    piece = lambda rows: pl.BlockSpec((rows, block), lambda i: (0, i))
    outs = pl.pallas_call(
        ffn_grad_kernel,
        grid=(depth // block,),
        in_specs=[piece(a.shape[0]) for a in hns + cots]
        + [VMEM] * 2
        + [pl.BlockSpec((block, FF_PAD), lambda i: (i, 2))],
        out_specs=(pl.BlockSpec((block, 3 * FF_PAD), lambda i: (i, 0)),) + (piece(256),) * 4,
        out_shape=(jax.ShapeDtypeStruct((depth, REST + OUT), bf16),)
        + (jax.ShapeDtypeStruct((256, depth), bf16),) * 4,
        cost_estimate=pl.CostEstimate(
            flops=8 * 1024 * depth * FF_PAD, bytes_accessed=30 * 2**20, transcendentals=0
        ),
        compiler_params=BIG,
        name="ffn_grad",
    )(*hns, *cots, dgu, hid, w)
    return outs[0], outs[1:]


def dh_kernel(p0, p1, p2, p3, w_ref, ob_ref, _, do_ref, grads_hbm, part, sem):
    for k in range(4):
        cols = slice(k * 512, k * 512 + 512)
        dh = jnp.concatenate([r[:, cols] for r in (p0, p1, p2, p3)], 0)
        part[cols, :] = mm(dh, ob_ref[...], TN).astype(bf16)
    copy = pltpu.make_async_copy(part, grads_hbm.at[:, REST:], sem)
    copy.start()
    for k, pieces in enumerate(((p0, p1), (p2, p3))):
        dh = jnp.concatenate([r[...] for r in pieces], 0)
        do_ref[k * 256 : k * 256 + 256, :] = mm(dh, w_ref[...], NN).astype(bf16)
    copy.wait()


def dh_project(pieces, w, ob, grads):
    depth = w.shape[0]
    hbm = pl.BlockSpec(memory_space=pl.ANY)
    return pl.pallas_call(
        dh_kernel,
        in_specs=[VMEM] * 6 + [hbm],
        out_specs=(VMEM, hbm),
        out_shape=(
            jax.ShapeDtypeStruct((ROWS, OUT), bf16),
            jax.ShapeDtypeStruct(grads.shape, bf16),
        ),
        scratch_shapes=[pltpu.VMEM((depth, OUT), bf16), pltpu.SemaphoreType.DMA(())],
        input_output_aliases={6: 1},
        cost_estimate=pl.CostEstimate(
            flops=4 * ROWS * depth * OUT, bytes_accessed=8 * 2**20, transcendentals=0
        ),
        compiler_params=BIG,
        name="dh_project",
    )(*pieces, w, ob, grads)


def dq_kernel(dq_ref, cos_ref, sin_ref, x0, x1, dqr_ref, grad_ref):
    @pl.when(pl.program_id(0) == 0)
    def _():
        cosine, sine = cos_ref[...], -sin_ref[...]
        for part in range(OUT // 128):
            cols = slice(part * 128, part * 128 + 128)
            dqr_ref[:, cols] = turn(dq_ref[:, cols], cosine, sine).astype(bf16)

    xh = jnp.concatenate([x0[...], x1[...]], 0)
    grad_ref[...] = mm(xh, dqr_ref[...], TN).astype(bf16)


def dq_project(dq, cosine, sine, xs):
    depth = xs[0].shape[1]
    block = 512
    return pl.pallas_call(
        dq_kernel,
        grid=(depth // block,),
        in_specs=[VMEM] * 3 + [pl.BlockSpec((256, block), lambda i: (0, i))] * 2,
        out_specs=(VMEM, pl.BlockSpec((block, OUT), lambda i: (i, 0))),
        out_shape=(
            jax.ShapeDtypeStruct((ROWS, OUT), bf16),
            jax.ShapeDtypeStruct((depth, OUT), bf16),
        ),
        cost_estimate=pl.CostEstimate(
            flops=2 * ROWS * depth * OUT, bytes_accessed=8 * 2**20, transcendentals=0
        ),
        compiler_params=BIG,
        name="dq_project",
    )(dq, cosine, sine, *xs)


def kv_grad_kernel(x0, x1, dkv_ref, out_ref):
    xh = jnp.concatenate([x0[...], x1[...]], 0)
    out_ref[...] = mm(xh, dkv_ref[...], TN).astype(bf16)


def kv_grad(xs, dkv):
    depth = xs[0].shape[1]
    block = 512
    return pl.pallas_call(
        kv_grad_kernel,
        grid=(depth // block,),
        in_specs=[pl.BlockSpec((256, block), lambda i: (0, i))] * 2 + [VMEM],
        out_specs=pl.BlockSpec((block, 2 * HD), lambda i: (i, 0)),
        out_shape=jax.ShapeDtypeStruct((depth, 2 * HD), bf16),
        cost_estimate=pl.CostEstimate(
            flops=4 * ROWS * depth * HD, bytes_accessed=6 * 2**20, transcendentals=0
        ),
        compiler_params=BIG,
        name="kv_grad",
    )(*xs, dkv)


def dqkv_kernel(dqr_ref, dkv_ref, other_ref, w_ref, cos_ref, sin_ref, dkvr_ref, send, keep):
    dkv = dkv_ref[...] + other_ref[...].astype(f32)
    lane = lax.broadcasted_iota(jnp.int32, dkv.shape, 1)
    dkvr = jnp.where(lane < HD, turn(dkv, cos_ref[...], -sin_ref[...]), dkv).astype(bf16)
    dkvr_ref[...] = dkvr
    dn = mm(jnp.concatenate([dqr_ref[...], dkvr], 1), w_ref[...], NT).astype(bf16)
    for step, out_ref in enumerate((send, keep)):

        @pl.when(pl.program_id(0) == step)
        def _():
            out_ref[...] = dn


def dqkv_project(dqr, dkv, other, w, cosine, sine):
    depth = w.shape[0]
    rowwise = lambda width: pl.BlockSpec((256, width), lambda i: (1 - i, 0))
    whole = pl.BlockSpec((256, depth), lambda i: (0, 0))
    return pl.pallas_call(
        dqkv_kernel,
        grid=(2,),
        in_specs=[rowwise(OUT), rowwise(128), rowwise(128), VMEM, rowwise(128), rowwise(128)],
        out_specs=(rowwise(128), whole, whole),
        out_shape=(jax.ShapeDtypeStruct((ROWS, 2 * HD), bf16),)
        + (jax.ShapeDtypeStruct((256, depth), bf16),) * 2,
        cost_estimate=pl.CostEstimate(
            flops=2 * ROWS * depth * QKV, bytes_accessed=10 * 2**20, transcendentals=0
        ),
        compiler_params=BIG,
        name="dqkv_project",
    )(dqr, dkv, other, w, cosine, sine)


def swap(value, axes):
    count = 2 ** len(axes)
    return lax.ppermute(value, axes, [(i, count - 1 - i) for i in range(count)])


def crossed(value, axis, mask):
    return lax.ppermute(value, axis, [(i, i ^ mask) for i in range(4)])


def shifted(value, steps):
    first, last = max(0, -steps), min(4, 4 - steps)
    return lax.ppermute(value, "z", [(i, i + steps) for i in range(first, last)])


def gather_chips(own):
    return swap(own, ("yl",)), swap(own, ("yh", "yl")), swap(own, ("yh",))


def gather_cores(own, by_l):
    return [own, by_l, swap(own, ("c",)), swap(by_l, ("c",))]


def sum_cores(keep, send):
    return keep.astype(f32) + swap(send, ("c",)).astype(f32)


def from_chip(total):
    return swap(total[128:].astype(bf16), ("yl",))


def from_chips(near, far):
    far = far.astype(bf16)
    return from_chip(near), swap(far[128:], ("yh", "yl")), swap(far[:128], ("yh",))


def sum_chips(near, *received):
    return near[:128] + sum(part.astype(f32) for part in received)


def pick(parts, index):
    return lax.dynamic_index_in_dim(parts, index, 0, False)


def in_order(which, mine, got, axis=0):
    return jnp.where(which == 0, jnp.stack([mine, got], axis), jnp.stack([got, mine], axis))


def trade_cores(parts, core):
    parts = jnp.moveaxis(parts, -3, 0)
    return in_order(core, pick(parts, core), swap(pick(parts, 1 - core), ("c",)), -3)


def both_halves(own, other, yl):
    return jnp.where(yl == 0, jnp.concatenate([own, other], 0), jnp.concatenate([other, own], 0))


def on_device(
    tokens, w_query, w_key, w_value, w_output, w_gate, w_up, w_down, norm_attn, norm_ffn, cotangent
):
    together = lax.optimization_barrier
    z, yh = lax.axis_index("z"), lax.axis_index("yh")
    core, yl = lax.axis_index("c"), lax.axis_index("yl")
    gain_one = norm_attn.astype(f32)[:, None]
    gain_two = norm_ffn.astype(f32)[:, None]
    flip = (core * 2 + yl) * 128
    at = jnp.stack([z, flip, core, yl, lax.axis_index("x"), yh]).astype(jnp.int32)

    xh, inverse_one, cot_here = order(at, tokens[0], cotangent[0])
    inputs = lax.dynamic_slice_in_dim(tokens[0], yl * 128, 128, 0).astype(f32)

    xhs = [xh, swap(xh, ("c",))]
    copies, rest, out_rows = prepare(
        w_query, w_key, w_value, w_output.T, w_gate, w_up, w_down.T, gain_one, gain_two
    )

    w_qkv = lax.all_to_all(copies, ALL, 0, 0).reshape(2048, QKV)
    out_rows = trade_cores(out_rows, core).reshape(64, OUT)
    out_rows = in_order(yh, out_rows, swap(out_rows, ("yh",))).reshape(128, OUT)
    rest = trade_cores(rest.reshape(2, 2, 32, REST), core)

    positions = ((z * 2 + yh) * ROWS + (jnp.arange(ROWS, dtype=jnp.int32) ^ flip)).astype(f32)
    freqs = rope_base ** (-2.0 * jnp.arange(HD // 2, dtype=f32) / HD)
    angles = positions[:, None] * freqs[None, :]
    cosine, sine = jnp.cos(angles), jnp.sin(angles)
    cosine = jnp.concatenate([cosine] * 4, -1)
    sine = jnp.concatenate([-sine, sine, -sine, sine], -1)

    w_qkv, cosine, sine, rest, out_rows, xhs = together(
        (w_qkv, cosine, sine, rest, out_rows, xhs)
    )

    q, kv = qkv_project(xhs, w_qkv, cosine, sine)
    kv, out_rows = together((kv, out_rows))
    kv_other = swap(kv, ("yh",))
    rest = in_order(yh, pick(rest, yh), swap(pick(rest, 1 - yh), ("yh",))).reshape(128, REST)
    ws = jnp.concatenate([out_rows] + [crossed(out_rows, "x", mask) for mask in (1, 2, 3)], 0)
    kv = jnp.concatenate([kv, kv_other], 0)
    kvs = [kv] + [shifted(kv, by) for by in (1, 2, 3)]
    kvs, ws, cot_here, rest = together((kvs, ws, cot_here, rest))
    w_ffn = lax.all_gather(rest, ("x", "z"), axis=0, tiled=True)
    ws = [ws] + [crossed(ws, "z", mask) for mask in (1, 2, 3)]
    cot_c, cot_h = swap(cot_here, ("c",)), swap(cot_here, ("yh",))
    ob, o_t, lse = attn_fwd(at, q, kvs)
    ob, ws, cot_h = together((ob, ws, cot_h))
    cots = [cot_here, cot_c, cot_h, swap(cot_h, ("c",))]
    keep, send, w_out = branch_project(at, ob, ws)
    total = sum_cores(keep, send)
    middle = inputs + sum_chips(total, from_chip(total))
    inverse_two = lax.rsqrt(jnp.mean(middle * middle, axis=-1, keepdims=True) + epsilon)
    hn = (middle * inverse_two).astype(bf16)

    received = gather_chips(hn)
    dhid = dhid_project(cots, w_ffn)
    (by_l, by_d, by_h), dhid = together((received, dhid))
    hns = gather_cores(hn, by_l) + [by_h, by_d, swap(by_h, ("c",)), swap(by_d, ("c",))]
    hid, dgu, dns = ffn(hns, dhid, w_ffn)
    near, far = sum_cores(*dns[:2]), sum_cores(*dns[2:])
    received = from_chips(near, far)
    grads, ys = ffn_grad(hns, cots, dgu, hid, w_ffn)
    received, grads = together((received, grads))
    dn2 = sum_chips(near, *received)
    dh = (
        cots[0][:128].astype(f32)
        + inverse_two * dn2
        - middle * inverse_two**3 * jnp.mean(dn2 * middle, axis=-1, keepdims=True)
    )
    dh_low, ys = together((dh.astype(bf16), ys))
    by_l, y_near, y_far = swap(dh_low, ("yl",)), sum_cores(*ys[:2]), sum_cores(*ys[2:])
    by_l, y_near, y_far = together((by_l, y_near, y_far))
    dhs = gather_cores(dh_low, by_l)

    do, grads = dh_project(dhs, w_out, ob, grads)
    grads = lax.psum_scatter(grads, ("x", "z"), scatter_dimension=0, tiled=True)
    do, y_near, y_far = together((do, y_near, y_far))
    received = from_chips(y_near, y_far)
    dq, *dkvs = attn_bwd(at, q, kvs, do, o_t, lse)
    received, dkvs = together((received, dkvs))
    block_out = (middle + sum_chips(y_near, *received)).astype(bf16)
    block_out, dkvs, dq = together((block_out, dkvs, dq))
    block_other = swap(block_out, ("yl",))
    dkvs = dkvs[:1] + [shifted(dkvs[by], -by) for by in (1, 2, 3)]

    def to_owners(grad, axis):
        parts = grad.reshape(4, grad.shape[0] // 4, -1)
        mine = lax.axis_index(axis)
        return [pick(parts, mine)] + [crossed(pick(parts, mine ^ m), axis, m) for m in (1, 2, 3)]

    added = lambda parts: sum(part.astype(f32) for part in parts).astype(bf16)
    dqr, grad_q = dq_project(dq, cosine, sine, xhs)
    grad_q = lax.all_to_all(grad_q.reshape(4, ROWS, OUT), "x", 0, 0)
    dkvs, block_other, dqr = together((dkvs, block_other, dqr))
    block_out = both_halves(block_out, block_other, yl)
    dkv = sum(part.astype(f32) for part in dkvs)
    other, grad_q = together((swap(dkv[ROWS:].astype(bf16), ("yh",)), grad_q))
    dkvr, send, keep = dqkv_project(dqr, dkv[:ROWS], other, w_qkv, cosine, sine)
    total, dkvr, grad_q = together((sum_cores(keep, send), dkvr, added(grad_q)))
    received, grad_kv, grad_q = together(
        (from_chip(total), kv_grad(xhs, dkvr), to_owners(grad_q, "z"))
    )
    grad_kv = lax.all_to_all(grad_kv.reshape(16, 128, 2 * HD), ("x", "z"), 0, 0)
    dn1 = sum_chips(total, received)
    input_grad = (
        dh
        + inverse_one * dn1
        - inputs * inverse_one**3 * jnp.mean(dn1 * inputs, axis=-1, keepdims=True)
    )
    other, grad_kv = together((swap(input_grad.astype(bf16), ("yl",)), grad_kv))
    input_grad = both_halves(input_grad, other.astype(f32), yl)
    grad_kv = jnp.sum(grad_kv.astype(f32), 0).astype(bf16)
    grads = jnp.concatenate([grads, added(grad_q), grad_kv], -1)
    grads = trade_cores(grads.reshape(2, 2, 32, REST + OUT + QKV), core)
    mine, got = pick(grads, yh), swap(pick(grads, 1 - yh), ("yh",))
    attn_grads = mine[..., REST:].astype(f32) + got[..., REST:].astype(f32)
    grad_qkv = attn_grads[..., OUT:]
    grad_gate, grad_up, grad_down, grad_out, gain_grad_two = finish_ffn(
        in_order(yh, mine[..., :REST], got[..., :REST]).reshape(4, 32, REST),
        attn_grads[..., :OUT],
        w_gate,
        w_up,
        gain_two,
    )
    grad_query, grad_key, grad_value, gain_grad_one = finish_qkv(
        grad_qkv, w_query, w_key, w_value, gain_one
    )
    gain_grad_one = gain_grad_one + swap(gain_grad_one, ("yl",))
    gain_grad_two = gain_grad_two + swap(gain_grad_two, ("yl",))
    return (
        block_out[None],
        input_grad[None],
        grad_query,
        grad_key,
        grad_value,
        grad_out.T,
        grad_gate,
        grad_up,
        grad_down.T,
        gain_grad_one[:, 0],
        gain_grad_two[:, 0],
    )


def solution(mesh):
    mesh = Mesh(mesh.devices.reshape(4, 4, 2, 2, 2), ("x", "z", "yh", "c", "yl"))
    ctx = ("z", "yh", "c")
    rows, cols = P(ALL, "yl"), P("yl", ALL)
    seq = P("x", ctx, None)
    vec = P(ALL)
    in_specs = (seq, rows, rows, rows, cols, rows, rows, cols, vec, vec, seq)
    out_specs = (seq, seq, rows, rows, rows, cols, rows, rows, cols, vec, vec)
    return jax.shard_map(
        on_device, mesh=mesh, in_specs=in_specs, out_specs=out_specs, check_vma=False
    )
```

```python
import functools

import jax
import jax.numpy as jnp
from jax import lax
from jax.experimental import pallas as pl
from jax.experimental.pallas import tpu as pltpu
from jax.sharding import Mesh, PartitionSpec as P

HD = 64
HEADS = 8
FF_BLOCK = 704
FF_PAD = 768
OUT = HEADS * HD
QKV = OUT + 2 * HD
REST = 3 * FF_PAD
ROWS = 512
LOG2E = 1.4426950408889634
epsilon = 1e-05
rope_base = 10000.0
masked_low = -1e30
f32 = jnp.float32
bf16 = jnp.bfloat16

ALL = ("x", "z", "yh", "c")

NN = (((1,), (0,)), ((), ()))
NT = (((1,), (1,)), ((), ()))
TN = (((0,), (0,)), ((), ()))

VMEM = pl.BlockSpec(memory_space=pltpu.VMEM)
SMEM = pl.BlockSpec(memory_space=pltpu.SMEM)
BIG = pltpu.CompilerParams(vmem_limit_bytes=56 * 2**20)


def mm(a, b, dims):
    return lax.dot_general(a, b, dims, preferred_element_type=f32)


def turn(u, cosine, sine_signed):
    width = u.shape[-1]
    lane = lax.broadcasted_iota(jnp.int32, u.shape, 1)
    turned = jnp.where(
        lane % HD < HD // 2, pltpu.roll(u, width - HD // 2, 1), pltpu.roll(u, HD // 2, 1)
    )
    return u * cosine + turned * sine_signed


def order_kernel(at_ref, x_ref, cot_ref, xh_ref, inv_ref, cot_out):
    for half in range(2):
        first = pl.multiple_of((at_ref[3] ^ half) * 128, 128)
        rows = slice(half * 128, half * 128 + 128)
        x = x_ref[pl.ds(first, 128), :].astype(f32)
        inverse = lax.rsqrt(jnp.mean(x * x, axis=-1, keepdims=True) + epsilon)
        xh_ref[rows, :] = (x * inverse).astype(bf16)
        cot_out[rows, :] = cot_ref[pl.ds(first, 128), :]
        if half == 0:
            inv_ref[...] = inverse


def order(at, x, cot):
    low = jax.ShapeDtypeStruct(x.shape, bf16)
    return pl.pallas_call(
        order_kernel,
        in_specs=[SMEM, VMEM, VMEM],
        out_specs=(VMEM,) * 3,
        out_shape=(low, jax.ShapeDtypeStruct((128, 1), f32), low),
        cost_estimate=pl.CostEstimate(flops=2**20, bytes_accessed=4 * 2**20, transcendentals=0),
        compiler_params=BIG,
        name="order",
    )(at, x, cot)


def prepare_kernel(wq, wk, wv, wo_t, wg, wu, wd_t, g_one, g_two, qkv_ref, rest_ref, out_ref):
    g_one, g_two = g_one[...], g_two[...]
    scaled = lambda ref, gain: (ref[...].astype(f32) * gain).astype(bf16)
    query, key, value = scaled(wq, g_one), scaled(wk, g_one), scaled(wv, g_one)
    for core in range(2):
        head = slice(core * HD, core * HD + HD)
        rows = jnp.concatenate([query[:, core * OUT : core * OUT + OUT], key[:, head], value[:, head]], 1)
        for copy in range(32):
            qkv_ref[copy * 2 + core] = rows
        out_ref[core] = wo_t[:, core * OUT : core * OUT + OUT]
    lane = lax.broadcasted_iota(jnp.int32, (32, FF_PAD), 1)
    for k, (ref, gain) in enumerate(((wg, g_two), (wu, g_two), (wd_t, None))):
        w = ref[...].astype(f32)
        w = w if gain is None else w * gain
        for part in range(4):
            shift = (w.shape[1] - part * FF_BLOCK) % w.shape[1]
            block = pltpu.roll(w, shift, 1)[:, :FF_PAD] if shift else w[:, :FF_PAD]
            block = jnp.where(lane < FF_BLOCK, block, 0.0)
            rest_ref[part, :, k * FF_PAD : (k + 1) * FF_PAD] = block.astype(bf16)


def prepare(*args):
    return pl.pallas_call(
        prepare_kernel,
        in_specs=[VMEM] * 9,
        out_specs=(VMEM,) * 3,
        out_shape=(
            jax.ShapeDtypeStruct((64, 32, QKV), bf16),
            jax.ShapeDtypeStruct((4, 32, REST), bf16),
            jax.ShapeDtypeStruct((2, 32, OUT), bf16),
        ),
        cost_estimate=pl.CostEstimate(flops=2**20, bytes_accessed=3 * 2**20, transcendentals=0),
        compiler_params=BIG,
        name="prepare",
    )(*args)


def finish_ffn_kernel(parts, out_parts, wg, wu, g_two, gate_ref, up_ref, down_ref, out_ref, gain_ref):
    def joined(first):
        total = jnp.zeros(gate_ref.shape, f32)
        for part in range(4):
            block = parts[part, :, first : first + FF_PAD].astype(f32)
            block = jnp.concatenate(
                [block, jnp.zeros((32, total.shape[1] - FF_PAD), f32)], 1
            )
            total = total + (pltpu.roll(block, part * FF_BLOCK, 1) if part else block)
        return total

    gate, up = joined(0), joined(FF_PAD)
    gain_ref[...] = jnp.sum(
        wg[...].astype(f32) * gate + wu[...].astype(f32) * up, axis=1, keepdims=True
    )
    gate_ref[...] = gate * g_two[...]
    up_ref[...] = up * g_two[...]
    down_ref[...] = joined(2 * FF_PAD)
    out_ref[...] = jnp.concatenate([out_parts[0], out_parts[1]], 1)


def finish_ffn(parts, out_parts, wg, wu, g_two):
    wide = jax.ShapeDtypeStruct(wg.shape, f32)
    return pl.pallas_call(
        finish_ffn_kernel,
        in_specs=[VMEM] * 5,
        out_specs=(VMEM,) * 5,
        out_shape=(
            wide,
            wide,
            wide,
            jax.ShapeDtypeStruct((32, 2 * OUT), f32),
            jax.ShapeDtypeStruct((32, 1), f32),
        ),
        cost_estimate=pl.CostEstimate(flops=2**20, bytes_accessed=3 * 2**20, transcendentals=0),
        compiler_params=BIG,
        name="finish_ffn",
    )(parts, out_parts, wg, wu, g_two)


def finish_qkv_kernel(parts, wq, wk, wv, g_one, q_ref, k_ref, v_ref, gain_ref):
    joined = lambda first, width: jnp.concatenate(
        [parts[core, :, first : first + width] for core in range(2)], 1
    )
    query, key, value = joined(0, OUT), joined(OUT, HD), joined(OUT + HD, HD)
    total = jnp.sum(wq[...].astype(f32) * query, axis=1, keepdims=True)
    total = total + jnp.sum(
        wk[...].astype(f32) * key + wv[...].astype(f32) * value, axis=1, keepdims=True
    )
    gain_ref[...] = total
    q_ref[...] = query * g_one[...]
    k_ref[...] = key * g_one[...]
    v_ref[...] = value * g_one[...]


def finish_qkv(parts, wq, wk, wv, g_one):
    shapes = [w.shape for w in (wq, wk, wv)] + [(32, 1)]
    return pl.pallas_call(
        finish_qkv_kernel,
        in_specs=[VMEM] * 5,
        out_specs=(VMEM,) * 4,
        out_shape=tuple(jax.ShapeDtypeStruct(shape, f32) for shape in shapes),
        cost_estimate=pl.CostEstimate(flops=2**18, bytes_accessed=2**19, transcendentals=0),
        compiler_params=BIG,
        name="finish_qkv",
    )(parts, wq, wk, wv, g_one)


def qkv_kernel(x0, x1, w_ref, cos_ref, sin_ref, q_ref, kv_ref):
    scale = HD**-0.5 * LOG2E
    for part, x_ref in enumerate((x0, x1)):
        rows = slice(part * 256, part * 256 + 256)
        lin = mm(x_ref[...], w_ref[...], NN)
        cosine, sine = cos_ref[rows], sin_ref[rows]
        for k in range(OUT // 128):
            cols = slice(k * 128, k * 128 + 128)
            q_ref[rows, cols] = (turn(lin[:, cols], cosine, sine) * scale).astype(bf16)
        kv = lin[:, OUT:]
        lane = lax.broadcasted_iota(jnp.int32, kv.shape, 1)
        kv_ref[rows, :] = jnp.where(lane < HD, turn(kv, cosine, sine), kv).astype(bf16)


def qkv_project(xs, w, cosine, sine):
    return pl.pallas_call(
        qkv_kernel,
        in_specs=[VMEM] * 5,
        out_specs=(VMEM, VMEM),
        out_shape=(
            jax.ShapeDtypeStruct((ROWS, OUT), bf16),
            jax.ShapeDtypeStruct((ROWS, 2 * HD), bf16),
        ),
        cost_estimate=pl.CostEstimate(
            flops=2 * ROWS * 2048 * QKV, bytes_accessed=6 * 2**20, transcendentals=0
        ),
        compiler_params=BIG,
        name="qkv_project",
    )(*xs, w, cosine, sine)


def attn_fwd_kernel(
    at_ref, q_ref, kv0, kv1, kv2, kv3, o_ref, ot_ref, lse_ref, q_pad, keys_all, values_t
):
    depth, flip, later = at_ref[0], at_ref[1], at_ref[5]
    for h in range(HEADS):
        q_pad[h, :, :HD] = q_ref[:, h * HD : (h + 1) * HD]
        q_pad[h, :, HD:] = jnp.zeros((ROWS, HD), bf16)
    for b, kv_ref in enumerate((kv0, kv1, kv2, kv3)):

        @pl.when(depth >= b)
        def _():
            keys_all[b] = kv_ref[...]
            values_t[b, :HD] = kv_ref[...].T[HD:]
            values_t[b, HD:] = jnp.ones((16, 2 * ROWS), bf16)

    outs = []
    for first in range(0, HEADS, 4):
        heads = range(first, first + 4)

        def block(b, offset, state, masked):
            keys = keys_all[b, pl.ds(offset, ROWS), :]
            values = values_t[b, :, pl.ds(offset, ROWS)]
            scores = [mm(keys, q_pad[h], NT) for h in heads]
            if masked:
                k_pos = lax.broadcasted_iota(jnp.int32, (ROWS, ROWS), 0) ^ flip
                q_pos = lax.broadcasted_iota(jnp.int32, (ROWS, ROWS), 1) ^ flip
                scores = [jnp.where(k_pos <= q_pos, s, masked_low) for s in scores]
            out = []
            for (top, acc), s in zip(state, scores):
                new_top = jnp.maximum(top, jnp.max(s, axis=0, keepdims=True))
                p = jnp.exp2(s - new_top).astype(bf16)
                acc = acc * jnp.exp2(top - new_top) + mm(values, p, NN)
                out.append((new_top, acc))
            return tuple(out)

        state = tuple(
            (jnp.full((1, ROWS), masked_low, f32), jnp.zeros((HD + 16, ROWS), f32)) for _ in heads
        )
        state = block(0, 0, state, True)
        state = lax.fori_loop(0, later, lambda j, st: block(0, ROWS, st, False), state)
        state = lax.fori_loop(
            0,
            2 * depth,
            lambda j, st: block(1 + j // 2, pl.multiple_of((j % 2) * ROWS, ROWS), st, False),
            state,
        )
        for h, (top, acc) in zip(heads, state):
            total = acc[HD : HD + 1]
            lse_ref[pl.ds(h, 1), :] = top + jnp.log2(total)
            outs.append(acc[:HD] * (1.0 / total))
    o_t = jnp.concatenate(outs, 0)
    ot_ref[...] = o_t
    o_ref[...] = o_t.T.astype(bf16)


def attn_fwd(at, q, kvs):
    return pl.pallas_call(
        attn_fwd_kernel,
        out_shape=(
            jax.ShapeDtypeStruct((ROWS, OUT), bf16),
            jax.ShapeDtypeStruct((OUT, ROWS), f32),
            jax.ShapeDtypeStruct((HEADS, ROWS), f32),
        ),
        in_specs=[SMEM] + [VMEM] * 5,
        out_specs=(VMEM,) * 3,
        scratch_shapes=[
            pltpu.VMEM((HEADS, ROWS, 128), bf16),
            pltpu.VMEM((4, 2 * ROWS, 128), bf16),
            pltpu.VMEM((4, HD + 16, 2 * ROWS), bf16),
        ],
        cost_estimate=pl.CostEstimate(
            flops=25 * 10**9, bytes_accessed=6 * 2**20, transcendentals=12 * 10**6
        ),
        compiler_params=BIG,
        name="attn_fwd",
    )(at, q, *kvs)


def branch_kernel(at_ref, o_ref, w0, w1, w2, w3, keep, send, w_ref):
    for i, piece in enumerate((w0, w1, w2, w3)):
        for j in range(4):
            first = ((at_ref[4] ^ j) * 4 + (at_ref[0] ^ i)) * 128
            w_ref[pl.ds(pl.multiple_of(first, 128), 128), :] = piece[j * 128 : j * 128 + 128]
    send[...] = mm(o_ref[256:], w_ref[...], NT).astype(bf16)
    keep[...] = mm(o_ref[:256], w_ref[...], NT).astype(bf16)


def branch_project(at, o, ws):
    depth = 4 * ws[0].shape[0]
    part = jax.ShapeDtypeStruct((256, depth), bf16)
    return pl.pallas_call(
        branch_kernel,
        in_specs=[SMEM] + [VMEM] * 5,
        out_specs=(VMEM,) * 3,
        out_shape=(part, part, jax.ShapeDtypeStruct((depth, OUT), bf16)),
        cost_estimate=pl.CostEstimate(
            flops=2 * ROWS * depth * OUT, bytes_accessed=6 * 2**20, transcendentals=0
        ),
        compiler_params=BIG,
        name="branch_project",
    )(at, o, *ws)


def attn_bwd_kernel(
    at_ref, q_ref, kv0, kv1, kv2, kv3, do_ref, ot_ref, lse_ref,
    dq_ref, dkv0, dkv1, dkv2, dkv3,
    q_pad, do_pad, keys_all, keys_t, dkv_all, dqt, delta,
):
    depth, flip, later = at_ref[0], at_ref[1], at_ref[5]
    nothing = jnp.zeros((ROWS, HD), bf16)
    do_t = do_ref[...].astype(f32).T
    for h in range(HEADS):
        cols = slice(h * HD, (h + 1) * HD)
        q_pad[h, :, :HD] = q_ref[:, cols]
        q_pad[h, :, HD:] = nothing
        do_pad[h, :, :HD] = nothing
        do_pad[h, :, HD:] = do_ref[:, cols]
        delta[pl.ds(h, 1), :] = jnp.sum(do_t[cols] * ot_ref[cols, :], axis=0, keepdims=True)
    for b, kv_ref in enumerate((kv0, kv1, kv2, kv3)):

        @pl.when(depth >= b)
        def _():
            keys_all[b] = kv_ref[...]
            keys_t[b] = kv_ref[...].T[:HD]

    dqt[...] = jnp.zeros_like(dqt)
    lane = lax.broadcasted_iota(jnp.int32, (1, 128), 1)
    out_scale = jnp.where(lane < HD, 1.0 / LOG2E, 1.0)

    def part(b, first, count, masked):
        at = slice(first, first + count)
        keys, turned = keys_all[b, at, :], keys_t[b, :, at]
        if masked:
            k_pos = lax.broadcasted_iota(jnp.int32, (count, ROWS), 0) ^ flip
            q_pos = lax.broadcasted_iota(jnp.int32, (count, ROWS), 1) ^ flip
            visible = k_pos <= q_pos
        dkv = jnp.zeros((count, 128), f32)
        for h in range(HEADS):
            query, grad = q_pad[h], do_pad[h]
            p = jnp.exp2(mm(keys, query, NT) - lse_ref[pl.ds(h, 1), :])
            if masked:
                p = jnp.where(visible, p, 0.0)
            dp = mm(keys, grad, NT)
            ds = (p * (dp - delta[pl.ds(h, 1), :])).astype(bf16)
            dkv = dkv + mm(p.astype(bf16), grad, NN) + mm(ds, query, NN)
            dqt[h * HD : (h + 1) * HD, :] += mm(turned, ds, NN)
        dkv_all[b, at, :] = (dkv * out_scale).astype(bf16)

    def far(j, _):
        part(1 + j, 0, 2 * ROWS, False)
        return 0

    lax.fori_loop(0, depth, far, 0)
    part(0, 0, ROWS, True)

    @pl.when(later == 1)
    def _():
        part(0, ROWS, ROWS, False)

    @pl.when(later == 0)
    def _():
        dkv_all[0, ROWS:, :] = jnp.zeros((ROWS, 128), bf16)

    dq_ref[...] = dqt[...].T * HD**-0.5
    for b, out_ref in enumerate((dkv0, dkv1, dkv2, dkv3)):
        out_ref[...] = dkv_all[b]


def attn_bwd(at, q, kvs, do, ot, lse):
    block = jax.ShapeDtypeStruct(kvs[0].shape, bf16)
    return pl.pallas_call(
        attn_bwd_kernel,
        out_shape=(jax.ShapeDtypeStruct((ROWS, OUT), f32), block, block, block, block),
        in_specs=[SMEM] + [VMEM] * 8,
        out_specs=(VMEM,) * 5,
        scratch_shapes=[
            pltpu.VMEM((HEADS, ROWS, 128), bf16),
            pltpu.VMEM((HEADS, ROWS, 128), bf16),
            pltpu.VMEM((4, 2 * ROWS, 128), bf16),
            pltpu.VMEM((4, HD, 2 * ROWS), bf16),
            pltpu.VMEM((4, 2 * ROWS, 128), bf16),
            pltpu.VMEM((OUT, ROWS), f32),
            pltpu.VMEM((HEADS, ROWS), f32),
        ],
        cost_estimate=pl.CostEstimate(
            flops=50 * 10**9, bytes_accessed=8 * 2**20, transcendentals=12 * 10**6
        ),
        compiler_params=BIG,
        name="attn_bwd",
    )(at, q, *kvs, do, ot, lse)


def dhid_kernel(*refs):
    w_ref, out_ref = refs[4:]
    for part, cot_ref in enumerate(refs[:4]):
        out_ref[part * 256 : part * 256 + 256, :] = mm(cot_ref[...], w_ref[...], NN)


def dhid_project(cots, w):
    depth = w.shape[0]
    return pl.pallas_call(
        dhid_kernel,
        grid=(1,),
        in_specs=[VMEM] * 4 + [pl.BlockSpec((depth, FF_PAD), lambda i: (0, 2))],
        out_specs=VMEM,
        out_shape=jax.ShapeDtypeStruct((1024, FF_PAD), f32),
        cost_estimate=pl.CostEstimate(
            flops=2 * 1024 * depth * FF_PAD, bytes_accessed=10 * 2**20, transcendentals=0
        ),
        compiler_params=BIG,
        name="dhid_project",
    )(*cots, w)


def ffn_kernel(*refs):
    hns, dhid_ref, w_hbm = refs[:8], refs[8], refs[9]
    hid_ref, dgu_ref = refs[10:12]
    dns = refs[12:16]
    hn_buf, dn_buf, w_ref, w_sems, in_sems, out_sems = refs[16:]
    step = pl.program_id(0)
    parts = [slice(k * FF_PAD, (k + 1) * FF_PAD) for k in range(2)]
    weights = [
        pltpu.make_async_copy(w_hbm.at[:, parts[k]], w_ref.at[:, parts[k]], w_sems.at[k])
        for k in range(2)
    ]

    def fetch(s):
        return [
            pltpu.make_async_copy(
                hns[4 * s + k], hn_buf.at[s, k * 128 : k * 128 + 128], in_sems.at[s, k]
            )
            for k in range(4)
        ]

    def flush(s):
        return [
            pltpu.make_async_copy(
                dn_buf.at[s, k * 256 : k * 256 + 256], dns[2 * s + k], out_sems.at[s, k]
            )
            for k in range(2)
        ]

    def at(s, action, copies):
        @pl.when(step == s)
        def _():
            for copy in copies:
                action(copy)

    start = lambda copy: copy.start()
    wait = lambda copy: copy.wait()
    at(0, start, fetch(0) + weights + fetch(1))
    for s in range(2):
        at(s, wait, fetch(s))
    at(0, wait, weights[:1])
    hn = hn_buf[step]
    gate = mm(hn, w_ref[:, parts[0]], NN)
    at(0, wait, weights[1:])
    up = mm(hn, w_ref[:, parts[1]], NN)
    dhid = dhid_ref[...]
    sg = 1.0 / (1.0 + jnp.exp(-gate))
    act = gate * sg
    hid_ref[...] = (act * up).astype(bf16)
    dgu_ref[:, parts[0]] = (dhid * up * sg * (1.0 + gate * (1.0 - sg))).astype(bf16)
    dgu_ref[:, parts[1]] = (dhid * act).astype(bf16)
    dn_buf[step] = mm(dgu_ref[...], w_ref[...], NT).astype(bf16)
    for s in range(2):
        at(s, start, flush(s))
    at(1, wait, flush(0) + flush(1))


def ffn(hns, dhid, w):
    depth = w.shape[0]
    rowwise = lambda width: pl.BlockSpec((512, width), lambda i: (i, 0))
    hbm = pl.BlockSpec(memory_space=pl.ANY)
    quarter = jax.ShapeDtypeStruct((256, depth), bf16)
    outs = pl.pallas_call(
        ffn_kernel,
        grid=(2,),
        in_specs=[hbm] * 8 + [rowwise(FF_PAD), hbm],
        out_specs=(rowwise(FF_PAD), rowwise(2 * FF_PAD)) + (hbm,) * 4,
        out_shape=(
            jax.ShapeDtypeStruct((1024, FF_PAD), bf16),
            jax.ShapeDtypeStruct((1024, 2 * FF_PAD), bf16),
        )
        + (quarter,) * 4,
        scratch_shapes=[
            pltpu.VMEM((2, 512, depth), bf16),
            pltpu.VMEM((2, 512, depth), bf16),
            pltpu.VMEM((depth, 2 * FF_PAD), bf16),
            pltpu.SemaphoreType.DMA((2,)),
            pltpu.SemaphoreType.DMA((2, 4)),
            pltpu.SemaphoreType.DMA((2, 2)),
        ],
        cost_estimate=pl.CostEstimate(
            flops=8 * 1024 * depth * FF_PAD,
            bytes_accessed=25 * 2**20,
            transcendentals=1024 * FF_PAD,
        ),
        compiler_params=BIG,
        name="ffn",
    )(*hns, dhid, w)
    return outs[0], outs[1], outs[2:]


def ffn_grad_kernel(*refs):
    hn = jnp.concatenate([r[...] for r in refs[:8]], 0)
    cot = jnp.concatenate([r[...] for r in refs[8:12]], 0)
    dgu_ref, hid_ref, w_ref, out_ref = refs[12:16]
    hid = hid_ref[...]
    out_ref[:, : 2 * FF_PAD] = mm(hn, dgu_ref[...], TN).astype(bf16)
    out_ref[:, 2 * FF_PAD :] = mm(cot, hid, TN).astype(bf16)
    for part, y_ref in enumerate(refs[16:]):
        y_ref[...] = mm(hid[part * 256 : part * 256 + 256], w_ref[...], NT).astype(bf16)


def ffn_grad(hns, cots, dgu, hid, w):
    depth = hns[0].shape[1]
    block = 256
    piece = lambda rows: pl.BlockSpec((rows, block), lambda i: (0, i))
    outs = pl.pallas_call(
        ffn_grad_kernel,
        grid=(depth // block,),
        in_specs=[piece(a.shape[0]) for a in hns + cots]
        + [VMEM] * 2
        + [pl.BlockSpec((block, FF_PAD), lambda i: (i, 2))],
        out_specs=(pl.BlockSpec((block, 3 * FF_PAD), lambda i: (i, 0)),) + (piece(256),) * 4,
        out_shape=(jax.ShapeDtypeStruct((depth, REST + OUT), bf16),)
        + (jax.ShapeDtypeStruct((256, depth), bf16),) * 4,
        cost_estimate=pl.CostEstimate(
            flops=8 * 1024 * depth * FF_PAD, bytes_accessed=30 * 2**20, transcendentals=0
        ),
        compiler_params=BIG,
        name="ffn_grad",
    )(*hns, *cots, dgu, hid, w)
    return outs[0], outs[1:]


def dh_kernel(p0, p1, p2, p3, w_ref, ob_ref, _, do_ref, grads_hbm, part, sem):
    for k in range(4):
        cols = slice(k * 512, k * 512 + 512)
        dh = jnp.concatenate([r[:, cols] for r in (p0, p1, p2, p3)], 0)
        part[cols, :] = mm(dh, ob_ref[...], TN).astype(bf16)
    copy = pltpu.make_async_copy(part, grads_hbm.at[:, REST:], sem)
    copy.start()
    for k, pieces in enumerate(((p0, p1), (p2, p3))):
        dh = jnp.concatenate([r[...] for r in pieces], 0)
        do_ref[k * 256 : k * 256 + 256, :] = mm(dh, w_ref[...], NN).astype(bf16)
    copy.wait()


def dh_project(pieces, w, ob, grads):
    depth = w.shape[0]
    hbm = pl.BlockSpec(memory_space=pl.ANY)
    return pl.pallas_call(
        dh_kernel,
        in_specs=[VMEM] * 6 + [hbm],
        out_specs=(VMEM, hbm),
        out_shape=(
            jax.ShapeDtypeStruct((ROWS, OUT), bf16),
            jax.ShapeDtypeStruct(grads.shape, bf16),
        ),
        scratch_shapes=[pltpu.VMEM((depth, OUT), bf16), pltpu.SemaphoreType.DMA(())],
        input_output_aliases={6: 1},
        cost_estimate=pl.CostEstimate(
            flops=4 * ROWS * depth * OUT, bytes_accessed=8 * 2**20, transcendentals=0
        ),
        compiler_params=BIG,
        name="dh_project",
    )(*pieces, w, ob, grads)


def dq_kernel(dq_ref, cos_ref, sin_ref, x0, x1, dqr_ref, grad_ref):
    @pl.when(pl.program_id(0) == 0)
    def _():
        cosine, sine = cos_ref[...], -sin_ref[...]
        for part in range(OUT // 128):
            cols = slice(part * 128, part * 128 + 128)
            dqr_ref[:, cols] = turn(dq_ref[:, cols], cosine, sine).astype(bf16)

    xh = jnp.concatenate([x0[...], x1[...]], 0)
    grad_ref[...] = mm(xh, dqr_ref[...], TN).astype(bf16)


def dq_project(dq, cosine, sine, xs):
    depth = xs[0].shape[1]
    block = 512
    return pl.pallas_call(
        dq_kernel,
        grid=(depth // block,),
        in_specs=[VMEM] * 3 + [pl.BlockSpec((256, block), lambda i: (0, i))] * 2,
        out_specs=(VMEM, pl.BlockSpec((block, OUT), lambda i: (i, 0))),
        out_shape=(
            jax.ShapeDtypeStruct((ROWS, OUT), bf16),
            jax.ShapeDtypeStruct((depth, OUT), bf16),
        ),
        cost_estimate=pl.CostEstimate(
            flops=2 * ROWS * depth * OUT, bytes_accessed=8 * 2**20, transcendentals=0
        ),
        compiler_params=BIG,
        name="dq_project",
    )(dq, cosine, sine, *xs)


def kv_grad_kernel(x0, x1, dkv_ref, out_ref):
    xh = jnp.concatenate([x0[...], x1[...]], 0)
    out_ref[...] = mm(xh, dkv_ref[...], TN).astype(bf16)


def kv_grad(xs, dkv):
    depth = xs[0].shape[1]
    block = 512
    return pl.pallas_call(
        kv_grad_kernel,
        grid=(depth // block,),
        in_specs=[pl.BlockSpec((256, block), lambda i: (0, i))] * 2 + [VMEM],
        out_specs=pl.BlockSpec((block, 2 * HD), lambda i: (i, 0)),
        out_shape=jax.ShapeDtypeStruct((depth, 2 * HD), bf16),
        cost_estimate=pl.CostEstimate(
            flops=4 * ROWS * depth * HD, bytes_accessed=6 * 2**20, transcendentals=0
        ),
        compiler_params=BIG,
        name="kv_grad",
    )(*xs, dkv)


def dqkv_kernel(dqr_ref, dkv_ref, other_ref, w_ref, cos_ref, sin_ref, dkvr_ref, send, keep):
    dkv = dkv_ref[...] + other_ref[...].astype(f32)
    lane = lax.broadcasted_iota(jnp.int32, dkv.shape, 1)
    dkvr = jnp.where(lane < HD, turn(dkv, cos_ref[...], -sin_ref[...]), dkv).astype(bf16)
    dkvr_ref[...] = dkvr
    dn = mm(jnp.concatenate([dqr_ref[...], dkvr], 1), w_ref[...], NT).astype(bf16)
    for step, out_ref in enumerate((send, keep)):

        @pl.when(pl.program_id(0) == step)
        def _():
            out_ref[...] = dn


def dqkv_project(dqr, dkv, other, w, cosine, sine):
    depth = w.shape[0]
    rowwise = lambda width: pl.BlockSpec((256, width), lambda i: (1 - i, 0))
    whole = pl.BlockSpec((256, depth), lambda i: (0, 0))
    return pl.pallas_call(
        dqkv_kernel,
        grid=(2,),
        in_specs=[rowwise(OUT), rowwise(128), rowwise(128), VMEM, rowwise(128), rowwise(128)],
        out_specs=(rowwise(128), whole, whole),
        out_shape=(jax.ShapeDtypeStruct((ROWS, 2 * HD), bf16),)
        + (jax.ShapeDtypeStruct((256, depth), bf16),) * 2,
        cost_estimate=pl.CostEstimate(
            flops=2 * ROWS * depth * QKV, bytes_accessed=10 * 2**20, transcendentals=0
        ),
        compiler_params=BIG,
        name="dqkv_project",
    )(dqr, dkv, other, w, cosine, sine)


def swap(value, axes):
    count = 2 ** len(axes)
    return lax.ppermute(value, axes, [(i, count - 1 - i) for i in range(count)])


def crossed(value, axis, mask):
    return lax.ppermute(value, axis, [(i, i ^ mask) for i in range(4)])


def shifted(value, steps):
    first, last = max(0, -steps), min(4, 4 - steps)
    return lax.ppermute(value, "z", [(i, i + steps) for i in range(first, last)])


def gather_chips(own):
    return swap(own, ("yl",)), swap(own, ("yh", "yl")), swap(own, ("yh",))


def gather_cores(own, by_l):
    return [own, by_l, swap(own, ("c",)), swap(by_l, ("c",))]


def sum_cores(keep, send):
    return keep.astype(f32) + swap(send, ("c",)).astype(f32)


def from_chip(total):
    return swap(total[128:].astype(bf16), ("yl",))


def from_chips(near, far):
    far = far.astype(bf16)
    return from_chip(near), swap(far[128:], ("yh", "yl")), swap(far[:128], ("yh",))


def sum_chips(near, *received):
    return near[:128] + sum(part.astype(f32) for part in received)


def pick(parts, index):
    return lax.dynamic_index_in_dim(parts, index, 0, False)


def in_order(which, mine, got, axis=0):
    return jnp.where(which == 0, jnp.stack([mine, got], axis), jnp.stack([got, mine], axis))


def trade_cores(parts, core):
    parts = jnp.moveaxis(parts, -3, 0)
    return in_order(core, pick(parts, core), swap(pick(parts, 1 - core), ("c",)), -3)


def both_halves(own, other, yl):
    return jnp.where(yl == 0, jnp.concatenate([own, other], 0), jnp.concatenate([other, own], 0))


def on_device(
    tokens, w_query, w_key, w_value, w_output, w_gate, w_up, w_down, norm_attn, norm_ffn, cotangent
):
    together = lax.optimization_barrier
    z, yh = lax.axis_index("z"), lax.axis_index("yh")
    core, yl = lax.axis_index("c"), lax.axis_index("yl")
    gain_one = norm_attn.astype(f32)[:, None]
    gain_two = norm_ffn.astype(f32)[:, None]
    flip = (core * 2 + yl) * 128
    at = jnp.stack([z, flip, core, yl, lax.axis_index("x"), yh]).astype(jnp.int32)

    xh, inverse_one, cot_here = order(at, tokens[0], cotangent[0])
    inputs = lax.dynamic_slice_in_dim(tokens[0], yl * 128, 128, 0).astype(f32)

    xhs = [xh, swap(xh, ("c",))]
    copies, rest, out_rows = prepare(
        w_query, w_key, w_value, w_output.T, w_gate, w_up, w_down.T, gain_one, gain_two
    )

    w_qkv = lax.all_to_all(copies, ALL, 0, 0).reshape(2048, QKV)
    out_rows = trade_cores(out_rows, core).reshape(64, OUT)
    out_rows = in_order(yh, out_rows, swap(out_rows, ("yh",))).reshape(128, OUT)
    rest = trade_cores(rest.reshape(2, 2, 32, REST), core)

    positions = ((z * 2 + yh) * ROWS + (jnp.arange(ROWS, dtype=jnp.int32) ^ flip)).astype(f32)
    freqs = rope_base ** (-2.0 * jnp.arange(HD // 2, dtype=f32) / HD)
    angles = positions[:, None] * freqs[None, :]
    cosine, sine = jnp.cos(angles), jnp.sin(angles)
    cosine = jnp.concatenate([cosine] * 4, -1)
    sine = jnp.concatenate([-sine, sine, -sine, sine], -1)

    w_qkv, cosine, sine, rest, out_rows, xhs = together(
        (w_qkv, cosine, sine, rest, out_rows, xhs)
    )

    q, kv = qkv_project(xhs, w_qkv, cosine, sine)
    kv, out_rows = together((kv, out_rows))
    kv_other = swap(kv, ("yh",))
    rest = in_order(yh, pick(rest, yh), swap(pick(rest, 1 - yh), ("yh",))).reshape(128, REST)
    ws = jnp.concatenate([out_rows] + [crossed(out_rows, "x", mask) for mask in (1, 2, 3)], 0)
    kv = jnp.concatenate([kv, kv_other], 0)
    kvs = [kv] + [shifted(kv, by) for by in (1, 2, 3)]
    kvs, ws, cot_here, rest = together((kvs, ws, cot_here, rest))
    w_ffn = lax.all_gather(rest, ("x", "z"), axis=0, tiled=True)
    ws = [ws] + [crossed(ws, "z", mask) for mask in (1, 2, 3)]
    cot_c, cot_h = swap(cot_here, ("c",)), swap(cot_here, ("yh",))
    ob, o_t, lse = attn_fwd(at, q, kvs)
    ob, ws, cot_h = together((ob, ws, cot_h))
    cots = [cot_here, cot_c, cot_h, swap(cot_h, ("c",))]
    keep, send, w_out = branch_project(at, ob, ws)
    total = sum_cores(keep, send)
    middle = inputs + sum_chips(total, from_chip(total))
    inverse_two = lax.rsqrt(jnp.mean(middle * middle, axis=-1, keepdims=True) + epsilon)
    hn = (middle * inverse_two).astype(bf16)

    received = gather_chips(hn)
    dhid = dhid_project(cots, w_ffn)
    (by_l, by_d, by_h), dhid = together((received, dhid))
    hns = gather_cores(hn, by_l) + [by_h, by_d, swap(by_h, ("c",)), swap(by_d, ("c",))]
    hid, dgu, dns = ffn(hns, dhid, w_ffn)
    near, far = sum_cores(*dns[:2]), sum_cores(*dns[2:])
    received = from_chips(near, far)
    grads, ys = ffn_grad(hns, cots, dgu, hid, w_ffn)
    received, grads = together((received, grads))
    dn2 = sum_chips(near, *received)
    dh = (
        cots[0][:128].astype(f32)
        + inverse_two * dn2
        - middle * inverse_two**3 * jnp.mean(dn2 * middle, axis=-1, keepdims=True)
    )
    dh_low, ys = together((dh.astype(bf16), ys))
    by_l, y_near, y_far = swap(dh_low, ("yl",)), sum_cores(*ys[:2]), sum_cores(*ys[2:])
    by_l, y_near, y_far = together((by_l, y_near, y_far))
    dhs = gather_cores(dh_low, by_l)

    do, grads = dh_project(dhs, w_out, ob, grads)
    grads = lax.psum_scatter(grads, ("x", "z"), scatter_dimension=0, tiled=True)
    do, y_near, y_far = together((do, y_near, y_far))
    received = from_chips(y_near, y_far)
    dq, *dkvs = attn_bwd(at, q, kvs, do, o_t, lse)
    received, dkvs = together((received, dkvs))
    block_out = (middle + sum_chips(y_near, *received)).astype(bf16)
    block_out, dkvs, dq = together((block_out, dkvs, dq))
    block_other = swap(block_out, ("yl",))
    dkvs = dkvs[:1] + [shifted(dkvs[by], -by) for by in (1, 2, 3)]

    def to_owners(grad, axis):
        parts = grad.reshape(4, grad.shape[0] // 4, -1)
        mine = lax.axis_index(axis)
        return [pick(parts, mine)] + [crossed(pick(parts, mine ^ m), axis, m) for m in (1, 2, 3)]

    added = lambda parts: sum(part.astype(f32) for part in parts).astype(bf16)
    dqr, grad_q = dq_project(dq, cosine, sine, xhs)
    grad_q = lax.all_to_all(grad_q.reshape(4, ROWS, OUT), "x", 0, 0)
    dkvs, block_other, dqr = together((dkvs, block_other, dqr))
    block_out = both_halves(block_out, block_other, yl)
    dkv = sum(part.astype(f32) for part in dkvs)
    other, grad_q = together((swap(dkv[ROWS:].astype(bf16), ("yh",)), grad_q))
    dkvr, send, keep = dqkv_project(dqr, dkv[:ROWS], other, w_qkv, cosine, sine)
    total, dkvr, grad_q = together((sum_cores(keep, send), dkvr, added(grad_q)))
    received, grad_kv, grad_q = together(
        (from_chip(total), kv_grad(xhs, dkvr), to_owners(grad_q, "z"))
    )
    grad_kv = lax.all_to_all(grad_kv.reshape(16, 128, 2 * HD), ("x", "z"), 0, 0)
    dn1 = sum_chips(total, received)
    input_grad = (
        dh
        + inverse_one * dn1
        - inputs * inverse_one**3 * jnp.mean(dn1 * inputs, axis=-1, keepdims=True)
    )
    input_grad, grad_kv = together((input_grad, grad_kv))
    other = swap(input_grad.astype(bf16), ("yl",))
    input_grad = both_halves(input_grad, other.astype(f32), yl)
    grad_kv = jnp.sum(grad_kv.astype(f32), 0).astype(bf16)
    grads = jnp.concatenate([grads, added(grad_q), grad_kv], -1)
    grads = trade_cores(grads.reshape(2, 2, 32, REST + OUT + QKV), core)
    mine, got = pick(grads, yh), swap(pick(grads, 1 - yh), ("yh",))
    attn_grads = mine[..., REST:].astype(f32) + got[..., REST:].astype(f32)
    grad_qkv = attn_grads[..., OUT:]
    grad_gate, grad_up, grad_down, grad_out, gain_grad_two = finish_ffn(
        in_order(yh, mine[..., :REST], got[..., :REST]).reshape(4, 32, REST),
        attn_grads[..., :OUT],
        w_gate,
        w_up,
        gain_two,
    )
    grad_query, grad_key, grad_value, gain_grad_one = finish_qkv(
        grad_qkv, w_query, w_key, w_value, gain_one
    )
    gain_grad_one = gain_grad_one + swap(gain_grad_one, ("yl",))
    gain_grad_two = gain_grad_two + swap(gain_grad_two, ("yl",))
    return (
        block_out[None],
        input_grad[None],
        grad_query,
        grad_key,
        grad_value,
        grad_out.T,
        grad_gate,
        grad_up,
        grad_down.T,
        gain_grad_one[:, 0],
        gain_grad_two[:, 0],
    )


def solution(mesh):
    mesh = Mesh(mesh.devices.reshape(4, 4, 2, 2, 2), ("x", "z", "yh", "c", "yl"))
    ctx = ("z", "yh", "c")
    rows, cols = P(ALL, "yl"), P("yl", ALL)
    seq = P("x", ctx, None)
    vec = P(ALL)
    in_specs = (seq, rows, rows, rows, cols, rows, rows, cols, vec, vec, seq)
    out_specs = (seq, seq, rows, rows, rows, cols, rows, rows, cols, vec, vec)
    return jax.shard_map(
        on_device, mesh=mesh, in_specs=in_specs, out_specs=out_specs, check_vma=False
    )
```
